32 devices in a mesh: groups: 2 (over x), seq: 16 (over z, y, core).
Axes of the slice: x: 2, y: 2, z: 4, core: 2. Of those that a mesh axis runs over, the one named last changes fastest.
Arguments:
- queries: bfloat16 [8192, 1536], P(('groups', 'seq')), parts along dimension 0, may hold values from -5 to 5
- keys: bfloat16 [8192, 1536], P(('groups', 'seq')), parts along dimension 0, may hold values from -5 to 5
- values: bfloat16 [8192, 1536], P(('groups', 'seq')), parts along dimension 0, may hold values from -6 to 6
- frame_index: int32 [64], P(('groups', 'seq')), parts along dimension 0, may hold values from 0 to 15, never falling along the last dimension, each value on 1 to 4 neighbouring positions
- block_mask: int32 [32, 32], replicated, may hold values from 0 to 1, as said below
- out_weight: bfloat16 [1536, 3072], P('seq'), may hold values from -0.15625 to 0.15625
Outputs:
- projected: bfloat16 [8192, 3072], P(('groups', 'seq')), parts along dimension 0
The draws below stay inside these ranges and needn't reach their ends.
There are 2 independent parts, one for each index of `groups`. The reference program is written for one: setup_inputs(seed, part) draws one part's arguments, and reference() takes and returns one part's arrays. A program takes and returns all parts, laid end to end along the dimension named above; an argument that names none is the same for every part. Nothing has to cross between parts.
Inputs may be any that keep to these rules, and one draw needn't show every extreme that they name: `block_mask`: entry (i, j) can be 1 only where |i // B - j // B| <= 4 with B = 2; every diagonal entry is 1; some entry with |i // B - j // B| = 4 is 1.
All inputs are finite; a program needn't handle non-finite values.
Results may differ from the reference program's by a relative error of at most 0.0085.
Values may be sent and summed in bfloat16 or wider, within the bound.
No kernel may reach another device: no remote copies, remote signals or barrier semaphores. Data moves between devices by JAX's collectives and lax.ppermute only.
A program may use at most 128 MiB of HBM per device.

```python
import math
import jax
import jax.numpy as jnp
import numpy as np
from jax import lax

D = 3072
HEADS = 12
HDIM = 128
TCH = 16
BLK = 128
REACH = 4
TOK_DEV = 256
TOKENS = 4096
NBLK = 32
HD = 1536
N_SEQ = 16


def draw_queries(key, part):
    key = jax.random.fold_in(key, 21)
    return jnp.clip(jax.random.normal(key, (TOKENS, HD), jnp.float32), -5.0, 5.0).astype(jnp.bfloat16)


def draw_keys(key, part):
    key = jax.random.fold_in(key, 22)
    return jnp.clip(jax.random.normal(key, (TOKENS, HD), jnp.float32), -5.0, 5.0).astype(jnp.bfloat16)


def draw_block_mask(key, part):
    key = jax.random.fold_in(key, 31)
    per_dev = TOK_DEV // BLK
    devices = NBLK // per_dev
    query_block = jnp.arange(NBLK, dtype=jnp.int32)[:, None]
    key_block = jnp.arange(NBLK, dtype=jnp.int32)[None, :]
    query_dev = query_block // per_dev
    distance = jnp.abs(query_dev - key_block // per_dev)
    loads = jax.random.randint(jax.random.fold_in(key, 1), (devices,), 1, 5)
    weight_row = loads[query_dev]
    tickets = jax.random.randint(jax.random.fold_in(key, 2), (NBLK, NBLK), 0, 4 * (REACH + 1))
    chosen = (tickets < weight_row * (REACH + 2 - distance)) & (distance <= REACH)
    chosen = chosen | (query_block == key_block)
    chosen = chosen | (query_block % per_dev == 0) & (key_block == query_block + REACH * per_dev)
    return chosen.astype(jnp.int32)


def steps_of(own_key, shape, pieces, smallest, top_value):
    def one(position, shards_of):
        heights = jax.random.uniform(jax.random.fold_in(jax.random.fold_in(own_key, 6), position), (shards_of,), jnp.float32, smallest / len(pieces), top_value / len(pieces))
        return jnp.repeat(jnp.exp(heights), shape[position] // shards_of).reshape((-1,) + (1,) * (len(shape) - position - 1))

    loudness = one(*pieces[0])
    for cut in pieces[1:]:
        loudness = loudness * one(*cut)
    return loudness


def length_profile(amount, total, most, slope):
    weights = [(1 << 20) // math.isqrt(rank ** slope) + 1 for rank in range(2, amount + 1)]
    rest, holding = total - most - (amount - 1), [1] * (amount - 1)
    while rest > 0:
        candidates = [i for i in range(amount - 1) if holding[i] < most]
        mass, remaining = sum([weights[i] for i in candidates]), rest
        for i in candidates:
            extra = min(most - holding[i], max(1, remaining * weights[i] // mass), rest)
            holding[i] = holding[i] + extra
            rest = rest - extra
    return np.array([most] + holding)


def uneven_parts(stream_key, number_of, total, reach, lean):
    if number_of == 2:
        one = jax.random.randint(stream_key, (), max(1, total - reach), min(reach, total - 1) + 1)
        return jnp.stack([one, total - one])
    lengths = jnp.asarray(length_profile(number_of, total, reach, lean), jnp.int32)
    couples = (number_of - 1) // 2
    donor, receiver = lengths[1:1 + 2 * couples:2], lengths[2:2 + 2 * couples:2]
    slack = jnp.minimum(donor - 1, reach - receiver)
    shifted = jax.random.randint(jax.random.fold_in(stream_key, 1), (couples,), 0, 1 << 20) % (slack + 1)
    lengths = lengths.at[1:1 + 2 * couples:2].set(donor - shifted).at[2:2 + 2 * couples:2].set(receiver + shifted)
    return lengths[jax.random.permutation(jax.random.fold_in(stream_key, 2), number_of)]


def scatter_about(stream_key, dims, spread, limit, split=(), kind=jnp.bfloat16):
    array = jax.random.normal(stream_key, dims, jnp.float32) * spread
    if len(split) > 0:
        array = steps_of(stream_key, dims, split, -0.22, 0.18) * array
    return jnp.clip(array, min=-limit, max=limit).astype(kind)


def setup_inputs(seed: int = 0, part: int = 0) -> dict:
    seeds = jax.random.split(jax.random.key(seed), 7)
    part_splits = jax.random.split(jax.random.fold_in(seeds[6], part), 7)
    return {
        "queries": draw_queries(jax.random.fold_in(jax.random.fold_in(seeds[6], part), 71), part),
        "keys": draw_keys(jax.random.fold_in(jax.random.fold_in(seeds[6], part), 71), part),
        "values": scatter_about(part_splits[2], (TOKENS, HD), 1.0, 6.0, ((0, 16),)),
        "frame_index": jnp.searchsorted(jnp.cumsum(uneven_parts(part_splits[3], NBLK // 2, NBLK, 4, 0)), jnp.arange(NBLK), side="right").astype(jnp.int32),
        "block_mask": draw_block_mask(jax.random.fold_in(seeds[6], 71), part),
        "out_weight": scatter_about(seeds[5], (HD, D), HD ** -0.5, 0.15625, ((0, 16),)),
    }


def rotate_time(inputs, frames):
    count = inputs.shape[0]
    tok_frames = jnp.repeat(frames, BLK, total_repeat_length=count).astype(jnp.float32)
    half_ch = TCH // 2
    freqs = jnp.float32(256.0) ** (-jnp.arange(half_ch, dtype=jnp.float32) / half_ch)
    angles = tok_frames[:, None] * freqs[None, :]
    cosine = jnp.cos(angles)[:, None, :]
    sine = jnp.sin(angles)[:, None, :]
    shaped = inputs.astype(jnp.float32).reshape(count, HEADS, HDIM)
    first = shaped[..., :half_ch]
    second = shaped[..., half_ch:TCH]
    turned = jnp.concatenate([first * cosine - second * sine, second * cosine + first * sine, shaped[..., TCH:]], axis=-1)
    return turned.reshape(count, HEADS * HDIM).astype(jnp.bfloat16)

def reference(queries, keys, values, frame_index, block_mask, out_weight):
    query_rot = rotate_time(queries, frame_index)
    key_rot = rotate_time(keys, frame_index)
    per_dev = TOK_DEV // BLK
    margin = REACH * TOK_DEV
    key_pad = jnp.pad(key_rot, ((margin, margin), (0, 0)))
    value_pad = jnp.pad(values, ((margin, margin), (0, 0)))
    mask_pad = jnp.pad(block_mask, ((0, 0), (REACH * per_dev, REACH * per_dev)))
    span = (2 * REACH + 1) * TOK_DEV
    scale = 1.0 / math.sqrt(HDIM)

    def one_device(device):
        row_start = (device * TOK_DEV).astype(jnp.int32)
        query_block = lax.dynamic_slice_in_dim(query_rot, row_start, TOK_DEV, 0).reshape(TOK_DEV, HEADS, HDIM)
        key_block = lax.dynamic_slice_in_dim(key_pad, row_start, span, 0).reshape(span, HEADS, HDIM)
        value_block = lax.dynamic_slice_in_dim(value_pad, row_start, span, 0).reshape(span, HEADS, HDIM)
        block_start = (device * per_dev).astype(jnp.int32)
        allowed_blocks = lax.dynamic_slice(mask_pad, (block_start, block_start), (per_dev, (2 * REACH + 1) * per_dev))
        allowed = jnp.repeat(jnp.repeat(allowed_blocks, BLK, axis=0), BLK, axis=1) > 0
        scores = jnp.einsum('qhd,khd->hqk', query_block.astype(jnp.float32), key_block.astype(jnp.float32)) * scale
        scores = jnp.where(allowed[None], scores, jnp.float32(-1e+30))
        peak = lax.optimization_barrier(jnp.max(scores, axis=-1, keepdims=True))
        expo = jnp.exp(scores - peak)
        totals = lax.optimization_barrier(jnp.sum(expo, axis=-1))
        rounded = lax.optimization_barrier(expo.astype(jnp.bfloat16)).astype(jnp.float32)
        mixed = jnp.einsum('hqk,khd->hqd', rounded, value_block.astype(jnp.float32))
        attended = (mixed / totals[..., None]).transpose(1, 0, 2).reshape(TOK_DEV, HEADS * HDIM)
        return attended.astype(jnp.bfloat16)
    attended = lax.map(one_device, jnp.arange(N_SEQ, dtype=jnp.int32)).reshape(TOKENS, HEADS * HDIM)
    return jnp.dot(attended, out_weight, preferred_element_type=jnp.float32).astype(jnp.bfloat16)
```

```python
import functools
import math

import jax
import jax.numpy as jnp
from jax import lax
from jax.experimental import pallas as pl
from jax.experimental.pallas import tpu as pltpu
from jax.sharding import Mesh
from jax.sharding import PartitionSpec as P

HEADS = 12
HDIM = 128
TCH = 16
BLK = 128
LANES = 4
HL = HEADS // LANES
HC = HL * HDIM
BAND = 18
CH = 2
NEG = -1e30
TO_EXP2 = math.log2(math.e) / math.sqrt(HDIM)


def turn_tables(frame):
    lane = lax.broadcasted_iota(jnp.int32, (8, HDIM), 1)
    half = TCH // 2
    channel = lax.rem(lane, half).astype(jnp.float32)
    angle = frame.astype(jnp.float32) * jnp.exp2(-channel)
    cosine, sine = jnp.cos(angle), jnp.sin(angle)
    same = jnp.where(lane < TCH, cosine, 1.0)
    other = jnp.where(lane < half, -sine, jnp.where(lane < TCH, sine, 0.0))
    return same[:1], other[:1]


def turned(x, same, other):
    x = x.astype(jnp.float32)
    half = TCH // 2
    lane = lax.broadcasted_iota(jnp.int32, x.shape, 1)
    partner = jnp.where(lane < half, pltpu.roll(x, HDIM - half, 1), pltpu.roll(x, half, 1))
    return (x * same + partner * other).astype(jnp.bfloat16)


def turn_rows(frames, x_ref, o_ref):
    for block in range(x_ref.shape[0] // BLK):
        same, other = turn_tables(frames[block])
        rows = slice(block * BLK, (block + 1) * BLK)
        for head in range(HL):
            cols = slice(head * HDIM, (head + 1) * HDIM)
            o_ref[0, rows, cols] = turned(x_ref[rows, cols], same, other)


def pack_kv_kernel(frames, k_ref, v_ref, o_ref):
    turn_rows(frames, k_ref, o_ref)
    o_ref[0, :, HC:] = v_ref[...]


def pack_q_kernel(frames, q_ref, o_ref):
    turn_rows(frames, q_ref, o_ref)


def pack(kernel, frames, arrays, width):
    count = arrays[0].shape[0]
    return pl.pallas_call(
        kernel,
        out_shape=jax.ShapeDtypeStruct((LANES, count, width), jnp.bfloat16),
        grid=(LANES,),
        in_specs=[pl.BlockSpec(memory_space=pltpu.SMEM)]
        + [pl.BlockSpec((count, HC), lambda g: (0, g)) for _ in arrays],
        out_specs=pl.BlockSpec((1, count, width), lambda g: (g, 0, 0)),
    )(frames, *arrays)


def attend_kernel(
    mask, q_ref, here_ref, before_ref, after_ref, o_ref, kv, scores, peak, total, mixed, picks, sems
):
    step = pl.program_id(0)
    plane = lax.axis_index("plane")
    plane_blocks = here_ref.shape[0] // BLK
    nblk = mask.shape[0]
    copies = [
        pltpu.make_async_copy(ref, kv.at[pl.ds(i * here_ref.shape[0], here_ref.shape[0])], sems.at[i])
        for i, ref in enumerate((before_ref, here_ref, after_ref))
    ]

    @pl.when(step == 0)
    def _():
        for copy in copies:
            copy.start()
        for copy in copies:
            copy.wait()

    my_block = plane * plane_blocks + step
    first = (plane - 1) * plane_blocks

    def pick(i, count):
        at = first + i
        inside = (at >= 0) & (at < nblk)
        kept = inside & (mask[my_block, jnp.clip(at, 0, nblk - 1)] > 0)
        picks[count] = i
        return count + kept.astype(jnp.int32)

    count = lax.fori_loop(0, 3 * plane_blocks, pick, jnp.int32(0))
    for extra in range(CH - 1):
        picks[count + extra] = plane_blocks + step
    rounds = lax.div(count + (CH - 1), CH)
    peak[...] = jnp.full(peak.shape, NEG, jnp.float32)
    total[...] = jnp.zeros(total.shape, jnp.float32)
    mixed[...] = jnp.zeros(mixed.shape, jnp.float32)

    def score(r, carry):
        for c in range(CH):
            slot = r * CH + c
            rows = pl.ds(pl.multiple_of(picks[slot] * BLK, BLK), BLK)
            for h in range(HL):
                cols = slice(h * HDIM, (h + 1) * HDIM)
                s = lax.dot_general(
                    q_ref[:, cols],
                    kv[rows, cols],
                    (((1,), (1,)), ((), ())),
                    preferred_element_type=jnp.float32,
                )
                if c > 0:
                    s = jnp.where(slot < count, s, NEG)
                scores[h, slot] = s
                peak[h] = jnp.maximum(peak[h], s)
        return carry

    lax.fori_loop(0, rounds, score, 0)
    for h in range(HL):
        top = jnp.max(peak[h], axis=1, keepdims=True)
        peak[h] = jnp.broadcast_to(top, (BLK, BLK))

    def mix(r, carry):
        rows = [pl.ds(pl.multiple_of(picks[r * CH + c] * BLK, BLK), BLK) for c in range(CH)]
        for h in range(HL):
            vcols = slice(HC + h * HDIM, HC + (h + 1) * HDIM)
            parts = []
            for c in range(CH):
                e = jnp.exp2((scores[h, r * CH + c] - peak[h]) * TO_EXP2)
                total[h] += e
                parts.append(e.astype(jnp.bfloat16))
            mixed[h] += jnp.dot(
                jnp.concatenate(parts, axis=1),
                jnp.concatenate([kv[row, vcols] for row in rows], axis=0),
                preferred_element_type=jnp.float32,
            )
        return carry

    lax.fori_loop(0, rounds, mix, 0)
    for h in range(HL):
        whole = jnp.sum(total[h], axis=1, keepdims=True)
        o_ref[:, h * HDIM : (h + 1) * HDIM] = (mixed[h] / whole).astype(jnp.bfloat16)


def attend(mask, q, here, before, after):
    tokens = q.shape[0]
    slots = -(-BAND // CH) * CH
    hbm = pl.BlockSpec(memory_space=pl.ANY)
    return pl.pallas_call(
        attend_kernel,
        out_shape=jax.ShapeDtypeStruct((tokens, HC), jnp.bfloat16),
        grid=(tokens // BLK,),
        in_specs=[
            pl.BlockSpec(memory_space=pltpu.SMEM),
            pl.BlockSpec((BLK, HC), lambda b: (b, 0)),
            hbm,
            hbm,
            hbm,
        ],
        out_specs=pl.BlockSpec((BLK, HC), lambda b: (b, 0)),
        scratch_shapes=[
            pltpu.VMEM((3 * tokens, 2 * HC), jnp.bfloat16),
            pltpu.VMEM((HL, slots, BLK, BLK), jnp.float32),
            pltpu.VMEM((HL, BLK, BLK), jnp.float32),
            pltpu.VMEM((HL, BLK, BLK), jnp.float32),
            pltpu.VMEM((HL, BLK, HDIM), jnp.float32),
            pltpu.SMEM((3 * tokens // BLK + CH,), jnp.int32),
            pltpu.SemaphoreType.DMA((3,)),
        ],
        compiler_params=pltpu.CompilerParams(vmem_limit_bytes=40 * 1024 * 1024),
    )(mask, q, here, before, after)


def project_kernel(a_ref, w_ref, o_ref):
    acc = jnp.dot(a_ref[0], w_ref[:HC], preferred_element_type=jnp.float32)
    for g in range(1, LANES):
        acc += jnp.dot(a_ref[g], w_ref[g * HC : (g + 1) * HC], preferred_element_type=jnp.float32)
    o_ref[...] = acc.astype(jnp.bfloat16)


def project(attended, weight, width):
    groups, count, depth = attended.shape
    return pl.pallas_call(
        project_kernel,
        out_shape=jax.ShapeDtypeStruct((count, weight.shape[1]), jnp.bfloat16),
        grid=(weight.shape[1] // width,),
        in_specs=[
            pl.BlockSpec((groups, count, depth), lambda n: (0, 0, 0)),
            pl.BlockSpec((weight.shape[0], width), lambda n: (0, n)),
        ],
        out_specs=pl.BlockSpec((count, width), lambda n: (0, n)),
        compiler_params=pltpu.CompilerParams(vmem_limit_bytes=40 * 1024 * 1024),
    )(attended, weight)


def on_device(queries, keys, values, frame_index, block_mask, out_weight):
    count = queries.shape[0]
    planes = lax.axis_size("plane")
    weight = lax.all_gather(out_weight, ("plane", "lane"), axis=0, tiled=True)
    kv = pack(pack_kv_kernel, frame_index, (keys, values), 2 * HC)
    kv = lax.all_to_all(kv, "lane", 0, 0, tiled=True).reshape(LANES * count, 2 * HC)
    before = lax.ppermute(kv, "plane", [(p, p + 1) for p in range(planes - 1)])
    after = lax.ppermute(kv, "plane", [(p + 1, p) for p in range(planes - 1)])
    q = pack(pack_q_kernel, frame_index, (queries,), HC)
    q = lax.all_to_all(q, "lane", 0, 0, tiled=True).reshape(LANES * count, HC)
    attended = attend(block_mask, q, kv, before, after)
    attended = lax.all_to_all(attended.reshape(LANES, count, HC), "lane", 0, 0, tiled=True)
    return project(attended, weight, 512)


def solution(mesh):
    groups, seq = mesh.devices.shape
    split = Mesh(mesh.devices.reshape(groups, seq // LANES, LANES), ("groups", "plane", "lane"))
    tokens = P(("groups", "plane", "lane"), None)
    return jax.shard_map(
        on_device,
        mesh=split,
        in_specs=(
            tokens,
            tokens,
            tokens,
            P(("groups", "plane", "lane")),
            P(),
            P(("plane", "lane"), None),
        ),
        out_specs=tokens,
        check_vma=False,
    )
```

```python
import math

import jax
import jax.numpy as jnp
from jax import lax
from jax.experimental import pallas as pl
from jax.experimental.pallas import tpu as pltpu
from jax.sharding import Mesh
from jax.sharding import PartitionSpec as P

HEADS = 12
HDIM = 128
TCH = 16
BLK = 128
LANES = 4
HL = HEADS // LANES
HC = HL * HDIM
REACH = 4
NEG = -1e30
TO_EXP2 = math.log2(math.e) / math.sqrt(HDIM)


def turn_tables(frames, same, other):
    lane = lax.broadcasted_iota(jnp.int32, (8, HDIM), 1)
    half = TCH // 2
    channel = lax.rem(lane, half).astype(jnp.float32)
    for block in range(same.shape[0]):
        angle = frames[block].astype(jnp.float32) * jnp.exp2(-channel)
        cosine, sine = jnp.cos(angle), jnp.sin(angle)
        same[block] = jnp.where(lane < TCH, cosine, 1.0)
        other[block] = jnp.where(lane < half, -sine, jnp.where(lane < TCH, sine, 0.0))


def turn_rows(frames, x_ref, o_ref, same, other):
    @pl.when(pl.program_id(0) == 0)
    def _():
        turn_tables(frames, same, other)

    half = TCH // 2
    lane = lax.broadcasted_iota(jnp.int32, (BLK, HDIM), 1)
    for block in range(x_ref.shape[0] // BLK):
        rows = slice(block * BLK, (block + 1) * BLK)
        for head in range(HL):
            cols = slice(head * HDIM, (head + 1) * HDIM)
            x = x_ref[rows, cols].astype(jnp.float32)
            partner = jnp.where(lane < half, pltpu.roll(x, HDIM - half, 1), pltpu.roll(x, half, 1))
            o_ref[0, rows, cols] = (x * same[block, :1] + partner * other[block, :1]).astype(jnp.bfloat16)


def pack_kv_kernel(frames, k_ref, v_ref, o_ref, same, other):
    turn_rows(frames, k_ref, o_ref, same, other)
    o_ref[0, :, HC:] = v_ref[...]


def pack_q_kernel(frames, q_ref, o_ref, same, other):
    turn_rows(frames, q_ref, o_ref, same, other)


def pack(kernel, frames, arrays, width):
    count = arrays[0].shape[0]
    table = pltpu.VMEM((count // BLK, 8, HDIM), jnp.float32)
    return pl.pallas_call(
        kernel,
        out_shape=jax.ShapeDtypeStruct((LANES, count, width), jnp.bfloat16),
        grid=(LANES,),
        in_specs=[pl.BlockSpec(memory_space=pltpu.SMEM)]
        + [pl.BlockSpec((count, HC), lambda g: (0, g)) for _ in arrays],
        out_specs=pl.BlockSpec((1, count, width), lambda g: (g, 0, 0)),
        scratch_shapes=[table, table],
    )(frames, *arrays)


def attend_kernel(mask, q_ref, here_ref, before_ref, after_ref, o_ref, kv, scores, weights, sems):
    tile, head = pl.program_id(0), pl.program_id(1)
    plane = lax.axis_index("plane")
    plane_rows = here_ref.shape[0]
    rows = q_ref.shape[0]
    per_dev = rows // BLK
    nblk = mask.shape[0]

    @pl.when((tile == 0) & (head == 0))
    def _():
        copies = [
            pltpu.make_async_copy(ref, kv.at[pl.ds(i * plane_rows, plane_rows)], sems.at[i])
            for i, ref in enumerate((before_ref, here_ref, after_ref))
        ]
        for copy in copies:
            copy.start()
        for copy in copies:
            copy.wait()

    me = plane * LANES + tile
    start = pl.multiple_of(tile * rows, BLK)
    kcols = pl.ds(pl.multiple_of(head * HDIM, HDIM), HDIM)
    vcols = pl.ds(pl.multiple_of(HC + head * HDIM, HDIM), HDIM)
    q = q_ref[...]
    peak = jnp.full((rows, BLK), NEG, jnp.float32)
    for i in range(2 * REACH + 1):
        keys = kv[pl.ds(pl.multiple_of(start + i * rows, BLK), rows), kcols]
        s = lax.dot_general(q, keys, (((1,), (1,)), ((), ())), preferred_element_type=jnp.float32)
        for b in range(per_dev):
            key_block = (me - REACH + i) * per_dev + b
            inside = (key_block >= 0) & (key_block < nblk)
            column = jnp.clip(key_block, 0, nblk - 1)
            parts = []
            for a in range(per_dev):
                kept = inside & (mask[me * per_dev + a, column] > 0)
                bias = jnp.where(kept, 0.0, NEG)
                parts.append(s[a * BLK : (a + 1) * BLK, b * BLK : (b + 1) * BLK] + bias)
            part = jnp.concatenate(parts, axis=0)
            peak = jnp.maximum(peak, part)
            at = i * rows + b * BLK
            scores[:, at : at + BLK] = part
    top = jnp.max(peak, axis=1, keepdims=True)
    total = jnp.zeros((rows, BLK), jnp.float32)
    for j in range((2 * REACH + 1) * per_dev):
        cols = slice(j * BLK, (j + 1) * BLK)
        e = jnp.exp2((scores[:, cols] - top) * TO_EXP2)
        total += e
        weights[:, cols] = e.astype(jnp.bfloat16)
    values = kv[pl.ds(start, (2 * REACH + 1) * rows), vcols]
    mixed = jnp.dot(weights[...], values, preferred_element_type=jnp.float32)
    o_ref[...] = (mixed / jnp.sum(total, axis=1, keepdims=True)).astype(jnp.bfloat16)


def attend(mask, q, here, before, after):
    tokens = q.shape[0]
    rows = tokens // LANES
    span = (2 * REACH + 1) * rows
    hbm = pl.BlockSpec(memory_space=pl.ANY)
    return pl.pallas_call(
        attend_kernel,
        out_shape=jax.ShapeDtypeStruct((tokens, HC), jnp.bfloat16),
        grid=(LANES, HL),
        in_specs=[
            pl.BlockSpec(memory_space=pltpu.SMEM),
            pl.BlockSpec((rows, HDIM), lambda t, h: (t, h)),
            hbm,
            hbm,
            hbm,
        ],
        out_specs=pl.BlockSpec((rows, HDIM), lambda t, h: (t, h)),
        scratch_shapes=[
            pltpu.VMEM((3 * tokens, 2 * HC), jnp.bfloat16),
            pltpu.VMEM((rows, span), jnp.float32),
            pltpu.VMEM((rows, span), jnp.bfloat16),
            pltpu.SemaphoreType.DMA((3,)),
        ],
        compiler_params=pltpu.CompilerParams(vmem_limit_bytes=56 * 1024 * 1024),
    )(mask, q, here, before, after)


def project_kernel(a_ref, w_ref, o_ref):
    acc = jnp.dot(a_ref[0], w_ref[0, 0, :HC], preferred_element_type=jnp.float32)
    for g in range(1, LANES):
        acc += jnp.dot(a_ref[g], w_ref[0, 0, g * HC : (g + 1) * HC], preferred_element_type=jnp.float32)
    o_ref[...] = acc.astype(jnp.bfloat16)


def project(attended, weight):
    lanes, count, depth = attended.shape
    cores, groups, channels, width = weight.shape
    return pl.pallas_call(
        project_kernel,
        out_shape=jax.ShapeDtypeStruct((count, cores * groups * width), jnp.bfloat16),
        grid=(groups, cores),
        in_specs=[
            pl.BlockSpec((lanes, count, depth), lambda g, c: (0, 0, 0)),
            pl.BlockSpec((1, 1, channels, width), lambda g, c: (c, g, 0, 0)),
        ],
        out_specs=pl.BlockSpec((count, width), lambda g, c: (0, g * cores + c)),
        compiler_params=pltpu.CompilerParams(vmem_limit_bytes=56 * 1024 * 1024),
    )(attended, weight)


def gather_weight(own):
    groups = lax.axis_size("groups")
    rows, columns = own.shape
    width = columns // (2 * groups)
    start = lax.axis_index("groups") * 2 * width
    halves = lax.dynamic_slice_in_dim(own, start, 2 * width, 1).reshape(rows, 2, width)
    halves = lax.all_to_all(halves.transpose(1, 0, 2), "core", 0, 0, tiled=True)
    part = lax.all_gather(halves.reshape(2 * rows, width), ("plane", "row"), axis=0, tiled=True)
    return lax.all_gather(lax.all_gather(part, "groups"), "core")


def on_device(queries, keys, values, frame_index, block_mask, out_weight):
    count = queries.shape[0]
    planes = lax.axis_size("plane")
    lane = ("row", "core")
    weight = gather_weight(out_weight)
    kv = pack(pack_kv_kernel, frame_index, (keys, values), 2 * HC)
    kv = lax.all_to_all(kv, lane, 0, 0, tiled=True).reshape(LANES * count, 2 * HC)
    before = lax.ppermute(kv, "plane", [(p, p + 1) for p in range(planes - 1)])
    after = lax.ppermute(kv, "plane", [(p + 1, p) for p in range(planes - 1)])
    q = pack(pack_q_kernel, frame_index, (queries,), HC)
    q = lax.all_to_all(q, lane, 0, 0, tiled=True).reshape(LANES * count, HC)
    attended = attend(block_mask, q, kv, before, after)
    attended = lax.all_to_all(attended.reshape(LANES, count, HC), lane, 0, 0, tiled=True)
    return project(attended, weight)


def solution(mesh):
    groups, seq = mesh.devices.shape
    split = Mesh(
        mesh.devices.reshape(groups, seq // LANES, LANES // 2, 2), ("groups", "plane", "row", "core")
    )
    along = ("plane", "row", "core")
    tokens = P(("groups",) + along, None)
    return jax.shard_map(
        on_device,
        mesh=split,
        in_specs=(tokens, tokens, tokens, P(("groups",) + along), P(), P(along, None)),
        out_specs=tokens,
        check_vma=False,
    )
```

```python
import math

import jax
import jax.numpy as jnp
from jax import lax
from jax.experimental import pallas as pl
from jax.experimental.pallas import tpu as pltpu
from jax.sharding import Mesh
from jax.sharding import PartitionSpec as P

HEADS = 12
HDIM = 128
TCH = 16
BLK = 128
LANES = 4
HL = HEADS // LANES
HC = HL * HDIM
REACH = 4
NEG = -1e30
TO_EXP2 = math.log2(math.e) / math.sqrt(HDIM)


def turn_tables(frames, same, other):
    lane = lax.broadcasted_iota(jnp.int32, (8, HDIM), 1)
    half = TCH // 2
    channel = lax.rem(lane, half).astype(jnp.float32)
    for block in range(same.shape[0]):
        angle = frames[block].astype(jnp.float32) * jnp.exp2(-channel)
        cosine, sine = jnp.cos(angle), jnp.sin(angle)
        same[block] = jnp.where(lane < TCH, cosine, 1.0)
        other[block] = jnp.where(lane < half, -sine, jnp.where(lane < TCH, sine, 0.0))


def lane_of(step):
    row, core = lax.axis_index("row"), lax.axis_index("core")
    return lax.bitwise_xor(row, step // 2) * 2 + lax.bitwise_xor(core, step % 2)


def turn_into(frames, x_ref, outs, same, other):
    turn_tables(frames, same, other)
    half = TCH // 2
    lane = lax.broadcasted_iota(jnp.int32, (BLK, HDIM), 1)
    for step in range(LANES):
        for head in range(HL):
            start = pl.multiple_of(lane_of(step) * HC + head * HDIM, HDIM)
            for block in range(x_ref.shape[0] // BLK):
                rows = slice(block * BLK, (block + 1) * BLK)
                x = x_ref[rows, pl.ds(start, HDIM)].astype(jnp.float32)
                partner = jnp.where(lane < half, pltpu.roll(x, HDIM - half, 1), pltpu.roll(x, half, 1))
                turned = x * same[block, :1] + partner * other[block, :1]
                outs[step][rows, head * HDIM : (head + 1) * HDIM] = turned.astype(jnp.bfloat16)


def pack_kv_kernel(frames, k_ref, v_ref, *rest):
    outs, tables = rest[:LANES], rest[LANES:]
    turn_into(frames, k_ref, outs, *tables)
    for step in range(LANES):
        start = pl.multiple_of(lane_of(step) * HC, HDIM)
        outs[step][:, HC:] = v_ref[:, pl.ds(start, HC)]


def pack_q_kernel(frames, q_ref, *rest):
    turn_into(frames, q_ref, rest[:LANES], *rest[LANES:])


def pack(kernel, frames, arrays, width):
    count = arrays[0].shape[0]
    table = pltpu.VMEM((count // BLK, 8, HDIM), jnp.float32)
    return pl.pallas_call(
        kernel,
        out_shape=[jax.ShapeDtypeStruct((count, width), jnp.bfloat16)] * LANES,
        in_specs=[pl.BlockSpec(memory_space=pltpu.SMEM)]
        + [pl.BlockSpec(memory_space=pltpu.VMEM) for _ in arrays],
        out_specs=[pl.BlockSpec(memory_space=pltpu.VMEM)] * LANES,
        scratch_shapes=[table, table],
        compiler_params=pltpu.CompilerParams(vmem_limit_bytes=56 * 1024 * 1024),
    )(frames, *arrays)


def attend_kernel(mask, *refs):
    q_refs, kv_refs, rest = refs[:LANES], refs[LANES : 4 * LANES], refs[4 * LANES :]
    o_ref, q_all, kv, scores, weights, sems = rest
    tile = pl.program_id(0)
    plane = lax.axis_index("plane")
    rows = o_ref.shape[0]
    per_dev = rows // BLK
    nblk = mask.shape[0]

    @pl.when(tile == 0)
    def _():
        copies = []
        for step in range(LANES):
            at = pl.multiple_of(lane_of(step) * rows, BLK)
            copies.append((q_refs[step], q_all.at[pl.ds(at, rows)]))
        for part in range(3):
            for step in range(LANES):
                at = pl.multiple_of((part * LANES + lane_of(step)) * rows, BLK)
                copies.append((kv_refs[part * LANES + step], kv.at[pl.ds(at, rows)]))
        started = [
            pltpu.make_async_copy(source, target, sems.at[i]) for i, (source, target) in enumerate(copies)
        ]
        for copy in started:
            copy.start()
        for copy in started:
            copy.wait()

    me = plane * LANES + tile
    start = pl.multiple_of(tile * rows, BLK)
    biases = []
    for j in range((2 * REACH + 1) * per_dev):
        key_block = (me - REACH) * per_dev + j
        inside = (key_block >= 0) & (key_block < nblk)
        column = jnp.clip(key_block, 0, nblk - 1)
        biases.append(
            [jnp.where(inside & (mask[me * per_dev + a, column] > 0), 0.0, NEG) for a in range(per_dev)]
        )
    for h in range(HL):
        kcols = slice(h * HDIM, (h + 1) * HDIM)
        vcols = slice(HC + h * HDIM, HC + (h + 1) * HDIM)
        q = q_all[pl.ds(start, rows), kcols]
        peak = jnp.full((rows, BLK), NEG, jnp.float32)
        for i in range(2 * REACH + 1):
            keys = kv[pl.ds(pl.multiple_of(start + i * rows, BLK), rows), kcols]
            s = lax.dot_general(q, keys, (((1,), (1,)), ((), ())), preferred_element_type=jnp.float32)
            for b in range(per_dev):
                j = i * per_dev + b
                parts = [
                    s[a * BLK : (a + 1) * BLK, b * BLK : (b + 1) * BLK] + biases[j][a]
                    for a in range(per_dev)
                ]
                part = jnp.concatenate(parts, axis=0)
                peak = jnp.maximum(peak, part)
                scores[h, :, j * BLK : (j + 1) * BLK] = part
        top = jnp.max(peak, axis=1, keepdims=True)
        total = jnp.zeros((rows, BLK), jnp.float32)
        for j in range((2 * REACH + 1) * per_dev):
            cols = slice(j * BLK, (j + 1) * BLK)
            e = jnp.exp2((scores[h, :, cols] - top) * TO_EXP2)
            total += e
            weights[h, :, cols] = e.astype(jnp.bfloat16)
        values = kv[pl.ds(start, (2 * REACH + 1) * rows), vcols]
        mixed = jnp.dot(weights[h], values, preferred_element_type=jnp.float32)
        o_ref[:, kcols] = (mixed / jnp.sum(total, axis=1, keepdims=True)).astype(jnp.bfloat16)


def attend(mask, q, kv):
    rows = q[0].shape[0]
    span = (2 * REACH + 1) * rows
    hbm = pl.BlockSpec(memory_space=pl.ANY)
    return pl.pallas_call(
        attend_kernel,
        out_shape=jax.ShapeDtypeStruct((LANES * rows, HC), jnp.bfloat16),
        grid=(LANES,),
        in_specs=[pl.BlockSpec(memory_space=pltpu.SMEM)] + [hbm] * (4 * LANES),
        out_specs=pl.BlockSpec((rows, HC), lambda t: (t, 0)),
        scratch_shapes=[
            pltpu.VMEM((LANES * rows, HC), jnp.bfloat16),
            pltpu.VMEM((3 * LANES * rows, 2 * HC), jnp.bfloat16),
            pltpu.VMEM((HL, rows, span), jnp.float32),
            pltpu.VMEM((HL, rows, span), jnp.bfloat16),
            pltpu.SemaphoreType.DMA((4 * LANES,)),
        ],
        compiler_params=pltpu.CompilerParams(vmem_limit_bytes=56 * 1024 * 1024),
    )(mask, *q, *kv)


def project_kernel(shard, groups, a_ref, *refs):
    w_refs, (o_ref, by_shard) = refs[:-2], refs[-2:]
    step = pl.program_id(0)
    depth = by_shard.shape[2]
    width = w_refs[0].shape[2]
    columns = o_ref.shape[1] // groups

    @pl.when(step == 0)
    def _():
        for lane in range(LANES):
            parts = []
            for plane in range(depth // shard):
                channel = (plane * LANES + lane) * shard
                whole = a_ref[channel // HC]
                parts.append(whole[:, channel % HC : channel % HC + shard])
            by_shard[lane] = jnp.concatenate(parts, axis=1)

    row = lax.axis_index("row")
    mine = lax.axis_index("groups")
    for dx in range(groups):
        acc = None
        for dr in range(2):
            for core in range(2):
                part = jnp.dot(
                    by_shard[lax.bitwise_xor(row, dr) * 2 + core],
                    w_refs[dx * 2 + dr][core],
                    preferred_element_type=jnp.float32,
                )
                acc = part if acc is None else acc + part
        block = lax.rem(mine + groups - dx, groups)
        at = pl.multiple_of(block * columns + step * width, HDIM)
        o_ref[:, pl.ds(at, width)] = acc.astype(jnp.bfloat16)


def project(attended, weights, shard):
    lanes, count, depth = attended.shape
    groups = len(weights) // 2
    columns = weights[0].shape[2]
    steps = 3
    return pl.pallas_call(
        lambda *refs: project_kernel(shard, groups, *refs),
        out_shape=jax.ShapeDtypeStruct((count, groups * columns), jnp.bfloat16),
        grid=(steps,),
        in_specs=[pl.BlockSpec((lanes, count, depth), lambda n: (0, 0, 0))]
        + [pl.BlockSpec((2, depth, columns // steps), lambda n: (0, 0, n)) for _ in weights],
        out_specs=pl.BlockSpec((count, groups * columns), lambda n: (0, 0)),
        scratch_shapes=[pltpu.VMEM((lanes, count, depth), jnp.bfloat16)],
        compiler_params=pltpu.CompilerParams(vmem_limit_bytes=56 * 1024 * 1024),
    )(attended, *weights)


def after(x, *others):
    return lax.optimization_barrier((x, *others))[0]


def on_device(queries, keys, values, frame_index, block_mask, out_weight):
    count = queries.shape[0]
    planes, groups = lax.axis_size("plane"), lax.axis_size("groups")
    seq = ("plane", "row", "core")
    lane = ("row", "core")

    def index(p, r, c):
        return (p * 2 + r) * 2 + c

    every = [(p, r, c) for p in range(planes) for r in range(2) for c in range(2)]

    def to_lane(x, dr, dc):
        return lax.ppermute(x, seq, [(index(p, r, c), index(p, r ^ dr, c ^ dc)) for p, r, c in every])

    def to_plane(x, dp, dc):
        pairs = [
            (index(p, r, c), index(p + dp, r, c ^ dc)) for p, r, c in every if 0 <= p + dp < planes
        ]
        return lax.ppermute(x, seq, pairs)

    columns = out_weight.shape[1] // groups
    half = lax.dynamic_slice_in_dim(out_weight, lax.axis_index("groups") * columns, columns, 1)
    strip = lax.all_gather(half, "plane", axis=0, tiled=True)

    kv = pack(pack_kv_kernel, frame_index, (keys, values), 2 * HC)
    across = [to_lane(kv[2], 1, 0), to_lane(kv[3], 1, 1)]
    early = {(dp, dc): to_plane(kv[dc], dp, dc) for dc in range(2) for dp in (1, -1)}
    here = [kv[0], to_lane(kv[1], 0, 1)] + across
    q = pack(pack_q_kernel, frame_index, (after(queries, kv[0]),), HC)
    late = {(dp, dc): to_plane(across[dc], dp, 0) for dc in range(2) for dp in (1, -1)}
    q = [q[0]] + [to_lane(after(q[d], *across), d // 2, d % 2) for d in range(1, LANES)]
    lower = [early[1, 0], early[1, 1], late[1, 0], late[1, 1]]
    upper = [early[-1, 0], early[-1, 1], late[-1, 0], late[-1, 1]]

    def round_groups(x, dx):
        return lax.ppermute(x, "groups", [(g, (g + dx) % groups) for g in range(groups)])

    strip = after(strip, *across, *early.values(), here[1])
    other = lax.ppermute(strip, "row", [(0, 1), (1, 0)])
    arrived = [*late.values(), *q[1:]]
    other = after(other, *arrived)
    strips = {(0, 0): strip, (0, 1): other}
    for dx in range(1, groups):
        strips[dx, 0] = after(round_groups(strip, dx), *arrived)
        strips[dx, 1] = round_groups(other, dx)
    attended = attend(block_mask, q, lower + here + upper)
    for dx in range(1, groups):
        strips[dx, 1] = after(strips[dx, 1], attended)
    weights = [lax.all_gather(strips[dx, dr], "core") for dx in range(groups) for dr in range(2)]
    attended = lax.all_to_all(attended.reshape(LANES, count, HC), lane, 0, 0, tiled=True)
    return project(attended, weights, out_weight.shape[0])


def solution(mesh):
    groups, seq = mesh.devices.shape
    split = Mesh(
        mesh.devices.reshape(groups, seq // LANES, LANES // 2, 2), ("groups", "plane", "row", "core")
    )
    along = ("plane", "row", "core")
    tokens = P(("groups",) + along, None)
    return jax.shard_map(
        on_device,
        mesh=split,
        in_specs=(tokens, tokens, tokens, P(("groups",) + along), P(), P(along, None)),
        out_specs=tokens,
        check_vma=False,
    )
```

```python
import math

import jax
import jax.numpy as jnp
from jax import lax
from jax.experimental import pallas as pl
from jax.experimental.pallas import tpu as pltpu
from jax.sharding import Mesh
from jax.sharding import PartitionSpec as P

HEADS = 12
HDIM = 128
TCH = 16
BLK = 128
LANES = 4
HL = HEADS // LANES
HC = HL * HDIM
REACH = 4
NEG = -1e30
TO_EXP2 = math.log2(math.e) / math.sqrt(HDIM)


def turn_tables(frames, same, other):
    lane = lax.broadcasted_iota(jnp.int32, (8, HDIM), 1)
    half = TCH // 2
    channel = lax.rem(lane, half).astype(jnp.float32)
    for block in range(same.shape[0]):
        angle = frames[block].astype(jnp.float32) * jnp.exp2(-channel)
        cosine, sine = jnp.cos(angle), jnp.sin(angle)
        same[block] = jnp.where(lane < TCH, cosine, 1.0)
        other[block] = jnp.where(lane < half, -sine, jnp.where(lane < TCH, sine, 0.0))


def lane_of(step):
    row, core = lax.axis_index("row"), lax.axis_index("core")
    return lax.bitwise_xor(row, step // 2) * 2 + lax.bitwise_xor(core, step % 2)


def turn_into(frames, x_ref, outs, same, other):
    turn_tables(frames, same, other)
    half = TCH // 2
    lane = lax.broadcasted_iota(jnp.int32, (BLK, HDIM), 1)
    for step in range(LANES):
        for head in range(HL):
            start = pl.multiple_of(lane_of(step) * HC + head * HDIM, HDIM)
            for block in range(x_ref.shape[0] // BLK):
                rows = slice(block * BLK, (block + 1) * BLK)
                x = x_ref[rows, pl.ds(start, HDIM)].astype(jnp.float32)
                partner = jnp.where(lane < half, pltpu.roll(x, HDIM - half, 1), pltpu.roll(x, half, 1))
                turned = x * same[block, :1] + partner * other[block, :1]
                outs[step][rows, head * HDIM : (head + 1) * HDIM] = turned.astype(jnp.bfloat16)


def pack_kv_kernel(frames, k_ref, v_ref, *rest):
    outs, tables = rest[:LANES], rest[LANES:]
    turn_into(frames, k_ref, outs, *tables)
    for step in range(LANES):
        start = pl.multiple_of(lane_of(step) * HC, HDIM)
        outs[step][:, HC:] = v_ref[:, pl.ds(start, HC)]


def pack_q_kernel(frames, q_ref, *rest):
    turn_into(frames, q_ref, rest[:LANES], *rest[LANES:])


def pack(kernel, frames, arrays, width):
    count = arrays[0].shape[0]
    table = pltpu.VMEM((count // BLK, 8, HDIM), jnp.float32)
    return pl.pallas_call(
        kernel,
        out_shape=[jax.ShapeDtypeStruct((count, width), jnp.bfloat16)] * LANES,
        in_specs=[pl.BlockSpec(memory_space=pltpu.SMEM)]
        + [pl.BlockSpec(memory_space=pltpu.VMEM) for _ in arrays],
        out_specs=[pl.BlockSpec(memory_space=pltpu.VMEM)] * LANES,
        scratch_shapes=[table, table],
        compiler_params=pltpu.CompilerParams(vmem_limit_bytes=56 * 1024 * 1024),
    )(frames, *arrays)


def attend_kernel(tiles, mask, *refs):
    q_refs, kv_refs, rest = refs[: len(tiles)], refs[len(tiles) : len(tiles) + 3 * LANES], refs[len(tiles) + 3 * LANES :]
    o_refs, (kv, scores, weights, sems) = rest[: len(tiles)], rest[len(tiles) :]
    plane = lax.axis_index("plane")
    rows = o_refs[0].shape[0]
    per_dev = rows // BLK
    nblk = mask.shape[0]
    span = 2 * REACH + 1

    copies = []
    for part in range(3):
        for step in range(LANES):
            at = pl.multiple_of((part * LANES + lane_of(step)) * rows, BLK)
            i = part * LANES + step
            copies.append(pltpu.make_async_copy(kv_refs[i], kv.at[pl.ds(at, rows)], sems.at[i]))
    for copy in copies:
        copy.start()
    for copy in copies:
        copy.wait()

    for t, step in enumerate(tiles):
        tile = lane_of(step)
        me = plane * LANES + tile
        start = pl.multiple_of(tile * rows, BLK)
        biases = []
        for j in range(span * per_dev):
            key_block = (me - REACH) * per_dev + j
            inside = (key_block >= 0) & (key_block < nblk)
            column = jnp.clip(key_block, 0, nblk - 1)
            biases.append(
                [jnp.where(inside & (mask[me * per_dev + a, column] > 0), 0.0, NEG) for a in range(per_dev)]
            )

        def one_head(h, carry):
            kcols = pl.ds(pl.multiple_of(h * HDIM, HDIM), HDIM)
            vcols = pl.ds(pl.multiple_of(HC + h * HDIM, HDIM), HDIM)
            sums = []
            for a in range(per_dev):
                block = slice(a * BLK, (a + 1) * BLK)
                q = q_refs[t][block, kcols]
                peak = jnp.full((BLK, BLK), NEG, jnp.float32)
                for i in range(span):
                    keys = kv[pl.ds(pl.multiple_of(start + i * rows, BLK), rows), kcols]
                    s = lax.dot_general(q, keys, (((1,), (1,)), ((), ())), preferred_element_type=jnp.float32)
                    for b in range(per_dev):
                        j = i * per_dev + b
                        part = s[:, b * BLK : (b + 1) * BLK] + biases[j][a]
                        peak = jnp.maximum(peak, part)
                        scores[block, j * BLK : (j + 1) * BLK] = part
                top = jnp.broadcast_to(jnp.max(peak, axis=1, keepdims=True), (BLK, BLK))
                total = jnp.zeros((BLK, BLK), jnp.float32)
                for j in range(span * per_dev):
                    cols = slice(j * BLK, (j + 1) * BLK)
                    e = jnp.exp2((scores[block, cols] - top) * TO_EXP2)
                    total += e
                    weights[block, cols] = e.astype(jnp.bfloat16)
                sums.append(jnp.sum(total, axis=1, keepdims=True))
            values = kv[pl.ds(start, span * rows), vcols]
            mixed = jnp.dot(weights[...], values, preferred_element_type=jnp.float32)
            o_refs[t][:, kcols] = (mixed / jnp.concatenate(sums, axis=0)).astype(jnp.bfloat16)
            return carry

        lax.fori_loop(0, HL, one_head, 0)


def attend(tiles, mask, q, kv):
    rows = kv[0].shape[0]
    span = (2 * REACH + 1) * rows
    vmem = pl.BlockSpec(memory_space=pltpu.VMEM)
    return pl.pallas_call(
        lambda *refs: attend_kernel(tiles, *refs),
        out_shape=[jax.ShapeDtypeStruct((rows, HC), jnp.bfloat16)] * len(tiles),
        in_specs=[pl.BlockSpec(memory_space=pltpu.SMEM)]
        + [vmem] * len(tiles)
        + [pl.BlockSpec(memory_space=pl.ANY)] * (3 * LANES),
        out_specs=[vmem] * len(tiles),
        scratch_shapes=[
            pltpu.VMEM((3 * LANES * rows, 2 * HC), jnp.bfloat16),
            pltpu.VMEM((rows, span), jnp.float32),
            pltpu.VMEM((rows, span), jnp.bfloat16),
            pltpu.SemaphoreType.DMA((3 * LANES,)),
        ],
        compiler_params=pltpu.CompilerParams(vmem_limit_bytes=56 * 1024 * 1024),
    )(mask, *[q[t] for t in tiles], *kv)


def project_kernel(order, a_refs, w_ref, o_ref, by_lane, by_shard):
    depth = by_shard.shape[1]
    shard = depth // len(order)

    @pl.when(pl.program_id(0) == 0)
    def _():
        for step in range(LANES):
            by_lane[lane_of(step)] = a_refs[step][...]
        parts = []
        for place in order:
            lane, at = place * shard // HC, place * shard % HC
            parts.append(by_lane[lane][:, at : at + shard])
        by_shard[...] = jnp.concatenate(parts, axis=1)

    o_ref[...] = jnp.dot(by_shard[...], w_ref[...], preferred_element_type=jnp.float32).astype(jnp.bfloat16)


def project(attended, weight, order, steps):
    count, depth = attended[0].shape
    channels, columns = weight.shape
    width = columns // steps
    whole = pl.BlockSpec((count, depth), lambda n: (0, 0))
    return pl.pallas_call(
        lambda *refs: project_kernel(order, refs[:LANES], *refs[LANES:]),
        out_shape=jax.ShapeDtypeStruct((count, columns), jnp.bfloat16),
        grid=(steps,),
        in_specs=[whole] * LANES + [pl.BlockSpec((channels, width), lambda n: (0, n))],
        out_specs=pl.BlockSpec((count, width), lambda n: (0, n)),
        scratch_shapes=[
            pltpu.VMEM((LANES, count, depth), jnp.bfloat16),
            pltpu.VMEM((count, channels), jnp.bfloat16),
        ],
        compiler_params=pltpu.CompilerParams(vmem_limit_bytes=56 * 1024 * 1024),
    )(*attended, weight)


def after(x, *others):
    return lax.optimization_barrier((x, *others))[0]


def on_device(queries, keys, values, frame_index, block_mask, out_weight):
    count = queries.shape[0]
    planes = lax.axis_size("plane")
    seq = ("plane", "row", "core")

    def index(p, r, c):
        return (p * 2 + r) * 2 + c

    every = [(p, r, c) for p in range(planes) for r in range(2) for c in range(2)]

    def to_lane(x, dr, dc):
        return lax.ppermute(x, seq, [(index(p, r, c), index(p, r ^ dr, c ^ dc)) for p, r, c in every])

    def to_plane(x, dp, dc):
        pairs = [
            (index(p, r, c), index(p + dp, r, c ^ dc)) for p, r, c in every if 0 <= p + dp < planes
        ]
        return lax.ppermute(x, seq, pairs)

    walk = [(p, 0) for p in range(planes)] + [(p, 1) for p in reversed(range(planes))]
    order = [index(p, r, c) for p, r in walk for c in range(2)]
    weight = lax.all_gather(out_weight, seq, axis=0, tiled=True, axis_index_groups=[order])

    kv = pack(pack_kv_kernel, frame_index, (keys, values), 2 * HC)
    across = [to_lane(kv[2], 1, 0), to_lane(kv[3], 1, 1)]
    early = {(dp, dc): to_plane(kv[dc], dp, dc) for dc in range(2) for dp in (1, -1)}
    here = [kv[0], to_lane(kv[1], 0, 1)] + across
    q = pack(pack_q_kernel, frame_index, (after(queries, kv[0]),), HC)
    late = {(dp, dc): to_plane(across[dc], dp, 0) for dc in range(2) for dp in (1, -1)}
    q = [q[0]] + [to_lane(after(q[d], *across), d // 2, d % 2) for d in range(1, LANES)]
    lower = [early[1, 0], early[1, 1], late[1, 0], late[1, 1]]
    upper = [early[-1, 0], early[-1, 1], late[-1, 0], late[-1, 1]]

    pieces = lower + here + upper
    attended = dict(zip((2, 3), attend((2, 3), block_mask, q, pieces)))
    back = {d: to_lane(attended[d], 1, d % 2) for d in (2, 3)}
    attended = dict(zip((0, 1), attend((0, 1), after(block_mask, attended[2]), q, pieces)))
    mixed = [attended[0], to_lane(attended[1], 0, 1), back[2], back[3]]
    return project(mixed, weight, order, 6)


def solution(mesh):
    groups, seq = mesh.devices.shape
    split = Mesh(
        mesh.devices.reshape(groups, seq // LANES, LANES // 2, 2), ("groups", "plane", "row", "core")
    )
    along = ("plane", "row", "core")
    tokens = P(("groups",) + along, None)
    return jax.shard_map(
        on_device,
        mesh=split,
        in_specs=(tokens, tokens, tokens, P(("groups",) + along), P(), P(along, None)),
        out_specs=tokens,
        check_vma=False,
    )
```

```python
import math

import jax
import jax.numpy as jnp
from jax import lax
from jax.experimental import pallas as pl
from jax.experimental.pallas import tpu as pltpu
from jax.sharding import Mesh
from jax.sharding import PartitionSpec as P

HEADS = 12
HDIM = 128
TCH = 16
BLK = 128
LANES = 4
HL = HEADS // LANES
HC = HL * HDIM
REACH = 4
NEG = -1e30
TO_EXP2 = math.log2(math.e) / math.sqrt(HDIM)


def turn_tables(frames, same, other):
    lane = lax.broadcasted_iota(jnp.int32, (8, HDIM), 1)
    half = TCH // 2
    channel = lax.rem(lane, half).astype(jnp.float32)
    for block in range(same.shape[0]):
        angle = frames[block].astype(jnp.float32) * jnp.exp2(-channel)
        cosine, sine = jnp.cos(angle), jnp.sin(angle)
        same[block] = jnp.where(lane < TCH, cosine, 1.0)
        other[block] = jnp.where(lane < half, -sine, jnp.where(lane < TCH, sine, 0.0))


def lane_of(step):
    mine = lax.axis_index("row") * 2 + lax.axis_index("core")
    return lax.bitwise_xor(mine, step)


def turn_into(frames, x_ref, outs, same, other):
    turn_tables(frames, same, other)
    half = TCH // 2
    lane = lax.broadcasted_iota(jnp.int32, (BLK, HDIM), 1)
    for step in range(LANES):
        for head in range(HL):
            start = pl.multiple_of(lane_of(step) * HC + head * HDIM, HDIM)
            for block in range(x_ref.shape[0] // BLK):
                rows = slice(block * BLK, (block + 1) * BLK)
                x = x_ref[rows, pl.ds(start, HDIM)].astype(jnp.float32)
                partner = jnp.where(lane < half, pltpu.roll(x, HDIM - half, 1), pltpu.roll(x, half, 1))
                turned = x * same[block, :1] + partner * other[block, :1]
                outs[step][rows, head * HDIM : (head + 1) * HDIM] = turned.astype(jnp.bfloat16)


def pack_kv_kernel(frames, k_ref, v_ref, *rest):
    outs, tables = rest[:LANES], rest[LANES:]
    turn_into(frames, k_ref, outs, *tables)
    for step in range(LANES):
        start = pl.multiple_of(lane_of(step) * HC, HDIM)
        outs[step][:, HC:] = v_ref[:, pl.ds(start, HC)]


def pack_q_kernel(frames, q_ref, *rest):
    turn_into(frames, q_ref, rest[:LANES], *rest[LANES:])


def pack(kernel, frames, arrays, width):
    count = arrays[0].shape[0]
    table = pltpu.VMEM((count // BLK, 8, HDIM), jnp.float32)
    return pl.pallas_call(
        kernel,
        out_shape=[jax.ShapeDtypeStruct((count, width), jnp.bfloat16)] * LANES,
        in_specs=[pl.BlockSpec(memory_space=pltpu.SMEM)]
        + [pl.BlockSpec(memory_space=pltpu.VMEM) for _ in arrays],
        out_specs=[pl.BlockSpec(memory_space=pltpu.VMEM)] * LANES,
        scratch_shapes=[table, table],
        compiler_params=pltpu.CompilerParams(vmem_limit_bytes=56 * 1024 * 1024),
    )(frames, *arrays)


def biases_of(mask, me, devices, per_dev):
    nblk = mask.shape[0]
    biases = []
    for device in devices:
        for b in range(per_dev):
            key_block = device * per_dev + b
            inside = (key_block >= 0) & (key_block < nblk)
            column = jnp.clip(key_block, 0, nblk - 1)
            biases.append(
                [jnp.where(inside & (mask[me * per_dev + a, column] > 0), 0.0, NEG) for a in range(per_dev)]
            )
    return biases


def attend_head(h, q, kv, starts, biases, scores, weights, state):
    rows = q.shape[0]
    per_dev = rows // BLK
    kcols = slice(h * HDIM, (h + 1) * HDIM)
    vcols = slice(HC + h * HDIM, HC + (h + 1) * HDIM)
    peak = jnp.full((rows, BLK), NEG, jnp.float32)
    for i, start in enumerate(starts):
        keys = kv[pl.ds(start, rows), kcols]
        s = lax.dot_general(q, keys, (((1,), (1,)), ((), ())), preferred_element_type=jnp.float32)
        for b in range(per_dev):
            j = i * per_dev + b
            parts = [
                s[a * BLK : (a + 1) * BLK, b * BLK : (b + 1) * BLK] + biases[j][a] for a in range(per_dev)
            ]
            part = jnp.concatenate(parts, axis=0)
            peak = jnp.maximum(peak, part)
            scores[h, :, j * BLK : (j + 1) * BLK] = part
    top = jnp.max(peak, axis=1, keepdims=True)
    if state is not None:
        top = jnp.maximum(top, state[0])
    total = jnp.zeros((rows, BLK), jnp.float32)
    for j in range(len(starts) * per_dev):
        cols = slice(j * BLK, (j + 1) * BLK)
        e = jnp.exp2((scores[h, :, cols] - top) * TO_EXP2)
        total += e
        weights[h, :, cols] = e.astype(jnp.bfloat16)
    mixed = None
    for i, start in enumerate(starts):
        part = jnp.dot(
            weights[h, :, i * rows : (i + 1) * rows],
            kv[pl.ds(start, rows), vcols],
            preferred_element_type=jnp.float32,
        )
        mixed = part if mixed is None else mixed + part
    total = jnp.sum(total, axis=1, keepdims=True)
    if state is not None:
        shrink = jnp.exp2((state[0] - top) * TO_EXP2)
        total += state[1] * shrink
        mixed += state[2] * shrink
    return top, total, mixed


def fetch(pairs, sems):
    copies = [pltpu.make_async_copy(source, target, sems.at[i]) for i, (source, target) in enumerate(pairs)]
    for copy in copies:
        copy.start()
    for copy in copies:
        copy.wait()


def begin_kernel(mask, *refs):
    q_refs, kv_refs, rest = refs[:LANES], refs[LANES : 3 * LANES], refs[3 * LANES :]
    accs, stats, (q_all, kv, scores, weights, sems) = rest[:2], rest[2:4], rest[4:]
    rows = q_all.shape[1]
    per_dev = rows // BLK
    plane = lax.axis_index("plane")
    pairs = [(q_refs[step], q_all.at[step]) for step in range(LANES)]
    places = [LANES + lane_of(step) for step in range(LANES)]
    places += [part * LANES + lane_of(step) for part in (0, 2) for step in range(2)]
    for ref, place in zip(kv_refs, places):
        pairs.append((ref, kv.at[pl.ds(pl.multiple_of(place * rows, BLK), rows)]))
    fetch(pairs, sems)
    for group in range(2):

        def one_tile(core, carry):
            step = 2 * group + core
            tile = lane_of(step)
            me = plane * LANES + tile
            devices = [plane * LANES + lane for lane in range(LANES)]
            devices += chunk_devices_at(group, tile, False)
            starts = [pl.multiple_of((d - (plane - 1) * LANES) * rows, BLK) for d in devices]
            biases = biases_of(mask, me, devices, per_dev)
            for h in range(HL):
                cols = slice(h * HDIM, (h + 1) * HDIM)
                q = q_all[step, :, cols]
                top, total, mixed = attend_head(h, q, kv, starts, biases, scores, weights, None)
                accs[group][core, :, cols] = mixed
                stats[group][core, :, h : h + 1] = top
                stats[group][core, :, HL + h : HL + h + 1] = total
            return carry

        lax.fori_loop(0, 2, one_tile, 0)


def chunk_devices_at(group, tile, late):
    plane = lax.axis_index("plane")
    me = plane * LANES + tile
    row, core = lax.div(tile, 2), lax.rem(tile, 2)
    if late == (group == 1):
        return [me - REACH, me + REACH, jnp.where(core == 0, me - REACH + 1, me + REACH - 1)]
    first = jnp.where(row == 0, (plane - 1) * LANES + 2, (plane + 1) * LANES)
    return [first, first + 1]


def finish_kernel(group, mask, q_a, q_b, acc, stat, *refs):
    kv_refs, o_refs, (kv, scores, weights, sems) = refs[:LANES], refs[LANES : LANES + 2], refs[LANES + 2 :]
    rows = q_a.shape[0]
    per_dev = rows // BLK
    plane = lax.axis_index("plane")
    places = [part * LANES + lane_of(step) for part in (0, 2) for step in (2, 3)]
    fetch(
        [
            (ref, kv.at[pl.ds(pl.multiple_of(place * rows, BLK), rows)])
            for ref, place in zip(kv_refs, places)
        ],
        sems,
    )
    for core, (q_ref, o_ref) in enumerate(zip((q_a, q_b), o_refs)):
        tile = lane_of(2 * group + core)
        me = plane * LANES + tile
        devices = chunk_devices_at(group, tile, True)
        starts = [pl.multiple_of((d - (plane - 1) * LANES) * rows, BLK) for d in devices]
        biases = biases_of(mask, me, devices, per_dev)
        for h in range(HL):
            cols = slice(h * HDIM, (h + 1) * HDIM)
            state = (stat[core, :, h : h + 1], stat[core, :, HL + h : HL + h + 1], acc[core, :, cols])
            _, total, mixed = attend_head(h, q_ref[:, cols], kv, starts, biases, scores, weights, state)
            o_ref[:, cols] = (mixed / total).astype(jnp.bfloat16)


def attend_begin(mask, q, kv):
    rows = kv[0].shape[0]
    span = 7 * rows
    vmem = pl.BlockSpec(memory_space=pltpu.VMEM)
    return pl.pallas_call(
        begin_kernel,
        out_shape=[jax.ShapeDtypeStruct((2, rows, HC), jnp.float32)] * 2
        + [jax.ShapeDtypeStruct((2, rows, HDIM), jnp.float32)] * 2,
        in_specs=[pl.BlockSpec(memory_space=pltpu.SMEM)] + [pl.BlockSpec(memory_space=pl.ANY)] * (3 * LANES),
        out_specs=[vmem] * 4,
        scratch_shapes=[
            pltpu.VMEM((LANES, rows, HC), jnp.bfloat16),
            pltpu.VMEM((3 * LANES * rows, 2 * HC), jnp.bfloat16),
            pltpu.VMEM((HL, rows, span), jnp.float32),
            pltpu.VMEM((HL, rows, span), jnp.bfloat16),
            pltpu.SemaphoreType.DMA((3 * LANES,)),
        ],
        compiler_params=pltpu.CompilerParams(vmem_limit_bytes=56 * 1024 * 1024),
    )(mask, *q, *kv)


def attend_finish(group, mask, q, acc, stat, kv):
    rows = kv[0].shape[0]
    span = 3 * rows
    vmem = pl.BlockSpec(memory_space=pltpu.VMEM)
    return pl.pallas_call(
        lambda *refs: finish_kernel(group, *refs),
        out_shape=[jax.ShapeDtypeStruct((rows, HC), jnp.bfloat16)] * 2,
        in_specs=[pl.BlockSpec(memory_space=pltpu.SMEM)]
        + [vmem] * 4
        + [pl.BlockSpec(memory_space=pl.ANY)] * LANES,
        out_specs=[vmem] * 2,
        scratch_shapes=[
            pltpu.VMEM((3 * LANES * rows, 2 * HC), jnp.bfloat16),
            pltpu.VMEM((HL, rows, span), jnp.float32),
            pltpu.VMEM((HL, rows, span), jnp.bfloat16),
            pltpu.SemaphoreType.DMA((LANES,)),
        ],
        compiler_params=pltpu.CompilerParams(vmem_limit_bytes=56 * 1024 * 1024),
    )(mask, *q, acc, stat, *kv)


def project_kernel(order, groups, a_refs, w_refs, o_ref, by_lane, by_shard):
    step = pl.program_id(0)
    depth = by_shard.shape[1]
    shard = depth // len(order)

    @pl.when(step == 0)
    def _():
        for d in range(LANES):
            by_lane[lane_of(d)] = a_refs[d][...]
        parts = []
        for place in order:
            lane, at = place * shard // HC, place * shard % HC
            parts.append(by_lane[lane][:, at : at + shard])
        by_shard[...] = jnp.concatenate(parts, axis=1)

    mine, core = lax.axis_index("groups"), lax.axis_index("core")
    widths = [w.shape[1] for w in w_refs]
    steps = o_ref.shape[1] // (widths[0] + groups * widths[1])
    direct, strip, half = widths[0] * steps, widths[1] * steps, widths[1] * steps // 2
    places = [0, direct + mine * strip]
    for dx in range(1, groups):
        start = direct + lax.rem(mine + groups - dx, groups) * strip
        places += [start + core * half, start + (1 - core) * half]
    for w_ref, place, width in zip(w_refs, places, widths):
        out = jnp.dot(by_shard[...], w_ref[...], preferred_element_type=jnp.float32)
        at = pl.multiple_of(place + step * width, HDIM)
        o_ref[:, pl.ds(at, width)] = out.astype(jnp.bfloat16)


def project(attended, weights, order, groups):
    count, depth = attended[0].shape
    channels = weights[0].shape[0]
    steps = weights[-1].shape[1] // HDIM
    columns = weights[0].shape[1] + groups * weights[1].shape[1]
    whole = pl.BlockSpec((count, depth), lambda n: (0, 0))
    return pl.pallas_call(
        lambda *refs: project_kernel(order, groups, refs[:LANES], refs[LANES:-3], *refs[-3:]),
        out_shape=jax.ShapeDtypeStruct((count, columns), jnp.bfloat16),
        grid=(steps,),
        in_specs=[whole] * LANES
        + [pl.BlockSpec((channels, w.shape[1] // steps), lambda n: (0, n)) for w in weights],
        out_specs=pl.BlockSpec((count, columns), lambda n: (0, 0)),
        scratch_shapes=[
            pltpu.VMEM((LANES, count, depth), jnp.bfloat16),
            pltpu.VMEM((count, channels), jnp.bfloat16),
        ],
        compiler_params=pltpu.CompilerParams(vmem_limit_bytes=56 * 1024 * 1024),
    )(*attended, *weights)


def after(x, *others):
    return lax.optimization_barrier((x, *others))[0]


def on_device(queries, keys, values, frame_index, block_mask, out_weight):
    count = queries.shape[0]
    planes, groups = lax.axis_size("plane"), lax.axis_size("groups")
    seq = ("plane", "row", "core")

    def index(p, r, c):
        return (p * 2 + r) * 2 + c

    every = [(p, r, c) for p in range(planes) for r in range(2) for c in range(2)]

    def to_lane(x, dr, dc):
        return lax.ppermute(x, seq, [(index(p, r, c), index(p, r ^ dr, c ^ dc)) for p, r, c in every])

    def to_plane(x, dp, dc):
        pairs = [
            (index(p, r, c), index(p + dp, r, c ^ dc)) for p, r, c in every if 0 <= p + dp < planes
        ]
        return lax.ppermute(x, seq, pairs)

    walk = [(p, 0) for p in range(planes)] + [(p, 1) for p in reversed(range(planes))]
    order = [index(p, r, c) for p, r in walk for c in range(2)]

    def gather(part):
        return lax.all_gather(part, seq, axis=0, tiled=True, axis_index_groups=[order])

    columns = out_weight.shape[1]
    strip = 2 * columns // 3 // (groups * 2 * HDIM) * 2 * HDIM
    direct = columns - groups * strip
    strip_at = direct + lax.axis_index("groups") * strip
    own_strip = gather(lax.dynamic_slice_in_dim(out_weight, strip_at, strip, 1))

    kv = pack(pack_kv_kernel, frame_index, (keys, values), 2 * HC)
    across = [to_lane(kv[2], 1, 0), to_lane(kv[3], 1, 1)]
    early = {(dp, dc): to_plane(kv[dc], dp, dc) for dc in range(2) for dp in (1, -1)}
    here = [kv[0], to_lane(kv[1], 0, 1)] + across
    q = pack(pack_q_kernel, frame_index, (after(queries, across[0]),), HC)
    late = {(dp, dc): to_plane(across[dc], dp, 0) for dc in range(2) for dp in (1, -1)}
    q = [q[0]] + [to_lane(after(q[d], *across), d // 2, d % 2) for d in range(1, LANES)]

    own_strip = after(own_strip, *early.values())
    half = strip // 2
    core_at = lax.axis_index("core") * half
    sent = lax.dynamic_slice_in_dim(own_strip, core_at, half, 1)
    halves = [
        lax.ppermute(sent, "groups", [(g, (g + dx) % groups) for g in range(groups)])
        for dx in range(1, groups)
    ]
    begun = attend_begin(
        after(block_mask, sent), q, here + [early[dp, dc] for dp in (1, -1) for dc in range(2)]
    )
    late = [after(late[dp, dc], begun[0]) for dp in (1, -1) for dc in range(2)]
    direct_strip = gather(after(out_weight[:, :direct], *late))
    mixed = attend_finish(1, block_mask, q[2:], begun[1], begun[3], late)
    back = [to_lane(mixed[d], 1, d) for d in range(2)]
    mixed = attend_finish(0, after(block_mask, mixed[0]), q[:2], begun[0], begun[2], late)
    mixed = [mixed[0], to_lane(mixed[1], 0, 1)] + back
    weights = [direct_strip, own_strip]
    for x in halves:
        x = after(x, mixed[0])
        weights += [x, lax.ppermute(x, "core", [(0, 1), (1, 0)])]
    return project(mixed, weights, order, groups)


def solution(mesh):
    groups, seq = mesh.devices.shape
    split = Mesh(
        mesh.devices.reshape(groups, seq // LANES, LANES // 2, 2), ("groups", "plane", "row", "core")
    )
    along = ("plane", "row", "core")
    tokens = P(("groups",) + along, None)
    return jax.shard_map(
        on_device,
        mesh=split,
        in_specs=(tokens, tokens, tokens, P(("groups",) + along), P(), P(along, None)),
        out_specs=tokens,
        check_vma=False,
    )
```

```python
import math

import jax
import jax.numpy as jnp
from jax import lax
from jax.experimental import pallas as pl
from jax.experimental.pallas import tpu as pltpu
from jax.sharding import Mesh
from jax.sharding import PartitionSpec as P

HEADS = 12
HDIM = 128
TCH = 16
BLK = 128
LANES = 4
HL = HEADS // LANES
HC = HL * HDIM
REACH = 4
NEG = -1e30
BRIEF = pl.CostEstimate(flops=1024, bytes_accessed=1024, transcendentals=0)
TO_EXP2 = math.log2(math.e) / math.sqrt(HDIM)


def turn_tables(frames, same, other):
    lane = lax.broadcasted_iota(jnp.int32, (8, HDIM), 1)
    half = TCH // 2
    channel = lax.rem(lane, half).astype(jnp.float32)
    for block in range(same.shape[0]):
        angle = frames[block].astype(jnp.float32) * jnp.exp2(-channel)
        cosine, sine = jnp.cos(angle), jnp.sin(angle)
        same[block] = jnp.where(lane < TCH, cosine, 1.0)
        other[block] = jnp.where(lane < half, -sine, jnp.where(lane < TCH, sine, 0.0))


def lane_of(step):
    mine = lax.axis_index("row") * 2 + lax.axis_index("core")
    return lax.bitwise_xor(mine, step)


def turn_into(frames, x_ref, outs, same, other):
    turn_tables(frames, same, other)
    half = TCH // 2
    lane = lax.broadcasted_iota(jnp.int32, (BLK, HDIM), 1)
    for step in range(LANES):
        for head in range(HL):
            start = pl.multiple_of(lane_of(step) * HC + head * HDIM, HDIM)
            for block in range(x_ref.shape[0] // BLK):
                rows = slice(block * BLK, (block + 1) * BLK)
                x = x_ref[rows, pl.ds(start, HDIM)].astype(jnp.float32)
                partner = jnp.where(lane < half, pltpu.roll(x, HDIM - half, 1), pltpu.roll(x, half, 1))
                turned = x * same[block, :1] + partner * other[block, :1]
                outs[step][rows, head * HDIM : (head + 1) * HDIM] = turned.astype(jnp.bfloat16)


def pack_kv_kernel(frames, k_ref, v_ref, *rest):
    outs, tables = rest[:LANES], rest[LANES:]
    turn_into(frames, k_ref, outs, *tables)
    for step in range(LANES):
        start = pl.multiple_of(lane_of(step) * HC, HDIM)
        outs[step][:, HC:] = v_ref[:, pl.ds(start, HC)]


def pack_q_kernel(frames, q_ref, *rest):
    turn_into(frames, q_ref, rest[:LANES], *rest[LANES:])


def pack(kernel, frames, arrays, width):
    count = arrays[0].shape[0]
    table = pltpu.VMEM((count // BLK, 8, HDIM), jnp.float32)
    return pl.pallas_call(
        kernel,
        out_shape=[jax.ShapeDtypeStruct((count, width), jnp.bfloat16)] * LANES,
        in_specs=[pl.BlockSpec(memory_space=pltpu.SMEM)]
        + [pl.BlockSpec(memory_space=pltpu.VMEM) for _ in arrays],
        out_specs=[pl.BlockSpec(memory_space=pltpu.VMEM)] * LANES,
        scratch_shapes=[table, table],
        compiler_params=pltpu.CompilerParams(vmem_limit_bytes=56 * 1024 * 1024),
    )(frames, *arrays)


def biases_of(mask, me, devices, per_dev):
    nblk = mask.shape[0]
    biases = []
    for device in devices:
        for b in range(per_dev):
            key_block = device * per_dev + b
            inside = (key_block >= 0) & (key_block < nblk)
            column = jnp.clip(key_block, 0, nblk - 1)
            biases.append(
                [jnp.where(inside & (mask[me * per_dev + a, column] > 0), 0.0, NEG) for a in range(per_dev)]
            )
    return biases


def attend_head(h, q, kv, starts, biases, scores, weights, state):
    rows = q.shape[0]
    per_dev = rows // BLK
    kcols = slice(h * HDIM, (h + 1) * HDIM)
    vcols = slice(HC + h * HDIM, HC + (h + 1) * HDIM)
    peak = jnp.full((rows, BLK), NEG, jnp.float32)
    for i, start in enumerate(starts):
        keys = kv[pl.ds(start, rows), kcols]
        s = lax.dot_general(q, keys, (((1,), (1,)), ((), ())), preferred_element_type=jnp.float32)
        for b in range(per_dev):
            j = i * per_dev + b
            parts = [
                s[a * BLK : (a + 1) * BLK, b * BLK : (b + 1) * BLK] + biases[j][a] for a in range(per_dev)
            ]
            part = jnp.concatenate(parts, axis=0)
            peak = jnp.maximum(peak, part)
            scores[h, :, j * BLK : (j + 1) * BLK] = part
    top = jnp.max(peak, axis=1, keepdims=True)
    if state is not None:
        top = jnp.maximum(top, state[0])
    total = jnp.zeros((rows, BLK), jnp.float32)
    for j in range(len(starts) * per_dev):
        cols = slice(j * BLK, (j + 1) * BLK)
        e = jnp.exp2((scores[h, :, cols] - top) * TO_EXP2)
        total += e
        weights[h, :, cols] = e.astype(jnp.bfloat16)
    mixed = None
    for i, start in enumerate(starts):
        part = jnp.dot(
            weights[h, :, i * rows : (i + 1) * rows],
            kv[pl.ds(start, rows), vcols],
            preferred_element_type=jnp.float32,
        )
        mixed = part if mixed is None else mixed + part
    total = jnp.sum(total, axis=1, keepdims=True)
    if state is not None:
        shrink = jnp.exp2((state[0] - top) * TO_EXP2)
        total += state[1] * shrink
        mixed += state[2] * shrink
    return top, total, mixed


def fetch(pairs, sems):
    copies = [pltpu.make_async_copy(source, target, sems.at[i]) for i, (source, target) in enumerate(pairs)]
    for copy in copies:
        copy.start()
    for copy in copies:
        copy.wait()


def begin_kernel(mask, *refs):
    q_refs, kv_refs, rest = refs[:LANES], refs[LANES : 3 * LANES], refs[3 * LANES :]
    accs, stats, (q_all, kv, scores, weights, sems) = rest[:2], rest[2:4], rest[4:]
    rows = q_all.shape[1]
    per_dev = rows // BLK
    plane = lax.axis_index("plane")
    pairs = [(q_refs[step], q_all.at[step]) for step in range(LANES)]
    places = [LANES + lane_of(step) for step in range(LANES)]
    places += [part * LANES + lane_of(step) for part in (0, 2) for step in range(2)]
    for ref, place in zip(kv_refs, places):
        pairs.append((ref, kv.at[pl.ds(pl.multiple_of(place * rows, BLK), rows)]))
    fetch(pairs, sems)
    for group in range(2):

        def one_tile(core, carry):
            step = 2 * group + core
            tile = lane_of(step)
            me = plane * LANES + tile
            devices = [plane * LANES + lane for lane in range(LANES)]
            devices += chunk_devices_at(group, tile, False)
            starts = [pl.multiple_of((d - (plane - 1) * LANES) * rows, BLK) for d in devices]
            biases = biases_of(mask, me, devices, per_dev)
            for h in range(HL):
                cols = slice(h * HDIM, (h + 1) * HDIM)
                q = q_all[step, :, cols]
                top, total, mixed = attend_head(h, q, kv, starts, biases, scores, weights, None)
                accs[group][core, :, cols] = mixed
                stats[group][core, :, h : h + 1] = top
                stats[group][core, :, HL + h : HL + h + 1] = total
            return carry

        lax.fori_loop(0, 2, one_tile, 0)


def chunk_devices_at(group, tile, late):
    plane = lax.axis_index("plane")
    me = plane * LANES + tile
    row, core = lax.div(tile, 2), lax.rem(tile, 2)
    if late == (group == 1):
        return [me - REACH, me + REACH, jnp.where(core == 0, me - REACH + 1, me + REACH - 1)]
    first = jnp.where(row == 0, (plane - 1) * LANES + 2, (plane + 1) * LANES)
    return [first, first + 1]


def finish_kernel(steps, mask, *refs):
    count = len(steps)
    q_refs, accs, stats = refs[:count], refs[count : 2 * count], refs[2 * count : 3 * count]
    kv_refs, o_refs = refs[3 * count : 3 * count + LANES], refs[3 * count + LANES : 4 * count + LANES]
    kv, scores, weights, sems = refs[4 * count + LANES :]
    rows = q_refs[0].shape[0]
    per_dev = rows // BLK
    plane = lax.axis_index("plane")
    places = [part * LANES + lane_of(step) for part in (0, 2) for step in (2, 3)]
    fetch(
        [
            (ref, kv.at[pl.ds(pl.multiple_of(place * rows, BLK), rows)])
            for ref, place in zip(kv_refs, places)
        ],
        sems,
    )
    for step, q_ref, acc, stat, o_ref in zip(steps, q_refs, accs, stats, o_refs):
        tile = lane_of(step)
        me = plane * LANES + tile
        devices = chunk_devices_at(step // 2, tile, True)
        starts = [pl.multiple_of((d - (plane - 1) * LANES) * rows, BLK) for d in devices]
        biases = biases_of(mask, me, devices, per_dev)
        for h in range(HL):
            cols = slice(h * HDIM, (h + 1) * HDIM)
            state = (stat[0, :, h : h + 1], stat[0, :, HL + h : HL + h + 1], acc[0, :, cols])
            _, total, mixed = attend_head(h, q_ref[:, cols], kv, starts, biases, scores, weights, state)
            o_ref[:, cols] = (mixed / total).astype(jnp.bfloat16)


def attend_begin(mask, q, kv):
    rows = kv[0].shape[0]
    span = 7 * rows
    vmem = pl.BlockSpec(memory_space=pltpu.VMEM)
    return pl.pallas_call(
        begin_kernel,
        out_shape=[jax.ShapeDtypeStruct((2, rows, HC), jnp.float32)] * 2
        + [jax.ShapeDtypeStruct((2, rows, HDIM), jnp.float32)] * 2,
        in_specs=[pl.BlockSpec(memory_space=pltpu.SMEM)] + [pl.BlockSpec(memory_space=pl.ANY)] * (3 * LANES),
        out_specs=[vmem] * 4,
        scratch_shapes=[
            pltpu.VMEM((LANES, rows, HC), jnp.bfloat16),
            pltpu.VMEM((3 * LANES * rows, 2 * HC), jnp.bfloat16),
            pltpu.VMEM((HL, rows, span), jnp.float32),
            pltpu.VMEM((HL, rows, span), jnp.bfloat16),
            pltpu.SemaphoreType.DMA((3 * LANES,)),
        ],
        compiler_params=pltpu.CompilerParams(vmem_limit_bytes=56 * 1024 * 1024),
        cost_estimate=BRIEF,
    )(mask, *q, *kv)


def attend_finish(steps, mask, q, begun, kv):
    rows = kv[0].shape[0]
    span = 3 * rows
    vmem = pl.BlockSpec(memory_space=pltpu.VMEM)

    def of_tile(step, width):
        return pl.BlockSpec((1, rows, width), lambda i, step=step: (step % 2, 0, 0))

    return pl.pallas_call(
        lambda *refs: finish_kernel(steps, *refs),
        grid=(1,),
        out_shape=[jax.ShapeDtypeStruct((rows, HC), jnp.bfloat16)] * len(steps),
        in_specs=[pl.BlockSpec(memory_space=pltpu.SMEM)]
        + [vmem] * len(steps)
        + [of_tile(step, HC) for step in steps]
        + [of_tile(step, HDIM) for step in steps]
        + [pl.BlockSpec(memory_space=pl.ANY)] * LANES,
        out_specs=[vmem] * len(steps),
        scratch_shapes=[
            pltpu.VMEM((3 * LANES * rows, 2 * HC), jnp.bfloat16),
            pltpu.VMEM((HL, rows, span), jnp.float32),
            pltpu.VMEM((HL, rows, span), jnp.bfloat16),
            pltpu.SemaphoreType.DMA((LANES,)),
        ],
        compiler_params=pltpu.CompilerParams(vmem_limit_bytes=56 * 1024 * 1024),
        cost_estimate=BRIEF,
    )(
        mask,
        *[q[step] for step in steps],
        *[begun[step // 2] for step in steps],
        *[begun[2 + step // 2] for step in steps],
        *kv,
    )


def project_kernel(order, groups, a_refs, w_refs, o_ref, by_lane, by_shard):
    step = pl.program_id(0)
    depth = by_shard.shape[1]
    shard = depth // len(order)

    @pl.when(step == 0)
    def _():
        for d in range(LANES):
            by_lane[lane_of(d)] = a_refs[d][...]
        parts = []
        for place in order:
            lane, at = place * shard // HC, place * shard % HC
            parts.append(by_lane[lane][:, at : at + shard])
        by_shard[...] = jnp.concatenate(parts, axis=1)

    mine, core = lax.axis_index("groups"), lax.axis_index("core")
    widths = [w.shape[1] for w in w_refs]
    steps = o_ref.shape[1] // (widths[0] + groups * widths[1])
    direct, strip, half = widths[0] * steps, widths[1] * steps, widths[1] * steps // 2
    places = [0, direct + mine * strip]
    for dx in range(1, groups):
        start = direct + lax.rem(mine + groups - dx, groups) * strip
        places += [start + core * half, start + (1 - core) * half]
    for w_ref, place, width in zip(w_refs, places, widths):
        out = jnp.dot(by_shard[...], w_ref[...], preferred_element_type=jnp.float32)
        at = pl.multiple_of(place + step * width, HDIM)
        o_ref[:, pl.ds(at, width)] = out.astype(jnp.bfloat16)


def project(attended, weights, order, groups):
    count, depth = attended[0].shape
    channels = weights[0].shape[0]
    steps = weights[-1].shape[1] // HDIM
    columns = weights[0].shape[1] + groups * weights[1].shape[1]
    whole = pl.BlockSpec((count, depth), lambda n: (0, 0))
    return pl.pallas_call(
        lambda *refs: project_kernel(order, groups, refs[:LANES], refs[LANES:-3], *refs[-3:]),
        out_shape=jax.ShapeDtypeStruct((count, columns), jnp.bfloat16),
        grid=(steps,),
        in_specs=[whole] * LANES
        + [pl.BlockSpec((channels, w.shape[1] // steps), lambda n: (0, n)) for w in weights],
        out_specs=pl.BlockSpec((count, columns), lambda n: (0, 0)),
        scratch_shapes=[
            pltpu.VMEM((LANES, count, depth), jnp.bfloat16),
            pltpu.VMEM((count, channels), jnp.bfloat16),
        ],
        compiler_params=pltpu.CompilerParams(vmem_limit_bytes=56 * 1024 * 1024),
    )(*attended, *weights)


def after(x, *others):
    return lax.optimization_barrier((x, *others))[0]


def on_device(queries, keys, values, frame_index, block_mask, out_weight):
    count = queries.shape[0]
    planes, groups = lax.axis_size("plane"), lax.axis_size("groups")
    seq = ("plane", "row", "core")

    def index(p, r, c):
        return (p * 2 + r) * 2 + c

    every = [(p, r, c) for p in range(planes) for r in range(2) for c in range(2)]

    def to_lane(x, dr, dc):
        return lax.ppermute(x, seq, [(index(p, r, c), index(p, r ^ dr, c ^ dc)) for p, r, c in every])

    def to_plane(x, dp, dc):
        pairs = [
            (index(p, r, c), index(p + dp, r, c ^ dc)) for p, r, c in every if 0 <= p + dp < planes
        ]
        return lax.ppermute(x, seq, pairs)

    walk = [(p, 0) for p in range(planes)] + [(p, 1) for p in reversed(range(planes))]
    order = [index(p, r, c) for p, r in walk for c in range(2)]

    def gather(part):
        return lax.all_gather(part, seq, axis=0, tiled=True, axis_index_groups=[order])

    columns = out_weight.shape[1]
    strip = 2 * columns // 3 // (groups * 2 * HDIM) * 2 * HDIM
    direct = columns - groups * strip
    strip_at = direct + lax.axis_index("groups") * strip
    own_strip = gather(lax.dynamic_slice_in_dim(out_weight, strip_at, strip, 1))

    kv = pack(pack_kv_kernel, frame_index, (keys, values), 2 * HC)
    direct_strip = gather(after(out_weight, kv[0])[:, :direct])
    across = [to_lane(kv[2], 1, 0), to_lane(kv[3], 1, 1)]
    early = {(dp, dc): to_plane(kv[dc], dp, dc) for dc in range(2) for dp in (1, -1)}
    here = [kv[0], to_lane(kv[1], 0, 1)] + across
    q = pack(pack_q_kernel, frame_index, (after(queries, across[0]),), HC)
    onward = [after(x, *early.values(), here[1]) for x in across]
    late = {(dp, dc): to_plane(onward[dc], dp, 0) for dc in range(2) for dp in (1, -1)}
    q = [q[0]] + [to_lane(after(q[d], *across), d // 2, d % 2) for d in range(1, LANES)]

    own_strip = after(own_strip, *early.values(), q[1])
    half = strip // 2
    core_at = lax.axis_index("core") * half
    sent = lax.dynamic_slice_in_dim(own_strip, core_at, half, 1)
    halves = [
        lax.ppermute(sent, "groups", [(g, (g + dx) % groups) for g in range(groups)])
        for dx in range(1, groups)
    ]
    begun = attend_begin(
        after(block_mask, sent), q, here + [early[dp, dc] for dp in (1, -1) for dc in range(2)]
    )
    late = [after(late[dp, dc], begun[0]) for dp in (1, -1) for dc in range(2)]
    halves = [after(x, *late) for x in halves]
    swapped = [lax.ppermute(x, "core", [(0, 1), (1, 0)]) for x in halves]
    block_mask = after(block_mask, *halves)
    mixed = attend_finish((2, 3, 1), block_mask, q, begun, late)
    moved = [to_lane(x, step // 2, step % 2) for x, step in zip(mixed, (2, 3, 1))]
    own = attend_finish((0,), after(block_mask, mixed[0]), q, begun, late)
    mixed = [own[0], moved[2], moved[0], moved[1]]
    weights = [direct_strip, own_strip]
    for pair in zip(halves, swapped):
        weights += pair
    return project(mixed, weights, order, groups)


def solution(mesh):
    groups, seq = mesh.devices.shape
    split = Mesh(
        mesh.devices.reshape(groups, seq // LANES, LANES // 2, 2), ("groups", "plane", "row", "core")
    )
    along = ("plane", "row", "core")
    tokens = P(("groups",) + along, None)
    return jax.shard_map(
        on_device,
        mesh=split,
        in_specs=(tokens, tokens, tokens, P(("groups",) + along), P(), P(along, None)),
        out_specs=tokens,
        check_vma=False,
    )
```

```python
import math

import jax
import jax.numpy as jnp
from jax import lax
from jax.experimental import pallas as pl
from jax.experimental.pallas import tpu as pltpu
from jax.sharding import Mesh
from jax.sharding import PartitionSpec as P

HEADS = 12
HDIM = 128
TCH = 16
BLK = 128
LANES = 4
HL = HEADS // LANES
HC = HL * HDIM
REACH = 4
NEG = -1e30
BRIEF = pl.CostEstimate(flops=1024, bytes_accessed=1024, transcendentals=0)
TO_EXP2 = math.log2(math.e) / math.sqrt(HDIM)


def turn_tables(frames, same, other):
    lane = lax.broadcasted_iota(jnp.int32, (8, HDIM), 1)
    half = TCH // 2
    channel = lax.rem(lane, half).astype(jnp.float32)
    for block in range(same.shape[0]):
        angle = frames[block].astype(jnp.float32) * jnp.exp2(-channel)
        cosine, sine = jnp.cos(angle), jnp.sin(angle)
        same[block] = jnp.where(lane < TCH, cosine, 1.0)
        other[block] = jnp.where(lane < half, -sine, jnp.where(lane < TCH, sine, 0.0))


def lane_of(step):
    mine = lax.axis_index("row") * 2 + lax.axis_index("core")
    return lax.bitwise_xor(mine, step)


def turn_into(frames, x_ref, outs, same, other):
    turn_tables(frames, same, other)
    half = TCH // 2
    lane = lax.broadcasted_iota(jnp.int32, (BLK, HDIM), 1)
    for step in range(LANES):
        for head in range(HL):
            start = pl.multiple_of(lane_of(step) * HC + head * HDIM, HDIM)
            for block in range(x_ref.shape[0] // BLK):
                rows = slice(block * BLK, (block + 1) * BLK)
                x = x_ref[rows, pl.ds(start, HDIM)].astype(jnp.float32)
                partner = jnp.where(lane < half, pltpu.roll(x, HDIM - half, 1), pltpu.roll(x, half, 1))
                turned = x * same[block, :1] + partner * other[block, :1]
                cols = slice(head * HDIM, (head + 1) * HDIM)
                outs[step // 2][step % 2, rows, cols] = turned.astype(jnp.bfloat16)


def pack_kv_kernel(frames, k_ref, v_ref, *rest):
    outs, tables = rest[:2], rest[2:]
    turn_into(frames, k_ref, outs, *tables)
    for step in range(LANES):
        start = pl.multiple_of(lane_of(step) * HC, HDIM)
        outs[step // 2][step % 2, :, HC:] = v_ref[:, pl.ds(start, HC)]


def pack_q_kernel(frames, q_ref, *rest):
    turn_into(frames, q_ref, rest[:2], *rest[2:])


def pack(kernel, frames, arrays, width):
    count = arrays[0].shape[0]
    table = pltpu.VMEM((count // BLK, 8, HDIM), jnp.float32)
    return pl.pallas_call(
        kernel,
        out_shape=[jax.ShapeDtypeStruct((2, count, width), jnp.bfloat16)] * 2,
        in_specs=[pl.BlockSpec(memory_space=pltpu.SMEM)]
        + [pl.BlockSpec(memory_space=pltpu.VMEM) for _ in arrays],
        out_specs=[pl.BlockSpec(memory_space=pltpu.VMEM)] * 2,
        scratch_shapes=[table, table],
        compiler_params=pltpu.CompilerParams(vmem_limit_bytes=56 * 1024 * 1024),
    )(frames, *arrays)


def biases_of(mask, me, devices, per_dev):
    nblk = mask.shape[0]
    biases = []
    for device in devices:
        for b in range(per_dev):
            key_block = device * per_dev + b
            inside = (key_block >= 0) & (key_block < nblk)
            column = jnp.clip(key_block, 0, nblk - 1)
            biases.append(
                [jnp.where(inside & (mask[me * per_dev + a, column] > 0), 0.0, NEG) for a in range(per_dev)]
            )
    return biases


def attend_head(h, q, kv, starts, biases, scores, weights, state):
    rows = q.shape[0]
    per_dev = rows // BLK
    kcols = slice(h * HDIM, (h + 1) * HDIM)
    vcols = slice(HC + h * HDIM, HC + (h + 1) * HDIM)
    peak = jnp.full((rows, BLK), NEG, jnp.float32)
    for i, start in enumerate(starts):
        keys = kv[pl.ds(start, rows), kcols]
        s = lax.dot_general(q, keys, (((1,), (1,)), ((), ())), preferred_element_type=jnp.float32)
        for b in range(per_dev):
            j = i * per_dev + b
            parts = [
                s[a * BLK : (a + 1) * BLK, b * BLK : (b + 1) * BLK] + biases[j][a] for a in range(per_dev)
            ]
            part = jnp.concatenate(parts, axis=0)
            peak = jnp.maximum(peak, part)
            scores[h, :, j * BLK : (j + 1) * BLK] = part
    top = jnp.max(peak, axis=1, keepdims=True)
    if state is not None:
        top = jnp.maximum(top, state[0])
    total = jnp.zeros((rows, BLK), jnp.float32)
    for j in range(len(starts) * per_dev):
        cols = slice(j * BLK, (j + 1) * BLK)
        e = jnp.exp2((scores[h, :, cols] - top) * TO_EXP2)
        total += e
        weights[h, :, cols] = e.astype(jnp.bfloat16)
    mixed = None
    for i, start in enumerate(starts):
        part = jnp.dot(
            weights[h, :, i * rows : (i + 1) * rows],
            kv[pl.ds(start, rows), vcols],
            preferred_element_type=jnp.float32,
        )
        mixed = part if mixed is None else mixed + part
    total = jnp.sum(total, axis=1, keepdims=True)
    if state is not None:
        shrink = jnp.exp2((state[0] - top) * TO_EXP2)
        total += state[1] * shrink
        mixed += state[2] * shrink
    return top, total, mixed


def fetch(pairs, sems):
    copies = []
    for i, (source, target) in enumerate(pairs):
        source = source.at[0] if len(source.shape) == 3 else source
        copies.append(pltpu.make_async_copy(source, target, sems.at[i]))
    for copy in copies:
        copy.start()
    for copy in copies:
        copy.wait()


def begin_kernel(mask, *refs):
    q_refs, kv_refs, rest = refs[:LANES], refs[LANES : 3 * LANES], refs[3 * LANES :]
    accs, stats, (q_all, kv, scores, weights, sems) = rest[:2], rest[2:4], rest[4:]
    rows = q_all.shape[1]
    per_dev = rows // BLK
    plane = lax.axis_index("plane")
    pairs = [(q_refs[step], q_all.at[step]) for step in range(LANES)]
    places = [LANES + lane_of(step) for step in range(LANES)]
    places += [part * LANES + lane_of(step) for part in (0, 2) for step in range(2)]
    for ref, place in zip(kv_refs, places):
        pairs.append((ref, kv.at[pl.ds(pl.multiple_of(place * rows, BLK), rows)]))
    fetch(pairs, sems)
    for group in range(2):

        def one_tile(core, carry):
            step = 2 * group + core
            tile = lane_of(step)
            me = plane * LANES + tile
            devices = [plane * LANES + lane for lane in range(LANES)]
            devices += chunk_devices_at(group, tile, False)
            starts = [pl.multiple_of((d - (plane - 1) * LANES) * rows, BLK) for d in devices]
            biases = biases_of(mask, me, devices, per_dev)
            for h in range(HL):
                cols = slice(h * HDIM, (h + 1) * HDIM)
                q = q_all[step, :, cols]
                top, total, mixed = attend_head(h, q, kv, starts, biases, scores, weights, None)
                accs[group][core, :, cols] = mixed
                stats[group][core, :, h : h + 1] = top
                stats[group][core, :, HL + h : HL + h + 1] = total
            return carry

        lax.fori_loop(0, 2, one_tile, 0)


def chunk_devices_at(group, tile, late):
    plane = lax.axis_index("plane")
    me = plane * LANES + tile
    row, core = lax.div(tile, 2), lax.rem(tile, 2)
    if late == (group == 1):
        return [me - REACH, me + REACH, jnp.where(core == 0, me - REACH + 1, me + REACH - 1)]
    first = jnp.where(row == 0, (plane - 1) * LANES + 2, (plane + 1) * LANES)
    return [first, first + 1]


def finish_kernel(steps, mask, *refs):
    count = len(steps)
    q_refs, accs, stats = refs[:count], refs[count : 2 * count], refs[2 * count : 3 * count]
    kv_refs, o_refs = refs[3 * count : 3 * count + LANES], refs[3 * count + LANES : 4 * count + LANES]
    q_all, kv, scores, weights, sems = refs[4 * count + LANES :]
    rows = q_all.shape[1]
    per_dev = rows // BLK
    plane = lax.axis_index("plane")
    places = [part * LANES + lane_of(step) for part in (0, 2) for step in (2, 3)]
    pairs = [
        (ref, kv.at[pl.ds(pl.multiple_of(place * rows, BLK), rows)]) for ref, place in zip(kv_refs, places)
    ]
    pairs += [(ref, q_all.at[i]) for i, ref in enumerate(q_refs)]
    fetch(pairs, sems)
    for i, (step, acc, stat, o_ref) in enumerate(zip(steps, accs, stats, o_refs)):
        tile = lane_of(step)
        me = plane * LANES + tile
        devices = chunk_devices_at(step // 2, tile, True)
        starts = [pl.multiple_of((d - (plane - 1) * LANES) * rows, BLK) for d in devices]
        biases = biases_of(mask, me, devices, per_dev)
        for h in range(HL):
            cols = slice(h * HDIM, (h + 1) * HDIM)
            state = (stat[0, :, h : h + 1], stat[0, :, HL + h : HL + h + 1], acc[0, :, cols])
            _, total, mixed = attend_head(h, q_all[i, :, cols], kv, starts, biases, scores, weights, state)
            o_ref[:, cols] = (mixed / total).astype(jnp.bfloat16)


def attend_begin(mask, q, kv):
    rows = kv[1].shape[0]
    span = 7 * rows
    vmem = pl.BlockSpec(memory_space=pltpu.VMEM)
    return pl.pallas_call(
        begin_kernel,
        out_shape=[jax.ShapeDtypeStruct((2, rows, HC), jnp.float32)] * 2
        + [jax.ShapeDtypeStruct((2, rows, HDIM), jnp.float32)] * 2,
        in_specs=[pl.BlockSpec(memory_space=pltpu.SMEM)] + [pl.BlockSpec(memory_space=pl.ANY)] * (3 * LANES),
        out_specs=[vmem] * 4,
        scratch_shapes=[
            pltpu.VMEM((LANES, rows, HC), jnp.bfloat16),
            pltpu.VMEM((3 * LANES * rows, 2 * HC), jnp.bfloat16),
            pltpu.VMEM((HL, rows, span), jnp.float32),
            pltpu.VMEM((HL, rows, span), jnp.bfloat16),
            pltpu.SemaphoreType.DMA((3 * LANES,)),
        ],
        compiler_params=pltpu.CompilerParams(vmem_limit_bytes=56 * 1024 * 1024),
        cost_estimate=BRIEF,
    )(mask, *q, *kv)


def attend_finish(steps, mask, q, begun, kv):
    rows = begun[0].shape[1]
    span = 3 * rows
    vmem = pl.BlockSpec(memory_space=pltpu.VMEM)

    def of_tile(step, width):
        return pl.BlockSpec((1, rows, width), lambda i, step=step: (step % 2, 0, 0))

    return pl.pallas_call(
        lambda *refs: finish_kernel(steps, *refs),
        grid=(1,),
        out_shape=[jax.ShapeDtypeStruct((rows, HC), jnp.bfloat16)] * len(steps),
        in_specs=[pl.BlockSpec(memory_space=pltpu.SMEM)]
        + [pl.BlockSpec(memory_space=pl.ANY)] * len(steps)
        + [of_tile(step, HC) for step in steps]
        + [of_tile(step, HDIM) for step in steps]
        + [pl.BlockSpec(memory_space=pl.ANY)] * LANES,
        out_specs=[vmem] * len(steps),
        scratch_shapes=[
            pltpu.VMEM((len(steps), rows, HC), jnp.bfloat16),
            pltpu.VMEM((3 * LANES * rows, 2 * HC), jnp.bfloat16),
            pltpu.VMEM((HL, rows, span), jnp.float32),
            pltpu.VMEM((HL, rows, span), jnp.bfloat16),
            pltpu.SemaphoreType.DMA((LANES + len(steps),)),
        ],
        compiler_params=pltpu.CompilerParams(vmem_limit_bytes=56 * 1024 * 1024),
        cost_estimate=BRIEF,
    )(
        mask,
        *[q[step] for step in steps],
        *[begun[step // 2] for step in steps],
        *[begun[2 + step // 2] for step in steps],
        *kv,
    )


def project_kernel(order, groups, a_refs, w_refs, o_ref, by_lane, by_shard):
    step = pl.program_id(0)
    depth = by_shard.shape[1]
    shard = depth // len(order)

    @pl.when(step == 0)
    def _():
        for d in range(LANES):
            by_lane[lane_of(d)] = a_refs[d][...]
        parts = []
        for place in order:
            lane, at = place * shard // HC, place * shard % HC
            parts.append(by_lane[lane][:, at : at + shard])
        by_shard[...] = jnp.concatenate(parts, axis=1)

    mine, core = lax.axis_index("groups"), lax.axis_index("core")
    widths = [w.shape[1] for w in w_refs]
    steps = o_ref.shape[1] // (widths[0] + groups * widths[1])
    direct, strip, half = widths[0] * steps, widths[1] * steps, widths[1] * steps // 2
    places = [0, direct + mine * strip]
    for dx in range(1, groups):
        start = direct + lax.rem(mine + groups - dx, groups) * strip
        places += [start + core * half, start + (1 - core) * half]
    for w_ref, place, width in zip(w_refs, places, widths):
        out = jnp.dot(by_shard[...], w_ref[...], preferred_element_type=jnp.float32)
        at = pl.multiple_of(place + step * width, HDIM)
        o_ref[:, pl.ds(at, width)] = out.astype(jnp.bfloat16)


def project(attended, weights, order, groups):
    count, depth = attended[0].shape
    channels = weights[0].shape[0]
    steps = weights[-1].shape[1] // HDIM
    columns = weights[0].shape[1] + groups * weights[1].shape[1]
    whole = pl.BlockSpec((count, depth), lambda n: (0, 0))
    return pl.pallas_call(
        lambda *refs: project_kernel(order, groups, refs[:LANES], refs[LANES:-3], *refs[-3:]),
        out_shape=jax.ShapeDtypeStruct((count, columns), jnp.bfloat16),
        grid=(steps,),
        in_specs=[whole] * LANES
        + [pl.BlockSpec((channels, w.shape[1] // steps), lambda n: (0, n)) for w in weights],
        out_specs=pl.BlockSpec((count, columns), lambda n: (0, 0)),
        scratch_shapes=[
            pltpu.VMEM((LANES, count, depth), jnp.bfloat16),
            pltpu.VMEM((count, channels), jnp.bfloat16),
        ],
        compiler_params=pltpu.CompilerParams(vmem_limit_bytes=56 * 1024 * 1024),
    )(*attended, *weights)


def after(x, *others):
    return lax.optimization_barrier((x, *others))[0]


def on_device(queries, keys, values, frame_index, block_mask, out_weight):
    count = queries.shape[0]
    planes, groups = lax.axis_size("plane"), lax.axis_size("groups")
    seq = ("plane", "row", "core")

    def index(p, r, c):
        return (p * 2 + r) * 2 + c

    every = [(p, r, c) for p in range(planes) for r in range(2) for c in range(2)]

    def to_lane(x, dr, dc):
        return lax.ppermute(x, seq, [(index(p, r, c), index(p, r ^ dr, c ^ dc)) for p, r, c in every])

    def to_plane(x, dp):
        pairs = [(index(p, r, c), index(p + dp, r, c)) for p, r, c in every if 0 <= p + dp < planes]
        return lax.ppermute(x, seq, pairs)

    def swap(x):
        return to_lane(x[1], 0, 1)

    walk = [(p, 0) for p in range(planes)] + [(p, 1) for p in reversed(range(planes))]
    order = [index(p, r, c) for p, r in walk for c in range(2)]

    def gather(part):
        return lax.all_gather(part, seq, axis=0, tiled=True, axis_index_groups=[order])

    columns = out_weight.shape[1]
    strip = 2 * columns // 3 // (groups * 2 * HDIM) * 2 * HDIM
    direct = columns - groups * strip
    strip_at = direct + lax.axis_index("groups") * strip
    own_strip = gather(lax.dynamic_slice_in_dim(out_weight, strip_at, strip, 1))

    own, other = pack(pack_kv_kernel, frame_index, (keys, values), 2 * HC)
    across = to_lane(other, 1, 0)
    early = [to_plane(own, dp) for dp in (1, -1)]
    beside = swap(own)
    own_q, other_q = pack(pack_q_kernel, frame_index, (after(queries, beside),), HC)
    across_q = to_lane(other_q, 1, 0)
    across_beside = swap(across)
    here = [own, beside, across, across_beside]
    q = [own_q, swap(own_q), across_q, swap(across_q)]
    onward = after(across, *early)
    late = [to_plane(onward, dp) for dp in (1, -1)]
    direct_strip = gather(after(out_weight, across)[:, :direct])

    own_strip = after(own_strip, *early, across_beside)
    half = strip // 2
    core_at = lax.axis_index("core") * half
    sent = lax.dynamic_slice_in_dim(own_strip, core_at, half, 1)
    halves = [
        lax.ppermute(sent, "groups", [(g, (g + dx) % groups) for g in range(groups)])
        for dx in range(1, groups)
    ]
    pieces = [piece for x in early for piece in (x, swap(x))]
    begun = attend_begin(after(block_mask, sent), q, here + pieces)
    late = [after(x, begun[0]) for x in late]
    late = [piece for x in late for piece in (x, swap(x))]
    mixed = attend_finish((2, 3, 1), block_mask, q, begun, late)
    moved = [to_lane(x, step // 2, step % 2) for x, step in zip(mixed, (2, 3, 1))]
    halves = [after(x, mixed[0]) for x in halves]
    own = attend_finish((0,), after(block_mask, mixed[0], *halves), q, begun, late)
    mixed = [own[0], moved[2], moved[0], moved[1]]
    weights = [direct_strip, own_strip]
    for x in halves:
        weights += [x, lax.ppermute(x, "core", [(0, 1), (1, 0)])]
    return project(mixed, weights, order, groups)


def solution(mesh):
    groups, seq = mesh.devices.shape
    split = Mesh(
        mesh.devices.reshape(groups, seq // LANES, LANES // 2, 2), ("groups", "plane", "row", "core")
    )
    along = ("plane", "row", "core")
    tokens = P(("groups",) + along, None)
    return jax.shard_map(
        on_device,
        mesh=split,
        in_specs=(tokens, tokens, tokens, P(("groups",) + along), P(), P(along, None)),
        out_specs=tokens,
        check_vma=False,
    )
```

```python
import math

import jax
import jax.numpy as jnp
from jax import lax
from jax.experimental import pallas as pl
from jax.experimental.pallas import tpu as pltpu
from jax.sharding import Mesh
from jax.sharding import PartitionSpec as P

HEADS = 12
HDIM = 128
TCH = 16
BLK = 128
LANES = 4
HL = HEADS // LANES
HC = HL * HDIM
REACH = 4
NEG = -1e30
BRIEF = pl.CostEstimate(flops=1024, bytes_accessed=1024, transcendentals=0)
TO_EXP2 = math.log2(math.e) / math.sqrt(HDIM)


def turn_tables(frames, same, other):
    lane = lax.broadcasted_iota(jnp.int32, (8, HDIM), 1)
    half = TCH // 2
    channel = lax.rem(lane, half).astype(jnp.float32)
    for block in range(same.shape[0]):
        angle = frames[block].astype(jnp.float32) * jnp.exp2(-channel)
        cosine, sine = jnp.cos(angle), jnp.sin(angle)
        same[block] = jnp.where(lane < TCH, cosine, 1.0)
        other[block] = jnp.where(lane < half, -sine, jnp.where(lane < TCH, sine, 0.0))


def lane_of(step):
    mine = lax.axis_index("row") * 2 + lax.axis_index("core")
    return lax.bitwise_xor(mine, step)


def turn_into(frames, x_ref, outs, same, other):
    turn_tables(frames, same, other)
    half = TCH // 2
    lane = lax.broadcasted_iota(jnp.int32, (BLK, HDIM), 1)
    for step in range(LANES):
        for head in range(HL):
            start = pl.multiple_of(lane_of(step) * HC + head * HDIM, HDIM)
            for block in range(x_ref.shape[0] // BLK):
                rows = slice(block * BLK, (block + 1) * BLK)
                x = x_ref[rows, pl.ds(start, HDIM)].astype(jnp.float32)
                partner = jnp.where(lane < half, pltpu.roll(x, HDIM - half, 1), pltpu.roll(x, half, 1))
                turned = x * same[block, :1] + partner * other[block, :1]
                cols = slice(head * HDIM, (head + 1) * HDIM)
                outs[step // 2][step % 2, rows, cols] = turned.astype(jnp.bfloat16)


def pack_kv_kernel(frames, k_ref, v_ref, *rest):
    outs, tables = rest[:2], rest[2:]
    turn_into(frames, k_ref, outs, *tables)
    for step in range(LANES):
        start = pl.multiple_of(lane_of(step) * HC, HDIM)
        outs[step // 2][step % 2, :, HC:] = v_ref[:, pl.ds(start, HC)]


def pack_q_kernel(frames, q_ref, *rest):
    turn_into(frames, q_ref, rest[:2], *rest[2:])


def pack(kernel, frames, arrays, width):
    count = arrays[0].shape[0]
    table = pltpu.VMEM((count // BLK, 8, HDIM), jnp.float32)
    return pl.pallas_call(
        kernel,
        out_shape=[jax.ShapeDtypeStruct((2, count, width), jnp.bfloat16)] * 2,
        in_specs=[pl.BlockSpec(memory_space=pltpu.SMEM)]
        + [pl.BlockSpec(memory_space=pltpu.VMEM) for _ in arrays],
        out_specs=[pl.BlockSpec(memory_space=pltpu.VMEM)] * 2,
        scratch_shapes=[table, table],
        compiler_params=pltpu.CompilerParams(vmem_limit_bytes=56 * 1024 * 1024),
    )(frames, *arrays)


def biases_of(mask, me, devices, per_dev):
    nblk = mask.shape[0]
    biases = []
    for device in devices:
        for b in range(per_dev):
            key_block = device * per_dev + b
            inside = (key_block >= 0) & (key_block < nblk)
            column = jnp.clip(key_block, 0, nblk - 1)
            biases.append(
                [jnp.where(inside & (mask[me * per_dev + a, column] > 0), 0.0, NEG) for a in range(per_dev)]
            )
    return biases


def attend_head(h, q, kv, starts, biases, scores, weights, state):
    rows = q.shape[0]
    per_dev = rows // BLK
    kcols = slice(h * HDIM, (h + 1) * HDIM)
    vcols = slice(HC + h * HDIM, HC + (h + 1) * HDIM)
    peak = jnp.full((rows, BLK), NEG, jnp.float32)
    for i, start in enumerate(starts):
        keys = kv[pl.ds(start, rows), kcols]
        s = lax.dot_general(q, keys, (((1,), (1,)), ((), ())), preferred_element_type=jnp.float32)
        for b in range(per_dev):
            j = i * per_dev + b
            parts = [
                s[a * BLK : (a + 1) * BLK, b * BLK : (b + 1) * BLK] + biases[j][a] for a in range(per_dev)
            ]
            part = jnp.concatenate(parts, axis=0)
            peak = jnp.maximum(peak, part)
            scores[h, :, j * BLK : (j + 1) * BLK] = part
    top = jnp.max(peak, axis=1, keepdims=True)
    if state is not None:
        top = jnp.maximum(top, state[0])
    total = jnp.zeros((rows, BLK), jnp.float32)
    for j in range(len(starts) * per_dev):
        cols = slice(j * BLK, (j + 1) * BLK)
        e = jnp.exp2((scores[h, :, cols] - top) * TO_EXP2)
        total += e
        weights[h, :, cols] = e.astype(jnp.bfloat16)
    mixed = None
    for i, start in enumerate(starts):
        part = jnp.dot(
            weights[h, :, i * rows : (i + 1) * rows],
            kv[pl.ds(start, rows), vcols],
            preferred_element_type=jnp.float32,
        )
        mixed = part if mixed is None else mixed + part
    total = jnp.sum(total, axis=1, keepdims=True)
    if state is not None:
        shrink = jnp.exp2((state[0] - top) * TO_EXP2)
        total += state[1] * shrink
        mixed += state[2] * shrink
    return top, total, mixed


def fetch(pairs, sems):
    copies = []
    for i, (source, target) in enumerate(pairs):
        source = source.at[0] if len(source.shape) == 3 else source
        copies.append(pltpu.make_async_copy(source, target, sems.at[i]))
    for copy in copies:
        copy.start()
    for copy in copies:
        copy.wait()


def begin_kernel(mask, *refs):
    q_refs, kv_refs, rest = refs[:LANES], refs[LANES : 3 * LANES], refs[3 * LANES :]
    accs, stats, (q_all, kv, scores, weights, sems) = rest[:2], rest[2:4], rest[4:]
    rows = q_all.shape[1]
    per_dev = rows // BLK
    plane = lax.axis_index("plane")
    pairs = [(q_refs[step], q_all.at[step]) for step in range(LANES)]
    places = [LANES + lane_of(step) for step in range(LANES)]
    places += [part * LANES + lane_of(step) for part in (0, 2) for step in range(2)]
    for ref, place in zip(kv_refs, places):
        pairs.append((ref, kv.at[pl.ds(pl.multiple_of(place * rows, BLK), rows)]))
    fetch(pairs, sems)
    for group in range(2):

        def one_tile(core, carry):
            step = 2 * group + core
            tile = lane_of(step)
            me = plane * LANES + tile
            devices = [plane * LANES + lane for lane in range(LANES)]
            devices += chunk_devices_at(group, tile, False)
            starts = [pl.multiple_of((d - (plane - 1) * LANES) * rows, BLK) for d in devices]
            biases = biases_of(mask, me, devices, per_dev)
            for h in range(HL):
                cols = slice(h * HDIM, (h + 1) * HDIM)
                q = q_all[step, :, cols]
                top, total, mixed = attend_head(h, q, kv, starts, biases, scores, weights, None)
                accs[group][core, :, cols] = mixed
                stats[group][core, :, h : h + 1] = top
                stats[group][core, :, HL + h : HL + h + 1] = total
            return carry

        lax.fori_loop(0, 2, one_tile, 0)


def chunk_devices_at(group, tile, late):
    plane = lax.axis_index("plane")
    me = plane * LANES + tile
    row, core = lax.div(tile, 2), lax.rem(tile, 2)
    if late == (group == 1):
        return [me - REACH, me + REACH, jnp.where(core == 0, me - REACH + 1, me + REACH - 1)]
    first = jnp.where(row == 0, (plane - 1) * LANES + 2, (plane + 1) * LANES)
    return [first, first + 1]


def finish_kernel(steps, mask, *refs):
    count = len(steps)
    q_refs, accs, stats = refs[:count], refs[count : 2 * count], refs[2 * count : 3 * count]
    kv_refs, o_refs = refs[3 * count : 3 * count + LANES], refs[3 * count + LANES : 4 * count + LANES]
    q_all, kv, scores, weights, sems = refs[4 * count + LANES :]
    rows = q_all.shape[1]
    per_dev = rows // BLK
    plane = lax.axis_index("plane")
    places = [part * LANES + lane_of(step) for part in (0, 2) for step in (2, 3)]
    pairs = [
        (ref, kv.at[pl.ds(pl.multiple_of(place * rows, BLK), rows)]) for ref, place in zip(kv_refs, places)
    ]
    pairs += [(ref, q_all.at[i]) for i, ref in enumerate(q_refs)]
    fetch(pairs, sems)
    for i, (step, acc, stat, o_ref) in enumerate(zip(steps, accs, stats, o_refs)):
        tile = lane_of(step)
        me = plane * LANES + tile
        devices = chunk_devices_at(step // 2, tile, True)
        starts = [pl.multiple_of((d - (plane - 1) * LANES) * rows, BLK) for d in devices]
        biases = biases_of(mask, me, devices, per_dev)
        for h in range(HL):
            cols = slice(h * HDIM, (h + 1) * HDIM)
            state = (stat[0, :, h : h + 1], stat[0, :, HL + h : HL + h + 1], acc[0, :, cols])
            _, total, mixed = attend_head(h, q_all[i, :, cols], kv, starts, biases, scores, weights, state)
            o_ref[:, cols] = (mixed / total).astype(jnp.bfloat16)


def attend_begin(mask, q, kv):
    rows = kv[1].shape[0]
    span = 7 * rows
    vmem = pl.BlockSpec(memory_space=pltpu.VMEM)
    return pl.pallas_call(
        begin_kernel,
        out_shape=[jax.ShapeDtypeStruct((2, rows, HC), jnp.float32)] * 2
        + [jax.ShapeDtypeStruct((2, rows, HDIM), jnp.float32)] * 2,
        in_specs=[pl.BlockSpec(memory_space=pltpu.SMEM)] + [pl.BlockSpec(memory_space=pl.ANY)] * (3 * LANES),
        out_specs=[vmem] * 4,
        scratch_shapes=[
            pltpu.VMEM((LANES, rows, HC), jnp.bfloat16),
            pltpu.VMEM((3 * LANES * rows, 2 * HC), jnp.bfloat16),
            pltpu.VMEM((HL, rows, span), jnp.float32),
            pltpu.VMEM((HL, rows, span), jnp.bfloat16),
            pltpu.SemaphoreType.DMA((3 * LANES,)),
        ],
        compiler_params=pltpu.CompilerParams(vmem_limit_bytes=56 * 1024 * 1024),
        cost_estimate=BRIEF,
    )(mask, *q, *kv)


def attend_finish(steps, mask, q, begun, kv):
    rows = begun[0].shape[1]
    span = 3 * rows
    vmem = pl.BlockSpec(memory_space=pltpu.VMEM)

    def of_tile(step, width):
        return pl.BlockSpec((1, rows, width), lambda i, step=step: (step % 2, 0, 0))

    return pl.pallas_call(
        lambda *refs: finish_kernel(steps, *refs),
        grid=(1,),
        out_shape=[jax.ShapeDtypeStruct((rows, HC), jnp.bfloat16)] * len(steps),
        in_specs=[pl.BlockSpec(memory_space=pltpu.SMEM)]
        + [pl.BlockSpec(memory_space=pl.ANY)] * len(steps)
        + [of_tile(step, HC) for step in steps]
        + [of_tile(step, HDIM) for step in steps]
        + [pl.BlockSpec(memory_space=pl.ANY)] * LANES,
        out_specs=[vmem] * len(steps),
        scratch_shapes=[
            pltpu.VMEM((len(steps), rows, HC), jnp.bfloat16),
            pltpu.VMEM((3 * LANES * rows, 2 * HC), jnp.bfloat16),
            pltpu.VMEM((HL, rows, span), jnp.float32),
            pltpu.VMEM((HL, rows, span), jnp.bfloat16),
            pltpu.SemaphoreType.DMA((LANES + len(steps),)),
        ],
        compiler_params=pltpu.CompilerParams(vmem_limit_bytes=56 * 1024 * 1024),
        cost_estimate=BRIEF,
    )(
        mask,
        *[q[step] for step in steps],
        *[begun[step // 2] for step in steps],
        *[begun[2 + step // 2] for step in steps],
        *kv,
    )


def project_kernel(order, groups, a_refs, w_refs, o_ref, by_lane, by_shard):
    step = pl.program_id(0)
    depth = by_shard.shape[1]
    shard = depth // len(order)

    @pl.when(step == 0)
    def _():
        for d in range(LANES):
            by_lane[lane_of(d)] = a_refs[d][...]
        parts = []
        for place in order:
            lane, at = place * shard // HC, place * shard % HC
            parts.append(by_lane[lane][:, at : at + shard])
        by_shard[...] = jnp.concatenate(parts, axis=1)

    mine, core = lax.axis_index("groups"), lax.axis_index("core")
    widths = [w.shape[1] for w in w_refs]
    steps = o_ref.shape[1] // (widths[0] + groups * widths[1])
    direct, strip, half = widths[0] * steps, widths[1] * steps, widths[1] * steps // 2
    places = [0, direct + mine * strip]
    for dx in range(1, groups):
        start = direct + lax.rem(mine + groups - dx, groups) * strip
        places += [start + core * half, start + (1 - core) * half]
    for w_ref, place, width in zip(w_refs, places, widths):
        out = jnp.dot(by_shard[...], w_ref[...], preferred_element_type=jnp.float32)
        at = pl.multiple_of(place + step * width, HDIM)
        o_ref[:, pl.ds(at, width)] = out.astype(jnp.bfloat16)


def project(attended, weights, order, groups):
    count, depth = attended[0].shape
    channels = weights[0].shape[0]
    steps = weights[-1].shape[1] // HDIM
    columns = weights[0].shape[1] + groups * weights[1].shape[1]
    whole = pl.BlockSpec((count, depth), lambda n: (0, 0))
    return pl.pallas_call(
        lambda *refs: project_kernel(order, groups, refs[:LANES], refs[LANES:-3], *refs[-3:]),
        out_shape=jax.ShapeDtypeStruct((count, columns), jnp.bfloat16),
        grid=(steps,),
        in_specs=[whole] * LANES
        + [pl.BlockSpec((channels, w.shape[1] // steps), lambda n: (0, n)) for w in weights],
        out_specs=pl.BlockSpec((count, columns), lambda n: (0, 0)),
        scratch_shapes=[
            pltpu.VMEM((LANES, count, depth), jnp.bfloat16),
            pltpu.VMEM((count, channels), jnp.bfloat16),
        ],
        compiler_params=pltpu.CompilerParams(vmem_limit_bytes=56 * 1024 * 1024),
    )(*attended, *weights)


def after(x, *others):
    return lax.optimization_barrier((x, *others))[0]


def on_device(queries, keys, values, frame_index, block_mask, out_weight):
    count = queries.shape[0]
    planes, groups = lax.axis_size("plane"), lax.axis_size("groups")
    seq = ("plane", "row", "core")

    def index(p, r, c):
        return (p * 2 + r) * 2 + c

    every = [(p, r, c) for p in range(planes) for r in range(2) for c in range(2)]

    def to_lane(x, dr, dc):
        return lax.ppermute(x, seq, [(index(p, r, c), index(p, r ^ dr, c ^ dc)) for p, r, c in every])

    def to_plane(x, dp):
        pairs = [(index(p, r, c), index(p + dp, r, c)) for p, r, c in every if 0 <= p + dp < planes]
        return lax.ppermute(x, seq, pairs)

    def swap(x):
        return to_lane(x[1], 0, 1)

    walk = [(p, 0) for p in range(planes)] + [(p, 1) for p in reversed(range(planes))]
    order = [index(p, r, c) for p, r in walk for c in range(2)]

    def gather(part):
        return lax.all_gather(part, seq, axis=0, tiled=True, axis_index_groups=[order])

    columns = out_weight.shape[1]
    strip = 2 * columns // 3 // (groups * 2 * HDIM) * 2 * HDIM
    direct = columns - groups * strip
    strip_at = direct + lax.axis_index("groups") * strip
    own_strip = gather(lax.dynamic_slice_in_dim(out_weight, strip_at, strip, 1))

    own, other = pack(pack_kv_kernel, frame_index, (keys, values), 2 * HC)
    across = to_lane(other, 1, 0)
    early = [to_plane(own, dp) for dp in (1, -1)]
    beside = swap(own)
    own_q, other_q = pack(pack_q_kernel, frame_index, (after(queries, beside),), HC)
    across_q = to_lane(other_q, 1, 0)
    across_beside = swap(across)
    here = [own, beside, across, across_beside]
    q = [own_q, swap(own_q), across_q, swap(across_q)]
    onward = after(across, *early)
    late = [to_plane(onward, dp) for dp in (1, -1)]
    direct_strip = gather(after(out_weight, *early)[:, :direct])

    own_strip = after(own_strip, *early, across_beside)
    half = strip // 2
    core_at = lax.axis_index("core") * half
    sent = lax.dynamic_slice_in_dim(own_strip, core_at, half, 1)
    halves = [
        lax.ppermute(sent, "groups", [(g, (g + dx) % groups) for g in range(groups)])
        for dx in range(1, groups)
    ]
    pieces = [piece for x in early for piece in (x, swap(x))]
    begun = attend_begin(after(block_mask, sent), q, here + pieces)
    late = [after(x, begun[0]) for x in late]
    late = [piece for x in late for piece in (x, swap(x))]
    mixed = attend_finish((2, 3, 1), block_mask, q, begun, late)
    moved = [to_lane(x, step // 2, step % 2) for x, step in zip(mixed, (2, 3, 1))]
    halves = [after(x, mixed[0]) for x in halves]
    own = attend_finish((0,), after(block_mask, mixed[0], *halves), q, begun, late)
    mixed = [own[0], moved[2], moved[0], moved[1]]
    weights = [direct_strip, own_strip]
    for x in halves:
        weights += [x, lax.ppermute(x, "core", [(0, 1), (1, 0)])]
    return project(mixed, weights, order, groups)


def solution(mesh):
    groups, seq = mesh.devices.shape
    split = Mesh(
        mesh.devices.reshape(groups, seq // LANES, LANES // 2, 2), ("groups", "plane", "row", "core")
    )
    along = ("plane", "row", "core")
    tokens = P(("groups",) + along, None)
    return jax.shard_map(
        on_device,
        mesh=split,
        in_specs=(tokens, tokens, tokens, P(("groups",) + along), P(), P(along, None)),
        out_specs=tokens,
        check_vma=False,
    )
```

```python
import math

import jax
import jax.numpy as jnp
from jax import lax
from jax.experimental import pallas as pl
from jax.experimental.pallas import tpu as pltpu
from jax.sharding import Mesh
from jax.sharding import PartitionSpec as P

HEADS = 12
HDIM = 128
TCH = 16
BLK = 128
LANES = 4
HL = HEADS // LANES
HC = HL * HDIM
REACH = 4
NEG = -1e30
BRIEF = pl.CostEstimate(flops=1024, bytes_accessed=1024, transcendentals=0)
TO_EXP2 = math.log2(math.e) / math.sqrt(HDIM)


def turn_tables(frames, same, other):
    lane = lax.broadcasted_iota(jnp.int32, (8, HDIM), 1)
    half = TCH // 2
    channel = lax.rem(lane, half).astype(jnp.float32)
    for block in range(same.shape[0]):
        angle = frames[block].astype(jnp.float32) * jnp.exp2(-channel)
        cosine, sine = jnp.cos(angle), jnp.sin(angle)
        same[block] = jnp.where(lane < TCH, cosine, 1.0)
        other[block] = jnp.where(lane < half, -sine, jnp.where(lane < TCH, sine, 0.0))


def cut(own, strip_at, strip, direct):
    def kernel(at, own_ref, strip_ref, direct_ref):
        strip_ref[...] = own_ref[:, pl.ds(pl.multiple_of(at[0], HDIM), strip)]
        direct_ref[...] = own_ref[:, :direct]

    rows = own.shape[0]
    vmem = pl.BlockSpec(memory_space=pltpu.VMEM)
    return pl.pallas_call(
        kernel,
        out_shape=[jax.ShapeDtypeStruct((rows, width), jnp.bfloat16) for width in (strip, direct)],
        in_specs=[pl.BlockSpec(memory_space=pltpu.SMEM), vmem],
        out_specs=[vmem] * 2,
    )(jnp.full((1,), strip_at, jnp.int32), own)


def lane_of(step):
    mine = lax.axis_index("row") * 2 + lax.axis_index("core")
    return lax.bitwise_xor(mine, step)


def turn_into(frames, x_ref, outs, same, other):
    turn_tables(frames, same, other)
    half = TCH // 2
    lane = lax.broadcasted_iota(jnp.int32, (BLK, HDIM), 1)
    for step in range(LANES):
        for head in range(HL):
            start = pl.multiple_of(lane_of(step) * HC + head * HDIM, HDIM)
            for block in range(x_ref.shape[0] // BLK):
                rows = slice(block * BLK, (block + 1) * BLK)
                x = x_ref[rows, pl.ds(start, HDIM)].astype(jnp.float32)
                partner = jnp.where(lane < half, pltpu.roll(x, HDIM - half, 1), pltpu.roll(x, half, 1))
                turned = x * same[block, :1] + partner * other[block, :1]
                cols = slice(head * HDIM, (head + 1) * HDIM)
                outs[step // 2][step % 2, rows, cols] = turned.astype(jnp.bfloat16)


def pack_kv_kernel(frames, k_ref, v_ref, *rest):
    outs, tables = rest[:2], rest[2:]
    turn_into(frames, k_ref, outs, *tables)
    for step in range(LANES):
        start = pl.multiple_of(lane_of(step) * HC, HDIM)
        outs[step // 2][step % 2, :, HC:] = v_ref[:, pl.ds(start, HC)]


def pack_q_kernel(frames, q_ref, *rest):
    turn_into(frames, q_ref, rest[:2], *rest[2:])


def pack(kernel, frames, arrays, width):
    count = arrays[0].shape[0]
    table = pltpu.VMEM((count // BLK, 8, HDIM), jnp.float32)
    return pl.pallas_call(
        kernel,
        out_shape=[jax.ShapeDtypeStruct((2, count, width), jnp.bfloat16)] * 2,
        in_specs=[pl.BlockSpec(memory_space=pltpu.SMEM)]
        + [pl.BlockSpec(memory_space=pltpu.VMEM) for _ in arrays],
        out_specs=[pl.BlockSpec(memory_space=pltpu.VMEM)] * 2,
        scratch_shapes=[table, table],
        compiler_params=pltpu.CompilerParams(vmem_limit_bytes=56 * 1024 * 1024),
    )(frames, *arrays)


def biases_of(mask, me, devices, per_dev):
    nblk = mask.shape[0]
    biases = []
    for device in devices:
        for b in range(per_dev):
            key_block = device * per_dev + b
            inside = (key_block >= 0) & (key_block < nblk)
            column = jnp.clip(key_block, 0, nblk - 1)
            biases.append(
                [jnp.where(inside & (mask[me * per_dev + a, column] > 0), 0.0, NEG) for a in range(per_dev)]
            )
    return biases


def attend_head(h, q, kv, starts, biases, scores, weights, state):
    rows = q.shape[0]
    per_dev = rows // BLK
    kcols = slice(h * HDIM, (h + 1) * HDIM)
    vcols = slice(HC + h * HDIM, HC + (h + 1) * HDIM)
    peak = jnp.full((rows, BLK), NEG, jnp.float32)
    for i, start in enumerate(starts):
        keys = kv[pl.ds(start, rows), kcols]
        s = lax.dot_general(q, keys, (((1,), (1,)), ((), ())), preferred_element_type=jnp.float32)
        for b in range(per_dev):
            j = i * per_dev + b
            parts = [
                s[a * BLK : (a + 1) * BLK, b * BLK : (b + 1) * BLK] + biases[j][a] for a in range(per_dev)
            ]
            part = jnp.concatenate(parts, axis=0)
            peak = jnp.maximum(peak, part)
            scores[h, :, j * BLK : (j + 1) * BLK] = part
    top = jnp.max(peak, axis=1, keepdims=True)
    if state is not None:
        top = jnp.maximum(top, state[0])
    total = jnp.zeros((rows, BLK), jnp.float32)
    for j in range(len(starts) * per_dev):
        cols = slice(j * BLK, (j + 1) * BLK)
        e = jnp.exp2((scores[h, :, cols] - top) * TO_EXP2)
        total += e
        weights[h, :, cols] = e.astype(jnp.bfloat16)
    mixed = None
    for i, start in enumerate(starts):
        part = jnp.dot(
            weights[h, :, i * rows : (i + 1) * rows],
            kv[pl.ds(start, rows), vcols],
            preferred_element_type=jnp.float32,
        )
        mixed = part if mixed is None else mixed + part
    total = jnp.sum(total, axis=1, keepdims=True)
    if state is not None:
        shrink = jnp.exp2((state[0] - top) * TO_EXP2)
        total += state[1] * shrink
        mixed += state[2] * shrink
    return top, total, mixed


def fetch(pairs, sems):
    copies = []
    for i, (source, target) in enumerate(pairs):
        source = source.at[0] if len(source.shape) == 3 else source
        copies.append(pltpu.make_async_copy(source, target, sems.at[i]))
    for copy in copies:
        copy.start()
    for copy in copies:
        copy.wait()


def begin_kernel(mask, *refs):
    q_refs, kv_refs, rest = refs[:LANES], refs[LANES : 3 * LANES], refs[3 * LANES :]
    accs, stats, (q_all, kv, scores, weights, sems) = rest[:2], rest[2:4], rest[4:]
    rows = q_all.shape[1]
    per_dev = rows // BLK
    plane = lax.axis_index("plane")
    pairs = [(q_refs[step], q_all.at[step]) for step in range(LANES)]
    places = [LANES + lane_of(step) for step in range(LANES)]
    places += [part * LANES + lane_of(step) for part in (0, 2) for step in range(2)]
    for ref, place in zip(kv_refs, places):
        pairs.append((ref, kv.at[pl.ds(pl.multiple_of(place * rows, BLK), rows)]))
    fetch(pairs, sems)
    for group in range(2):

        def one_tile(core, carry):
            step = 2 * group + core
            tile = lane_of(step)
            me = plane * LANES + tile
            devices = [plane * LANES + lane for lane in range(LANES)]
            devices += chunk_devices_at(group, tile, False)
            starts = [pl.multiple_of((d - (plane - 1) * LANES) * rows, BLK) for d in devices]
            biases = biases_of(mask, me, devices, per_dev)
            for h in range(HL):
                cols = slice(h * HDIM, (h + 1) * HDIM)
                q = q_all[step, :, cols]
                top, total, mixed = attend_head(h, q, kv, starts, biases, scores, weights, None)
                accs[group][core, :, cols] = mixed
                stats[group][core, :, h : h + 1] = top
                stats[group][core, :, HL + h : HL + h + 1] = total
            return carry

        lax.fori_loop(0, 2, one_tile, 0)


def chunk_devices_at(group, tile, late):
    plane = lax.axis_index("plane")
    me = plane * LANES + tile
    row, core = lax.div(tile, 2), lax.rem(tile, 2)
    if late == (group == 1):
        return [me - REACH, me + REACH, jnp.where(core == 0, me - REACH + 1, me + REACH - 1)]
    first = jnp.where(row == 0, (plane - 1) * LANES + 2, (plane + 1) * LANES)
    return [first, first + 1]


def finish_kernel(steps, mask, *refs):
    count = len(steps)
    q_refs, accs, stats = refs[:count], refs[count : 2 * count], refs[2 * count : 3 * count]
    kv_refs, o_refs = refs[3 * count : 3 * count + LANES], refs[3 * count + LANES : 4 * count + LANES]
    q_all, kv, scores, weights, sems = refs[4 * count + LANES :]
    rows = q_all.shape[1]
    per_dev = rows // BLK
    plane = lax.axis_index("plane")
    places = [part * LANES + lane_of(step) for part in (0, 2) for step in (2, 3)]
    pairs = [
        (ref, kv.at[pl.ds(pl.multiple_of(place * rows, BLK), rows)]) for ref, place in zip(kv_refs, places)
    ]
    pairs += [(ref, q_all.at[i]) for i, ref in enumerate(q_refs)]
    fetch(pairs, sems)
    for i, (step, acc, stat, o_ref) in enumerate(zip(steps, accs, stats, o_refs)):
        tile = lane_of(step)
        me = plane * LANES + tile
        devices = chunk_devices_at(step // 2, tile, True)
        starts = [pl.multiple_of((d - (plane - 1) * LANES) * rows, BLK) for d in devices]
        biases = biases_of(mask, me, devices, per_dev)
        for h in range(HL):
            cols = slice(h * HDIM, (h + 1) * HDIM)
            state = (stat[0, :, h : h + 1], stat[0, :, HL + h : HL + h + 1], acc[0, :, cols])
            _, total, mixed = attend_head(h, q_all[i, :, cols], kv, starts, biases, scores, weights, state)
            o_ref[:, cols] = (mixed / total).astype(jnp.bfloat16)


def attend_begin(mask, q, kv):
    rows = kv[1].shape[0]
    span = 7 * rows
    vmem = pl.BlockSpec(memory_space=pltpu.VMEM)
    return pl.pallas_call(
        begin_kernel,
        out_shape=[jax.ShapeDtypeStruct((2, rows, HC), jnp.float32)] * 2
        + [jax.ShapeDtypeStruct((2, rows, HDIM), jnp.float32)] * 2,
        in_specs=[pl.BlockSpec(memory_space=pltpu.SMEM)] + [pl.BlockSpec(memory_space=pl.ANY)] * (3 * LANES),
        out_specs=[vmem] * 4,
        scratch_shapes=[
            pltpu.VMEM((LANES, rows, HC), jnp.bfloat16),
            pltpu.VMEM((3 * LANES * rows, 2 * HC), jnp.bfloat16),
            pltpu.VMEM((HL, rows, span), jnp.float32),
            pltpu.VMEM((HL, rows, span), jnp.bfloat16),
            pltpu.SemaphoreType.DMA((3 * LANES,)),
        ],
        compiler_params=pltpu.CompilerParams(vmem_limit_bytes=56 * 1024 * 1024),
        cost_estimate=BRIEF,
    )(mask, *q, *kv)


def attend_finish(steps, mask, q, begun, kv):
    rows = begun[0].shape[1]
    span = 3 * rows
    vmem = pl.BlockSpec(memory_space=pltpu.VMEM)

    def of_tile(step, width):
        return pl.BlockSpec((1, rows, width), lambda i, step=step: (step % 2, 0, 0))

    return pl.pallas_call(
        lambda *refs: finish_kernel(steps, *refs),
        grid=(1,),
        out_shape=[jax.ShapeDtypeStruct((rows, HC), jnp.bfloat16)] * len(steps),
        in_specs=[pl.BlockSpec(memory_space=pltpu.SMEM)]
        + [pl.BlockSpec(memory_space=pl.ANY)] * len(steps)
        + [of_tile(step, HC) for step in steps]
        + [of_tile(step, HDIM) for step in steps]
        + [pl.BlockSpec(memory_space=pl.ANY)] * LANES,
        out_specs=[vmem] * len(steps),
        scratch_shapes=[
            pltpu.VMEM((len(steps), rows, HC), jnp.bfloat16),
            pltpu.VMEM((3 * LANES * rows, 2 * HC), jnp.bfloat16),
            pltpu.VMEM((HL, rows, span), jnp.float32),
            pltpu.VMEM((HL, rows, span), jnp.bfloat16),
            pltpu.SemaphoreType.DMA((LANES + len(steps),)),
        ],
        compiler_params=pltpu.CompilerParams(vmem_limit_bytes=56 * 1024 * 1024),
        cost_estimate=BRIEF,
    )(
        mask,
        *[q[step] for step in steps],
        *[begun[step // 2] for step in steps],
        *[begun[2 + step // 2] for step in steps],
        *kv,
    )


def project_kernel(order, groups, a_refs, w_refs, o_ref, by_lane, by_shard):
    step = pl.program_id(0)
    depth = by_shard.shape[1]
    shard = depth // len(order)

    @pl.when(step == 0)
    def _():
        for d in range(LANES):
            by_lane[lane_of(d)] = a_refs[d][...]
        parts = []
        for place in order:
            lane, at = place * shard // HC, place * shard % HC
            parts.append(by_lane[lane][:, at : at + shard])
        by_shard[...] = jnp.concatenate(parts, axis=1)

    mine, core = lax.axis_index("groups"), lax.axis_index("core")
    widths = [w.shape[1] for w in w_refs]
    steps = o_ref.shape[1] // (widths[0] + groups * widths[1])
    direct, strip, half = widths[0] * steps, widths[1] * steps, widths[1] * steps // 2
    places = [0, direct + mine * strip]
    for dx in range(1, groups):
        start = direct + lax.rem(mine + groups - dx, groups) * strip
        places += [start + core * half, start + (1 - core) * half]
    for w_ref, place, width in zip(w_refs, places, widths):
        out = jnp.dot(by_shard[...], w_ref[...], preferred_element_type=jnp.float32)
        at = pl.multiple_of(place + step * width, HDIM)
        o_ref[:, pl.ds(at, width)] = out.astype(jnp.bfloat16)


def project(attended, weights, order, groups):
    count, depth = attended[0].shape
    channels = weights[0].shape[0]
    steps = weights[-1].shape[1] // HDIM
    columns = weights[0].shape[1] + groups * weights[1].shape[1]
    whole = pl.BlockSpec((count, depth), lambda n: (0, 0))
    return pl.pallas_call(
        lambda *refs: project_kernel(order, groups, refs[:LANES], refs[LANES:-3], *refs[-3:]),
        out_shape=jax.ShapeDtypeStruct((count, columns), jnp.bfloat16),
        grid=(steps,),
        in_specs=[whole] * LANES
        + [pl.BlockSpec((channels, w.shape[1] // steps), lambda n: (0, n)) for w in weights],
        out_specs=pl.BlockSpec((count, columns), lambda n: (0, 0)),
        scratch_shapes=[
            pltpu.VMEM((LANES, count, depth), jnp.bfloat16),
            pltpu.VMEM((count, channels), jnp.bfloat16),
        ],
        compiler_params=pltpu.CompilerParams(vmem_limit_bytes=56 * 1024 * 1024),
    )(*attended, *weights)


def after(x, *others):
    return lax.optimization_barrier((x, *others))[0]


def on_device(queries, keys, values, frame_index, block_mask, out_weight):
    count = queries.shape[0]
    planes, groups = lax.axis_size("plane"), lax.axis_size("groups")
    seq = ("plane", "row", "core")

    def index(p, r, c):
        return (p * 2 + r) * 2 + c

    every = [(p, r, c) for p in range(planes) for r in range(2) for c in range(2)]

    def to_lane(x, dr, dc):
        return lax.ppermute(x, seq, [(index(p, r, c), index(p, r ^ dr, c ^ dc)) for p, r, c in every])

    def to_plane(x, dp):
        pairs = [(index(p, r, c), index(p + dp, r, c)) for p, r, c in every if 0 <= p + dp < planes]
        return lax.ppermute(x, seq, pairs)

    def swap(x):
        return to_lane(x[1], 0, 1)

    walk = [(p, 0) for p in range(planes)] + [(p, 1) for p in reversed(range(planes))]
    order = [index(p, r, c) for p, r in walk for c in range(2)]

    def gather(part):
        return lax.all_gather(part, seq, axis=0, tiled=True, axis_index_groups=[order])

    columns = out_weight.shape[1]
    strip = 2 * columns // 3 // (groups * 2 * HDIM) * 2 * HDIM
    direct = columns - groups * strip
    strip_at = direct + lax.axis_index("groups") * strip
    own_strip, direct_strip = [gather(x) for x in cut(out_weight, strip_at, strip, direct)]

    own, other = pack(pack_kv_kernel, frame_index, (keys, values), 2 * HC)
    across = to_lane(other, 1, 0)
    early = [to_plane(own, dp) for dp in (1, -1)]
    beside = swap(own)
    own_q, other_q = pack(pack_q_kernel, frame_index, (after(queries, beside),), HC)
    across_q = to_lane(other_q, 1, 0)
    across_beside = swap(across)
    here = [own, beside, across, across_beside]
    q = [own_q, swap(own_q), across_q, swap(across_q)]
    onward = after(across, *early)
    late = [to_plane(onward, dp) for dp in (1, -1)]

    own_strip = after(own_strip, *early, across_beside)
    half = strip // 2
    core_at = lax.axis_index("core") * half
    sent = lax.dynamic_slice_in_dim(own_strip, core_at, half, 1)
    halves = [
        lax.ppermute(sent, "groups", [(g, (g + dx) % groups) for g in range(groups)])
        for dx in range(1, groups)
    ]
    pieces = [piece for x in early for piece in (x, swap(x))]
    begun = attend_begin(after(block_mask, sent), q, here + pieces)
    late = [after(x, begun[0]) for x in late]
    late = [piece for x in late for piece in (x, swap(x))]
    mixed = attend_finish((2, 3, 1), block_mask, q, begun, late)
    moved = [to_lane(x, step // 2, step % 2) for x, step in zip(mixed, (2, 3, 1))]
    halves = [after(x, mixed[0]) for x in halves]
    own = attend_finish((0,), after(block_mask, mixed[0], *halves), q, begun, late)
    mixed = [own[0], moved[2], moved[0], moved[1]]
    weights = [direct_strip, own_strip]
    for x in halves:
        weights += [x, lax.ppermute(x, "core", [(0, 1), (1, 0)])]
    return project(mixed, weights, order, groups)


def solution(mesh):
    groups, seq = mesh.devices.shape
    split = Mesh(
        mesh.devices.reshape(groups, seq // LANES, LANES // 2, 2), ("groups", "plane", "row", "core")
    )
    along = ("plane", "row", "core")
    tokens = P(("groups",) + along, None)
    return jax.shard_map(
        on_device,
        mesh=split,
        in_specs=(tokens, tokens, tokens, P(("groups",) + along), P(), P(along, None)),
        out_specs=tokens,
        check_vma=False,
    )
```

```python
import math

import jax
import jax.numpy as jnp
from jax import lax
from jax.experimental import pallas as pl
from jax.experimental.pallas import tpu as pltpu
from jax.sharding import Mesh
from jax.sharding import PartitionSpec as P

HEADS = 12
HDIM = 128
TCH = 16
BLK = 128
LANES = 4
HL = HEADS // LANES
HC = HL * HDIM
REACH = 4
NEG = -1e30
BRIEF = pl.CostEstimate(flops=1024, bytes_accessed=1024, transcendentals=0)
TO_EXP2 = math.log2(math.e) / math.sqrt(HDIM)


def turn_tables(frames, same, other):
    lane = lax.broadcasted_iota(jnp.int32, (8, HDIM), 1)
    half = TCH // 2
    channel = lax.rem(lane, half).astype(jnp.float32)
    for block in range(same.shape[0]):
        angle = frames[block].astype(jnp.float32) * jnp.exp2(-channel)
        cosine, sine = jnp.cos(angle), jnp.sin(angle)
        same[block] = jnp.where(lane < TCH, cosine, 1.0)
        other[block] = jnp.where(lane < half, -sine, jnp.where(lane < TCH, sine, 0.0))


def cut(own, start, widths):
    def kernel(at, own_ref, *refs):
        begin = 0
        for ref, width in zip(refs, widths):
            ref[...] = own_ref[:, pl.ds(pl.multiple_of(at[0] + begin, HDIM), width)]
            begin += width

    rows = own.shape[0]
    vmem = pl.BlockSpec(memory_space=pltpu.VMEM)
    return pl.pallas_call(
        kernel,
        out_shape=[jax.ShapeDtypeStruct((rows, width), jnp.bfloat16) for width in widths],
        in_specs=[pl.BlockSpec(memory_space=pltpu.SMEM), vmem],
        out_specs=[vmem] * len(widths),
    )(jnp.full((1,), start, jnp.int32), own)


def lane_of(step):
    mine = lax.axis_index("row") * 2 + lax.axis_index("core")
    return lax.bitwise_xor(mine, step)


def turn_into(frames, x_ref, outs, same, other):
    turn_tables(frames, same, other)
    half = TCH // 2
    lane = lax.broadcasted_iota(jnp.int32, (BLK, HDIM), 1)
    for step in range(LANES):
        for head in range(HL):
            start = pl.multiple_of(lane_of(step) * HC + head * HDIM, HDIM)
            for block in range(x_ref.shape[0] // BLK):
                rows = slice(block * BLK, (block + 1) * BLK)
                x = x_ref[rows, pl.ds(start, HDIM)].astype(jnp.float32)
                partner = jnp.where(lane < half, pltpu.roll(x, HDIM - half, 1), pltpu.roll(x, half, 1))
                turned = x * same[block, :1] + partner * other[block, :1]
                cols = slice(head * HDIM, (head + 1) * HDIM)
                outs[step // 2][step % 2, rows, cols] = turned.astype(jnp.bfloat16)


def pack_kv_kernel(frames, k_ref, v_ref, *rest):
    outs, tables = rest[:2], rest[2:]
    turn_into(frames, k_ref, outs, *tables)
    for step in range(LANES):
        start = pl.multiple_of(lane_of(step) * HC, HDIM)
        outs[step // 2][step % 2, :, HC:] = v_ref[:, pl.ds(start, HC)]


def pack_q_kernel(frames, q_ref, *rest):
    turn_into(frames, q_ref, rest[:2], *rest[2:])


def pack(kernel, frames, arrays, width):
    count = arrays[0].shape[0]
    table = pltpu.VMEM((count // BLK, 8, HDIM), jnp.float32)
    return pl.pallas_call(
        kernel,
        out_shape=[jax.ShapeDtypeStruct((2, count, width), jnp.bfloat16)] * 2,
        in_specs=[pl.BlockSpec(memory_space=pltpu.SMEM)]
        + [pl.BlockSpec(memory_space=pltpu.VMEM) for _ in arrays],
        out_specs=[pl.BlockSpec(memory_space=pltpu.VMEM)] * 2,
        scratch_shapes=[table, table],
        compiler_params=pltpu.CompilerParams(vmem_limit_bytes=56 * 1024 * 1024),
    )(frames, *arrays)


def biases_of(mask, me, devices, per_dev):
    nblk = mask.shape[0]
    biases = []
    for device in devices:
        for b in range(per_dev):
            key_block = device * per_dev + b
            inside = (key_block >= 0) & (key_block < nblk)
            column = jnp.clip(key_block, 0, nblk - 1)
            biases.append(
                [jnp.where(inside & (mask[me * per_dev + a, column] > 0), 0.0, NEG) for a in range(per_dev)]
            )
    return biases


def attend_head(h, q, kv, starts, biases, scores, weights, state):
    rows = q.shape[0]
    per_dev = rows // BLK
    kcols = slice(h * HDIM, (h + 1) * HDIM)
    vcols = slice(HC + h * HDIM, HC + (h + 1) * HDIM)
    peak = jnp.full((rows, BLK), NEG, jnp.float32)
    for i, start in enumerate(starts):
        keys = kv[pl.ds(start, rows), kcols]
        s = lax.dot_general(q, keys, (((1,), (1,)), ((), ())), preferred_element_type=jnp.float32)
        for b in range(per_dev):
            j = i * per_dev + b
            parts = [
                s[a * BLK : (a + 1) * BLK, b * BLK : (b + 1) * BLK] + biases[j][a] for a in range(per_dev)
            ]
            part = jnp.concatenate(parts, axis=0)
            peak = jnp.maximum(peak, part)
            scores[h, :, j * BLK : (j + 1) * BLK] = part
    top = jnp.max(peak, axis=1, keepdims=True)
    if state is not None:
        top = jnp.maximum(top, state[0])
    total = jnp.zeros((rows, BLK), jnp.float32)
    for j in range(len(starts) * per_dev):
        cols = slice(j * BLK, (j + 1) * BLK)
        e = jnp.exp2((scores[h, :, cols] - top) * TO_EXP2)
        total += e
        weights[h, :, cols] = e.astype(jnp.bfloat16)
    mixed = None
    for i, start in enumerate(starts):
        part = jnp.dot(
            weights[h, :, i * rows : (i + 1) * rows],
            kv[pl.ds(start, rows), vcols],
            preferred_element_type=jnp.float32,
        )
        mixed = part if mixed is None else mixed + part
    total = jnp.sum(total, axis=1, keepdims=True)
    if state is not None:
        shrink = jnp.exp2((state[0] - top) * TO_EXP2)
        total += state[1] * shrink
        mixed += state[2] * shrink
    return top, total, mixed


def fetch(pairs, sems):
    copies = []
    for i, (source, target) in enumerate(pairs):
        source = source.at[0] if len(source.shape) == 3 else source
        copies.append(pltpu.make_async_copy(source, target, sems.at[i]))
    for copy in copies:
        copy.start()
    for copy in copies:
        copy.wait()


def begin_kernel(mask, *refs):
    q_refs, kv_refs, rest = refs[:LANES], refs[LANES : 3 * LANES], refs[3 * LANES :]
    accs, stats, (q_all, kv, scores, weights, sems) = rest[:2], rest[2:4], rest[4:]
    rows = q_all.shape[1]
    per_dev = rows // BLK
    plane = lax.axis_index("plane")
    pairs = [(q_refs[step], q_all.at[step]) for step in range(LANES)]
    places = [LANES + lane_of(step) for step in range(LANES)]
    places += [part * LANES + lane_of(step) for part in (0, 2) for step in range(2)]
    for ref, place in zip(kv_refs, places):
        pairs.append((ref, kv.at[pl.ds(pl.multiple_of(place * rows, BLK), rows)]))
    fetch(pairs, sems)
    for group in range(2):

        def one_tile(core, carry):
            step = 2 * group + core
            tile = lane_of(step)
            me = plane * LANES + tile
            devices = [plane * LANES + lane for lane in range(LANES)]
            devices += chunk_devices_at(group, tile, False)
            starts = [pl.multiple_of((d - (plane - 1) * LANES) * rows, BLK) for d in devices]
            biases = biases_of(mask, me, devices, per_dev)
            for h in range(HL):
                cols = slice(h * HDIM, (h + 1) * HDIM)
                q = q_all[step, :, cols]
                top, total, mixed = attend_head(h, q, kv, starts, biases, scores, weights, None)
                accs[group][core, :, cols] = mixed
                stats[group][core, :, h : h + 1] = top
                stats[group][core, :, HL + h : HL + h + 1] = total
            return carry

        lax.fori_loop(0, 2, one_tile, 0)


def chunk_devices_at(group, tile, late):
    plane = lax.axis_index("plane")
    me = plane * LANES + tile
    row, core = lax.div(tile, 2), lax.rem(tile, 2)
    if late == (group == 1):
        return [me - REACH, me + REACH, jnp.where(core == 0, me - REACH + 1, me + REACH - 1)]
    first = jnp.where(row == 0, (plane - 1) * LANES + 2, (plane + 1) * LANES)
    return [first, first + 1]


def finish_kernel(steps, mask, *refs):
    count = len(steps)
    q_refs, accs, stats = refs[:count], refs[count : 2 * count], refs[2 * count : 3 * count]
    kv_refs, o_refs = refs[3 * count : 3 * count + LANES], refs[3 * count + LANES : 4 * count + LANES]
    q_all, kv, scores, weights, sems = refs[4 * count + LANES :]
    rows = q_all.shape[1]
    per_dev = rows // BLK
    plane = lax.axis_index("plane")
    places = [part * LANES + lane_of(step) for part in (0, 2) for step in (2, 3)]
    pairs = [
        (ref, kv.at[pl.ds(pl.multiple_of(place * rows, BLK), rows)]) for ref, place in zip(kv_refs, places)
    ]
    pairs += [(ref, q_all.at[i]) for i, ref in enumerate(q_refs)]
    fetch(pairs, sems)
    for i, (step, acc, stat, o_ref) in enumerate(zip(steps, accs, stats, o_refs)):
        tile = lane_of(step)
        me = plane * LANES + tile
        devices = chunk_devices_at(step // 2, tile, True)
        starts = [pl.multiple_of((d - (plane - 1) * LANES) * rows, BLK) for d in devices]
        biases = biases_of(mask, me, devices, per_dev)
        for h in range(HL):
            cols = slice(h * HDIM, (h + 1) * HDIM)
            state = (stat[0, :, h : h + 1], stat[0, :, HL + h : HL + h + 1], acc[0, :, cols])
            _, total, mixed = attend_head(h, q_all[i, :, cols], kv, starts, biases, scores, weights, state)
            o_ref[:, cols] = (mixed / total).astype(jnp.bfloat16)


def attend_begin(mask, q, kv):
    rows = kv[1].shape[0]
    span = 7 * rows
    vmem = pl.BlockSpec(memory_space=pltpu.VMEM)
    return pl.pallas_call(
        begin_kernel,
        out_shape=[jax.ShapeDtypeStruct((2, rows, HC), jnp.float32)] * 2
        + [jax.ShapeDtypeStruct((2, rows, HDIM), jnp.float32)] * 2,
        in_specs=[pl.BlockSpec(memory_space=pltpu.SMEM)] + [pl.BlockSpec(memory_space=pl.ANY)] * (3 * LANES),
        out_specs=[vmem] * 4,
        scratch_shapes=[
            pltpu.VMEM((LANES, rows, HC), jnp.bfloat16),
            pltpu.VMEM((3 * LANES * rows, 2 * HC), jnp.bfloat16),
            pltpu.VMEM((HL, rows, span), jnp.float32),
            pltpu.VMEM((HL, rows, span), jnp.bfloat16),
            pltpu.SemaphoreType.DMA((3 * LANES,)),
        ],
        compiler_params=pltpu.CompilerParams(vmem_limit_bytes=56 * 1024 * 1024),
        cost_estimate=BRIEF,
    )(mask, *q, *kv)


def attend_finish(steps, mask, q, begun, kv):
    rows = begun[0].shape[1]
    span = 3 * rows
    vmem = pl.BlockSpec(memory_space=pltpu.VMEM)

    def of_tile(step, width):
        return pl.BlockSpec((1, rows, width), lambda i, step=step: (step % 2, 0, 0))

    return pl.pallas_call(
        lambda *refs: finish_kernel(steps, *refs),
        grid=(1,),
        out_shape=[jax.ShapeDtypeStruct((rows, HC), jnp.bfloat16)] * len(steps),
        in_specs=[pl.BlockSpec(memory_space=pltpu.SMEM)]
        + [pl.BlockSpec(memory_space=pl.ANY)] * len(steps)
        + [of_tile(step, HC) for step in steps]
        + [of_tile(step, HDIM) for step in steps]
        + [pl.BlockSpec(memory_space=pl.ANY)] * LANES,
        out_specs=[vmem] * len(steps),
        scratch_shapes=[
            pltpu.VMEM((len(steps), rows, HC), jnp.bfloat16),
            pltpu.VMEM((3 * LANES * rows, 2 * HC), jnp.bfloat16),
            pltpu.VMEM((HL, rows, span), jnp.float32),
            pltpu.VMEM((HL, rows, span), jnp.bfloat16),
            pltpu.SemaphoreType.DMA((LANES + len(steps),)),
        ],
        compiler_params=pltpu.CompilerParams(vmem_limit_bytes=56 * 1024 * 1024),
        cost_estimate=BRIEF,
    )(
        mask,
        *[q[step] for step in steps],
        *[begun[step // 2] for step in steps],
        *[begun[2 + step // 2] for step in steps],
        *kv,
    )


def project_kernel(order, groups, steps, a_refs, w_refs, o_ref, by_lane, by_shard):
    step = pl.program_id(0)
    depth = by_shard.shape[1]
    shard = depth // len(order)

    @pl.when(step == 0)
    def _():
        for d in range(LANES):
            by_lane[lane_of(d)] = a_refs[d][...]
        parts = []
        for place in order:
            lane, at = place * shard // HC, place * shard % HC
            parts.append(by_lane[lane][:, at : at + shard])
        by_shard[...] = jnp.concatenate(parts, axis=1)

    mine, core = lax.axis_index("groups"), lax.axis_index("core")
    strip = o_ref.shape[1] // groups
    per_part = 2 * groups - 1
    begin = 0
    for part in range(len(w_refs) // per_part):
        own_ref, *half_refs = w_refs[part * per_part : (part + 1) * per_part]
        width = own_ref.shape[1]
        half = width // 2
        out = jnp.dot(by_shard[...], own_ref[...], preferred_element_type=jnp.float32)
        at = pl.multiple_of(mine * strip + begin + step * width, HDIM)
        o_ref[:, pl.ds(at, width)] = out.astype(jnp.bfloat16)
        for dx in range(1, groups):
            both = jnp.concatenate([ref[...] for ref in half_refs[2 * dx - 2 : 2 * dx]], axis=1)
            out = jnp.dot(by_shard[...], both, preferred_element_type=jnp.float32).astype(jnp.bfloat16)
            base = lax.rem(mine + groups - dx, groups) * strip + begin
            for i, which in enumerate((core, 1 - core)):
                at = pl.multiple_of(base + which * (half * steps) + step * half, HDIM)
                o_ref[:, pl.ds(at, half)] = out[:, i * half : (i + 1) * half]
        begin += width * steps


def project(attended, weights, order, groups):
    count, depth = attended[0].shape
    channels = weights[0].shape[0]
    steps = weights[-1].shape[1] // HDIM
    columns = groups * sum(w.shape[1] for w in weights[:: 2 * groups - 1])
    whole = pl.BlockSpec((count, depth), lambda n: (0, 0))
    return pl.pallas_call(
        lambda *refs: project_kernel(order, groups, steps, refs[:LANES], refs[LANES:-3], *refs[-3:]),
        out_shape=jax.ShapeDtypeStruct((count, columns), jnp.bfloat16),
        grid=(steps,),
        in_specs=[whole] * LANES
        + [pl.BlockSpec((channels, w.shape[1] // steps), lambda n: (0, n)) for w in weights],
        out_specs=pl.BlockSpec((count, columns), lambda n: (0, 0)),
        scratch_shapes=[
            pltpu.VMEM((LANES, count, depth), jnp.bfloat16),
            pltpu.VMEM((count, channels), jnp.bfloat16),
        ],
        compiler_params=pltpu.CompilerParams(vmem_limit_bytes=56 * 1024 * 1024),
    )(*attended, *weights)


def after(x, *others):
    return lax.optimization_barrier((x, *others))[0]


def on_device(queries, keys, values, frame_index, block_mask, out_weight):
    count = queries.shape[0]
    planes, groups = lax.axis_size("plane"), lax.axis_size("groups")
    seq = ("plane", "row", "core")

    def index(p, r, c):
        return (p * 2 + r) * 2 + c

    every = [(p, r, c) for p in range(planes) for r in range(2) for c in range(2)]

    def to_lane(x, dr, dc):
        return lax.ppermute(x, seq, [(index(p, r, c), index(p, r ^ dr, c ^ dc)) for p, r, c in every])

    def to_plane(x, dp):
        pairs = [(index(p, r, c), index(p + dp, r, c)) for p, r, c in every if 0 <= p + dp < planes]
        return lax.ppermute(x, seq, pairs)

    def swap(x):
        return to_lane(x[1], 0, 1)

    walk = [(p, 0) for p in range(planes)] + [(p, 1) for p in reversed(range(planes))]
    order = [index(p, r, c) for p, r in walk for c in range(2)]

    def gather(part):
        return lax.all_gather(part, seq, axis=0, tiled=True, axis_index_groups=[order])

    strip = out_weight.shape[1] // groups
    second = strip // 3 // (2 * HDIM) * 2 * HDIM
    strips = cut(out_weight, lax.axis_index("groups") * strip, (strip - second, second))
    strips = [gather(x) for x in strips]

    def exchange(part):
        half = part.shape[1] // 2
        sent = lax.dynamic_slice_in_dim(part, lax.axis_index("core") * half, half, 1)
        turns = [[(g, (g + dx) % groups) for g in range(groups)] for dx in range(1, groups)]
        return sent, [lax.ppermute(sent, "groups", turn) for turn in turns]

    own, other = pack(pack_kv_kernel, frame_index, (keys, values), 2 * HC)
    across = to_lane(other, 1, 0)
    early = [to_plane(own, dp) for dp in (1, -1)]
    beside = swap(own)
    own_q, other_q = pack(pack_q_kernel, frame_index, (after(queries, beside),), HC)
    across_q = to_lane(other_q, 1, 0)
    across_beside = swap(across)
    here = [own, beside, across, across_beside]
    q = [own_q, swap(own_q), across_q, swap(across_q)]
    onward = after(across, *early)
    late = [to_plane(onward, dp) for dp in (1, -1)]

    strips[0] = after(strips[0], *early, across_beside)
    sent, halves = exchange(strips[0])
    pieces = [piece for x in early for piece in (x, swap(x))]
    begun = attend_begin(after(block_mask, sent), q, here + pieces)
    strips[1] = after(strips[1], begun[0])
    _, second_halves = exchange(strips[1])
    late = [after(x, begun[0]) for x in late]
    late = [piece for x in late for piece in (x, swap(x))]
    mixed = attend_finish((2, 3, 1), block_mask, q, begun, late)
    moved = [to_lane(x, step // 2, step % 2) for x, step in zip(mixed, (2, 3, 1))]
    halves = [after(x, mixed[0]) for x in halves]
    own = attend_finish((0,), after(block_mask, mixed[0], *halves), q, begun, late)
    mixed = [own[0], moved[2], moved[0], moved[1]]
    second_halves = [after(x, own[0], *moved) for x in second_halves]
    weights = []
    for part, received in zip(strips, (halves, second_halves)):
        weights.append(part)
        for x in received:
            weights += [x, lax.ppermute(x, "core", [(0, 1), (1, 0)])]
    return project(mixed, weights, order, groups)


def solution(mesh):
    groups, seq = mesh.devices.shape
    split = Mesh(
        mesh.devices.reshape(groups, seq // LANES, LANES // 2, 2), ("groups", "plane", "row", "core")
    )
    along = ("plane", "row", "core")
    tokens = P(("groups",) + along, None)
    return jax.shard_map(
        on_device,
        mesh=split,
        in_specs=(tokens, tokens, tokens, P(("groups",) + along), P(), P(along, None)),
        out_specs=tokens,
        check_vma=False,
    )
```

```python
import math

import jax
import jax.numpy as jnp
from jax import lax
from jax.experimental import pallas as pl
from jax.experimental.pallas import tpu as pltpu
from jax.sharding import Mesh
from jax.sharding import PartitionSpec as P

HEADS = 12
HDIM = 128
TCH = 16
BLK = 128
LANES = 4
HL = HEADS // LANES
HC = HL * HDIM
REACH = 4
NEG = -1e30
BRIEF = pl.CostEstimate(flops=1024, bytes_accessed=1024, transcendentals=0)
TO_EXP2 = math.log2(math.e) / math.sqrt(HDIM)


def turn_tables(frames, same, other):
    lane = lax.broadcasted_iota(jnp.int32, (8, HDIM), 1)
    half = TCH // 2
    channel = lax.rem(lane, half).astype(jnp.float32)
    for block in range(same.shape[0]):
        angle = frames[block].astype(jnp.float32) * jnp.exp2(-channel)
        cosine, sine = jnp.cos(angle), jnp.sin(angle)
        same[block] = jnp.where(lane < TCH, cosine, 1.0)
        other[block] = jnp.where(lane < half, -sine, jnp.where(lane < TCH, sine, 0.0))


def cut(own, strip_at, strip, direct):
    def kernel(at, own_ref, strip_ref, direct_ref):
        strip_ref[...] = own_ref[:, pl.ds(pl.multiple_of(at[0], HDIM), strip)]
        direct_ref[...] = own_ref[:, :direct]

    rows = own.shape[0]
    vmem = pl.BlockSpec(memory_space=pltpu.VMEM)
    return pl.pallas_call(
        kernel,
        out_shape=[jax.ShapeDtypeStruct((rows, width), jnp.bfloat16) for width in (strip, direct)],
        in_specs=[pl.BlockSpec(memory_space=pltpu.SMEM), vmem],
        out_specs=[vmem] * 2,
    )(jnp.full((1,), strip_at, jnp.int32), own)


def lane_of(step):
    mine = lax.axis_index("row") * 2 + lax.axis_index("core")
    return lax.bitwise_xor(mine, step)


def turn_into(frames, x_ref, outs, same, other):
    turn_tables(frames, same, other)
    half = TCH // 2
    lane = lax.broadcasted_iota(jnp.int32, (BLK, HDIM), 1)
    for step in range(LANES):
        for head in range(HL):
            start = pl.multiple_of(lane_of(step) * HC + head * HDIM, HDIM)
            for block in range(x_ref.shape[0] // BLK):
                rows = slice(block * BLK, (block + 1) * BLK)
                x = x_ref[rows, pl.ds(start, HDIM)].astype(jnp.float32)
                partner = jnp.where(lane < half, pltpu.roll(x, HDIM - half, 1), pltpu.roll(x, half, 1))
                turned = x * same[block, :1] + partner * other[block, :1]
                cols = slice(head * HDIM, (head + 1) * HDIM)
                outs[step // 2][step % 2, rows, cols] = turned.astype(jnp.bfloat16)


def pack_kv_kernel(frames, k_ref, v_ref, *rest):
    outs, tables = rest[:3], rest[3:]
    turn_into(frames, k_ref, outs, *tables)
    for step in range(LANES):
        start = pl.multiple_of(lane_of(step) * HC, HDIM)
        outs[step // 2][step % 2, :, HC:] = v_ref[:, pl.ds(start, HC)]
    outs[2][...] = outs[0][1]


def pack_q_kernel(frames, q_ref, *rest):
    turn_into(frames, q_ref, rest[:3], *rest[3:])
    rest[2][...] = rest[0][1]


def pack(kernel, frames, arrays, width):
    count = arrays[0].shape[0]
    table = pltpu.VMEM((count // BLK, 8, HDIM), jnp.float32)
    return pl.pallas_call(
        kernel,
        out_shape=[jax.ShapeDtypeStruct((2, count, width), jnp.bfloat16)] * 2
        + [jax.ShapeDtypeStruct((count, width), jnp.bfloat16)],
        in_specs=[pl.BlockSpec(memory_space=pltpu.SMEM)]
        + [pl.BlockSpec(memory_space=pltpu.VMEM) for _ in arrays],
        out_specs=[pl.BlockSpec(memory_space=pltpu.VMEM)] * 3,
        scratch_shapes=[table, table],
        compiler_params=pltpu.CompilerParams(vmem_limit_bytes=56 * 1024 * 1024),
    )(frames, *arrays)


def biases_of(mask, me, devices, per_dev):
    nblk = mask.shape[0]
    biases = []
    for device in devices:
        for b in range(per_dev):
            key_block = device * per_dev + b
            inside = (key_block >= 0) & (key_block < nblk)
            column = jnp.clip(key_block, 0, nblk - 1)
            biases.append(
                [jnp.where(inside & (mask[me * per_dev + a, column] > 0), 0.0, NEG) for a in range(per_dev)]
            )
    return biases


def attend_head(h, q, kv, starts, biases, scores, weights, state):
    rows = q.shape[0]
    per_dev = rows // BLK
    kcols = slice(h * HDIM, (h + 1) * HDIM)
    vcols = slice(HC + h * HDIM, HC + (h + 1) * HDIM)
    peak = jnp.full((rows, BLK), NEG, jnp.float32)
    for i, start in enumerate(starts):
        keys = kv[pl.ds(start, rows), kcols]
        s = lax.dot_general(q, keys, (((1,), (1,)), ((), ())), preferred_element_type=jnp.float32)
        for b in range(per_dev):
            j = i * per_dev + b
            parts = [
                s[a * BLK : (a + 1) * BLK, b * BLK : (b + 1) * BLK] + biases[j][a] for a in range(per_dev)
            ]
            part = jnp.concatenate(parts, axis=0)
            peak = jnp.maximum(peak, part)
            scores[h, :, j * BLK : (j + 1) * BLK] = part
    top = jnp.max(peak, axis=1, keepdims=True)
    if state is not None:
        top = jnp.maximum(top, state[0])
    total = jnp.zeros((rows, BLK), jnp.float32)
    for j in range(len(starts) * per_dev):
        cols = slice(j * BLK, (j + 1) * BLK)
        e = jnp.exp2((scores[h, :, cols] - top) * TO_EXP2)
        total += e
        weights[h, :, cols] = e.astype(jnp.bfloat16)
    mixed = None
    for i, start in enumerate(starts):
        part = jnp.dot(
            weights[h, :, i * rows : (i + 1) * rows],
            kv[pl.ds(start, rows), vcols],
            preferred_element_type=jnp.float32,
        )
        mixed = part if mixed is None else mixed + part
    total = jnp.sum(total, axis=1, keepdims=True)
    if state is not None:
        shrink = jnp.exp2((state[0] - top) * TO_EXP2)
        total += state[1] * shrink
        mixed += state[2] * shrink
    return top, total, mixed


def fetch(pairs, sems):
    copies = []
    for i, (source, target) in enumerate(pairs):
        source = source.at[0] if len(source.shape) == 3 else source
        copies.append(pltpu.make_async_copy(source, target, sems.at[i]))
    for copy in copies:
        copy.start()
    for copy in copies:
        copy.wait()


def begin_kernel(mask, *refs):
    q_refs, kv_refs, rest = refs[:LANES], refs[LANES : 3 * LANES], refs[3 * LANES :]
    accs, stats, (q_all, kv, scores, weights, sems) = rest[:2], rest[2:4], rest[4:]
    rows = q_all.shape[1]
    per_dev = rows // BLK
    plane = lax.axis_index("plane")
    pairs = [(q_refs[step], q_all.at[step]) for step in range(LANES)]
    places = [LANES + lane_of(step) for step in range(LANES)]
    places += [part * LANES + lane_of(step) for part in (0, 2) for step in range(2)]
    for ref, place in zip(kv_refs, places):
        pairs.append((ref, kv.at[pl.ds(pl.multiple_of(place * rows, BLK), rows)]))
    fetch(pairs, sems)
    for group in range(2):

        def one_tile(core, carry):
            step = 2 * group + core
            tile = lane_of(step)
            me = plane * LANES + tile
            devices = [plane * LANES + lane for lane in range(LANES)]
            devices += chunk_devices_at(group, tile, False)
            starts = [pl.multiple_of((d - (plane - 1) * LANES) * rows, BLK) for d in devices]
            biases = biases_of(mask, me, devices, per_dev)
            for h in range(HL):
                cols = slice(h * HDIM, (h + 1) * HDIM)
                q = q_all[step, :, cols]
                top, total, mixed = attend_head(h, q, kv, starts, biases, scores, weights, None)
                accs[group][core, :, cols] = mixed
                stats[group][core, :, h : h + 1] = top
                stats[group][core, :, HL + h : HL + h + 1] = total
            return carry

        lax.fori_loop(0, 2, one_tile, 0)


def chunk_devices_at(group, tile, late):
    plane = lax.axis_index("plane")
    me = plane * LANES + tile
    row, core = lax.div(tile, 2), lax.rem(tile, 2)
    if late == (group == 1):
        return [me - REACH, me + REACH, jnp.where(core == 0, me - REACH + 1, me + REACH - 1)]
    first = jnp.where(row == 0, (plane - 1) * LANES + 2, (plane + 1) * LANES)
    return [first, first + 1]


def finish_kernel(steps, mask, *refs):
    count = len(steps)
    q_refs, accs, stats = refs[:count], refs[count : 2 * count], refs[2 * count : 3 * count]
    kv_refs, o_refs = refs[3 * count : 3 * count + LANES], refs[3 * count + LANES : 4 * count + LANES]
    q_all, kv, scores, weights, sems = refs[4 * count + LANES :]
    rows = q_all.shape[1]
    per_dev = rows // BLK
    plane = lax.axis_index("plane")
    places = [part * LANES + lane_of(step) for part in (0, 2) for step in (2, 3)]
    pairs = [
        (ref, kv.at[pl.ds(pl.multiple_of(place * rows, BLK), rows)]) for ref, place in zip(kv_refs, places)
    ]
    pairs += [(ref, q_all.at[i]) for i, ref in enumerate(q_refs)]
    fetch(pairs, sems)
    for i, (step, acc, stat, o_ref) in enumerate(zip(steps, accs, stats, o_refs)):
        tile = lane_of(step)
        me = plane * LANES + tile
        devices = chunk_devices_at(step // 2, tile, True)
        starts = [pl.multiple_of((d - (plane - 1) * LANES) * rows, BLK) for d in devices]
        biases = biases_of(mask, me, devices, per_dev)
        for h in range(HL):
            cols = slice(h * HDIM, (h + 1) * HDIM)
            state = (stat[0, :, h : h + 1], stat[0, :, HL + h : HL + h + 1], acc[0, :, cols])
            _, total, mixed = attend_head(h, q_all[i, :, cols], kv, starts, biases, scores, weights, state)
            o_ref[:, cols] = (mixed / total).astype(jnp.bfloat16)


def attend_begin(mask, q, kv):
    rows = kv[1].shape[0]
    span = 7 * rows
    vmem = pl.BlockSpec(memory_space=pltpu.VMEM)
    return pl.pallas_call(
        begin_kernel,
        out_shape=[jax.ShapeDtypeStruct((2, rows, HC), jnp.float32)] * 2
        + [jax.ShapeDtypeStruct((2, rows, HDIM), jnp.float32)] * 2,
        in_specs=[pl.BlockSpec(memory_space=pltpu.SMEM)] + [pl.BlockSpec(memory_space=pl.ANY)] * (3 * LANES),
        out_specs=[vmem] * 4,
        scratch_shapes=[
            pltpu.VMEM((LANES, rows, HC), jnp.bfloat16),
            pltpu.VMEM((3 * LANES * rows, 2 * HC), jnp.bfloat16),
            pltpu.VMEM((HL, rows, span), jnp.float32),
            pltpu.VMEM((HL, rows, span), jnp.bfloat16),
            pltpu.SemaphoreType.DMA((3 * LANES,)),
        ],
        compiler_params=pltpu.CompilerParams(vmem_limit_bytes=56 * 1024 * 1024),
        cost_estimate=BRIEF,
    )(mask, *q, *kv)


def attend_finish(steps, mask, q, begun, kv):
    rows = begun[0].shape[1]
    span = 3 * rows
    vmem = pl.BlockSpec(memory_space=pltpu.VMEM)

    def of_tile(step, width):
        return pl.BlockSpec((1, rows, width), lambda i, step=step: (step % 2, 0, 0))

    return pl.pallas_call(
        lambda *refs: finish_kernel(steps, *refs),
        grid=(1,),
        out_shape=[jax.ShapeDtypeStruct((rows, HC), jnp.bfloat16)] * len(steps),
        in_specs=[pl.BlockSpec(memory_space=pltpu.SMEM)]
        + [pl.BlockSpec(memory_space=pl.ANY)] * len(steps)
        + [of_tile(step, HC) for step in steps]
        + [of_tile(step, HDIM) for step in steps]
        + [pl.BlockSpec(memory_space=pl.ANY)] * LANES,
        out_specs=[vmem] * len(steps),
        scratch_shapes=[
            pltpu.VMEM((len(steps), rows, HC), jnp.bfloat16),
            pltpu.VMEM((3 * LANES * rows, 2 * HC), jnp.bfloat16),
            pltpu.VMEM((HL, rows, span), jnp.float32),
            pltpu.VMEM((HL, rows, span), jnp.bfloat16),
            pltpu.SemaphoreType.DMA((LANES + len(steps),)),
        ],
        compiler_params=pltpu.CompilerParams(vmem_limit_bytes=56 * 1024 * 1024),
        cost_estimate=BRIEF,
    )(
        mask,
        *[q[step] for step in steps],
        *[begun[step // 2] for step in steps],
        *[begun[2 + step // 2] for step in steps],
        *kv,
    )


def project_kernel(order, groups, a_refs, w_refs, o_ref, by_lane, by_shard, sems):
    step = pl.program_id(0)
    depth = by_shard.shape[1]
    shard = depth // len(order)

    @pl.when(step == 0)
    def _():
        fetch([(a_refs[d], by_lane.at[lane_of(d)]) for d in range(LANES)], sems)
        parts = []
        for place in order:
            lane, at = place * shard // HC, place * shard % HC
            parts.append(by_lane[lane][:, at : at + shard])
        by_shard[...] = jnp.concatenate(parts, axis=1)

    mine, core = lax.axis_index("groups"), lax.axis_index("core")
    widths = [w.shape[1] for w in w_refs]
    steps = o_ref.shape[1] // (widths[0] + groups * widths[1])
    direct, strip, half = widths[0] * steps, widths[1] * steps, widths[1] * steps // 2
    for w_ref, place in zip(w_refs, (0, direct + mine * strip)):
        width = w_ref.shape[1]
        out = jnp.dot(by_shard[...], w_ref[...], preferred_element_type=jnp.float32)
        o_ref[:, pl.ds(pl.multiple_of(place + step * width, HDIM), width)] = out.astype(jnp.bfloat16)
    width = half // steps
    for dx in range(1, groups):
        both = jnp.concatenate([ref[...] for ref in w_refs[2 * dx : 2 * dx + 2]], axis=1)
        out = jnp.dot(by_shard[...], both, preferred_element_type=jnp.float32).astype(jnp.bfloat16)
        start = direct + lax.rem(mine + groups - dx, groups) * strip + step * width
        for i, which in enumerate((core, 1 - core)):
            at = pl.multiple_of(start + which * half, HDIM)
            o_ref[:, pl.ds(at, width)] = out[:, i * width : (i + 1) * width]


def project(attended, weights, order, groups):
    count, depth = attended[0].shape
    channels = weights[0].shape[0]
    steps = weights[-1].shape[1] // HDIM
    columns = weights[0].shape[1] + groups * weights[1].shape[1]
    return pl.pallas_call(
        lambda *refs: project_kernel(order, groups, refs[:LANES], refs[LANES:-4], *refs[-4:]),
        out_shape=jax.ShapeDtypeStruct((count, columns), jnp.bfloat16),
        grid=(steps,),
        in_specs=[pl.BlockSpec(memory_space=pltpu.HBM)] * LANES
        + [pl.BlockSpec((channels, w.shape[1] // steps), lambda n: (0, n)) for w in weights],
        out_specs=pl.BlockSpec((count, columns), lambda n: (0, 0)),
        scratch_shapes=[
            pltpu.VMEM((LANES, count, depth), jnp.bfloat16),
            pltpu.VMEM((count, channels), jnp.bfloat16),
            pltpu.SemaphoreType.DMA((LANES,)),
        ],
        compiler_params=pltpu.CompilerParams(vmem_limit_bytes=56 * 1024 * 1024),
    )(*attended, *weights)


def after(x, *others):
    return lax.optimization_barrier((x, *others))[0]


def on_device(queries, keys, values, frame_index, block_mask, out_weight):
    count = queries.shape[0]
    planes, groups = lax.axis_size("plane"), lax.axis_size("groups")
    seq = ("plane", "row", "core")

    def index(p, r, c):
        return (p * 2 + r) * 2 + c

    every = [(p, r, c) for p in range(planes) for r in range(2) for c in range(2)]

    def to_lane(x, dr, dc):
        return lax.ppermute(x, seq, [(index(p, r, c), index(p, r ^ dr, c ^ dc)) for p, r, c in every])

    def to_plane(x, dp):
        pairs = [(index(p, r, c), index(p + dp, r, c)) for p, r, c in every if 0 <= p + dp < planes]
        return lax.ppermute(x, seq, pairs)

    def swap(x):
        return to_lane(x[1], 0, 1)

    walk = [(p, 0) for p in range(planes)] + [(p, 1) for p in reversed(range(planes))]
    order = [index(p, r, c) for p, r in walk for c in range(2)]

    def gather(part):
        return lax.all_gather(part, seq, axis=0, tiled=True, axis_index_groups=[order])

    columns = out_weight.shape[1]
    strip = 2 * columns // 3 // (groups * 2 * HDIM) * 2 * HDIM
    direct = columns - groups * strip
    strip_at = direct + lax.axis_index("groups") * strip
    own_strip, direct_strip = [gather(x) for x in cut(out_weight, strip_at, strip, direct)]

    own, other, own_beside = pack(pack_kv_kernel, frame_index, (keys, values), 2 * HC)
    across = to_lane(other, 1, 0)
    early = [to_plane(own, dp) for dp in (1, -1)]
    beside = to_lane(own_beside, 0, 1)
    own_q, other_q, own_q_beside = pack(pack_q_kernel, frame_index, (after(queries, beside),), HC)
    across_q = to_lane(other_q, 1, 0)
    across_beside = swap(across)
    here = [own, beside, across, across_beside]
    q = [own_q, to_lane(own_q_beside, 0, 1), across_q, swap(across_q)]
    onward = after(across, *early)
    late = [to_plane(onward, dp) for dp in (1, -1)]

    own_strip = after(own_strip, *early, across_beside)
    half = strip // 2
    core_at = lax.axis_index("core") * half
    sent = lax.dynamic_slice_in_dim(own_strip, core_at, half, 1)
    halves = [
        lax.ppermute(sent, "groups", [(g, (g + dx) % groups) for g in range(groups)])
        for dx in range(1, groups)
    ]
    pieces = [piece for x in early for piece in (x, swap(x))]
    begun = attend_begin(after(block_mask, sent), q, here + pieces)
    late = [after(x, begun[0]) for x in late]
    late = [piece for x in late for piece in (x, swap(x))]
    mixed = attend_finish((2, 3, 1), block_mask, q, begun, late)
    moved = [to_lane(x, step // 2, step % 2) for x, step in zip(mixed, (2, 3, 1))]
    halves = [after(x, mixed[0]) for x in halves]
    own = attend_finish((0,), after(block_mask, mixed[0], *halves), q, begun, late)
    mixed = [own[0], moved[2], moved[0], moved[1]]
    weights = [direct_strip, own_strip]
    for x in halves:
        weights += [x, lax.ppermute(x, "core", [(0, 1), (1, 0)])]
    return project(mixed, weights, order, groups)


def solution(mesh):
    groups, seq = mesh.devices.shape
    split = Mesh(
        mesh.devices.reshape(groups, seq // LANES, LANES // 2, 2), ("groups", "plane", "row", "core")
    )
    along = ("plane", "row", "core")
    tokens = P(("groups",) + along, None)
    return jax.shard_map(
        on_device,
        mesh=split,
        in_specs=(tokens, tokens, tokens, P(("groups",) + along), P(), P(along, None)),
        out_specs=tokens,
        check_vma=False,
    )
```

```python
import math

import jax
import jax.numpy as jnp
from jax import lax
from jax.experimental import pallas as pl
from jax.experimental.pallas import tpu as pltpu
from jax.sharding import Mesh
from jax.sharding import PartitionSpec as P

HEADS = 12
HDIM = 128
TCH = 16
BLK = 128
LANES = 4
HL = HEADS // LANES
HC = HL * HDIM
REACH = 4
NEG = -1e30
BRIEF = pl.CostEstimate(flops=1024, bytes_accessed=1024, transcendentals=0)
TO_EXP2 = math.log2(math.e) / math.sqrt(HDIM)


def turn_tables(frames, same, other):
    lane = lax.broadcasted_iota(jnp.int32, (8, HDIM), 1)
    half = TCH // 2
    channel = lax.rem(lane, half).astype(jnp.float32)
    for block in range(same.shape[0]):
        angle = frames[block].astype(jnp.float32) * jnp.exp2(-channel)
        cosine, sine = jnp.cos(angle), jnp.sin(angle)
        same[block] = jnp.where(lane < TCH, cosine, 1.0)
        other[block] = jnp.where(lane < half, -sine, jnp.where(lane < TCH, sine, 0.0))


def cut(own, strip_at, strip, direct):
    def kernel(at, own_ref, strip_ref, direct_ref):
        strip_ref[...] = own_ref[:, pl.ds(pl.multiple_of(at[0], HDIM), strip)]
        direct_ref[...] = own_ref[:, :direct]

    rows = own.shape[0]
    vmem = pl.BlockSpec(memory_space=pltpu.VMEM)
    return pl.pallas_call(
        kernel,
        out_shape=[jax.ShapeDtypeStruct((rows, width), jnp.bfloat16) for width in (strip, direct)],
        in_specs=[pl.BlockSpec(memory_space=pltpu.SMEM), vmem],
        out_specs=[vmem] * 2,
    )(jnp.full((1,), strip_at, jnp.int32), own)


def lane_of(step):
    mine = lax.axis_index("row") * 2 + lax.axis_index("core")
    return lax.bitwise_xor(mine, step)


def turn_into(frames, x_ref, outs, same, other):
    turn_tables(frames, same, other)
    half = TCH // 2
    lane = lax.broadcasted_iota(jnp.int32, (BLK, HDIM), 1)
    for step in range(LANES):
        for head in range(HL):
            start = pl.multiple_of(lane_of(step) * HC + head * HDIM, HDIM)
            for block in range(x_ref.shape[0] // BLK):
                rows = slice(block * BLK, (block + 1) * BLK)
                x = x_ref[rows, pl.ds(start, HDIM)].astype(jnp.float32)
                partner = jnp.where(lane < half, pltpu.roll(x, HDIM - half, 1), pltpu.roll(x, half, 1))
                turned = x * same[block, :1] + partner * other[block, :1]
                cols = slice(head * HDIM, (head + 1) * HDIM)
                outs[step // 2][step % 2, rows, cols] = turned.astype(jnp.bfloat16)


def pack_kv_kernel(frames, k_ref, v_ref, *rest):
    outs, tables = rest[:3], rest[3:]
    turn_into(frames, k_ref, outs, *tables)
    for step in range(LANES):
        start = pl.multiple_of(lane_of(step) * HC, HDIM)
        outs[step // 2][step % 2, :, HC:] = v_ref[:, pl.ds(start, HC)]
    outs[2][...] = outs[0][1]


def pack_q_kernel(frames, q_ref, *rest):
    turn_into(frames, q_ref, rest[:3], *rest[3:])
    rest[2][...] = rest[0][1]


def pack(kernel, frames, arrays, width):
    count = arrays[0].shape[0]
    table = pltpu.VMEM((count // BLK, 8, HDIM), jnp.float32)
    return pl.pallas_call(
        kernel,
        out_shape=[jax.ShapeDtypeStruct((2, count, width), jnp.bfloat16)] * 2
        + [jax.ShapeDtypeStruct((count, width), jnp.bfloat16)],
        in_specs=[pl.BlockSpec(memory_space=pltpu.SMEM)]
        + [pl.BlockSpec(memory_space=pltpu.VMEM) for _ in arrays],
        out_specs=[pl.BlockSpec(memory_space=pltpu.VMEM)] * 3,
        scratch_shapes=[table, table],
        compiler_params=pltpu.CompilerParams(vmem_limit_bytes=56 * 1024 * 1024),
    )(frames, *arrays)


def biases_of(mask, me, devices, per_dev):
    nblk = mask.shape[0]
    biases = []
    for device in devices:
        for b in range(per_dev):
            key_block = device * per_dev + b
            inside = (key_block >= 0) & (key_block < nblk)
            column = jnp.clip(key_block, 0, nblk - 1)
            biases.append(
                [jnp.where(inside & (mask[me * per_dev + a, column] > 0), 0.0, NEG) for a in range(per_dev)]
            )
    return biases


def attend_head(h, q, kv, starts, biases, scores, weights, state):
    rows = q.shape[0]
    per_dev = rows // BLK
    kcols = slice(h * HDIM, (h + 1) * HDIM)
    vcols = slice(HC + h * HDIM, HC + (h + 1) * HDIM)
    peak = jnp.full((rows, BLK), NEG, jnp.float32)
    for i, start in enumerate(starts):
        keys = kv[pl.ds(start, rows), kcols]
        s = lax.dot_general(q, keys, (((1,), (1,)), ((), ())), preferred_element_type=jnp.float32)
        for b in range(per_dev):
            j = i * per_dev + b
            parts = [
                s[a * BLK : (a + 1) * BLK, b * BLK : (b + 1) * BLK] + biases[j][a] for a in range(per_dev)
            ]
            part = jnp.concatenate(parts, axis=0)
            peak = jnp.maximum(peak, part)
            scores[h, :, j * BLK : (j + 1) * BLK] = part
    top = jnp.max(peak, axis=1, keepdims=True)
    if state is not None:
        top = jnp.maximum(top, state[0])
    total = jnp.zeros((rows, BLK), jnp.float32)
    for j in range(len(starts) * per_dev):
        cols = slice(j * BLK, (j + 1) * BLK)
        e = jnp.exp2((scores[h, :, cols] - top) * TO_EXP2)
        total += e
        weights[h, :, cols] = e.astype(jnp.bfloat16)
    mixed = None
    for i, start in enumerate(starts):
        part = jnp.dot(
            weights[h, :, i * rows : (i + 1) * rows],
            kv[pl.ds(start, rows), vcols],
            preferred_element_type=jnp.float32,
        )
        mixed = part if mixed is None else mixed + part
    total = jnp.sum(total, axis=1, keepdims=True)
    if state is not None:
        shrink = jnp.exp2((state[0] - top) * TO_EXP2)
        total += state[1] * shrink
        mixed += state[2] * shrink
    return top, total, mixed


def fetch(pairs, sems):
    copies = []
    for i, (source, target) in enumerate(pairs):
        source = source.at[0] if len(source.shape) == 3 else source
        copies.append(pltpu.make_async_copy(source, target, sems.at[i]))
    for copy in copies:
        copy.start()
    for copy in copies:
        copy.wait()


def begin_kernel(mask, *refs):
    q_refs, kv_refs, rest = refs[:LANES], refs[LANES : 3 * LANES], refs[3 * LANES :]
    accs, stats, (q_all, kv, scores, weights, sems) = rest[:2], rest[2:4], rest[4:]
    rows = q_all.shape[1]
    per_dev = rows // BLK
    plane = lax.axis_index("plane")
    pairs = [(q_refs[step], q_all.at[step]) for step in range(LANES)]
    places = [LANES + lane_of(step) for step in range(LANES)]
    places += [part * LANES + lane_of(step) for part in (0, 2) for step in range(2)]
    for ref, place in zip(kv_refs, places):
        pairs.append((ref, kv.at[pl.ds(pl.multiple_of(place * rows, BLK), rows)]))
    fetch(pairs, sems)
    for group in range(2):

        def one_tile(core, carry):
            step = 2 * group + core
            tile = lane_of(step)
            me = plane * LANES + tile
            devices = [plane * LANES + lane for lane in range(LANES)]
            devices += chunk_devices_at(group, tile, False)
            starts = [pl.multiple_of((d - (plane - 1) * LANES) * rows, BLK) for d in devices]
            biases = biases_of(mask, me, devices, per_dev)
            for h in range(HL):
                cols = slice(h * HDIM, (h + 1) * HDIM)
                q = q_all[step, :, cols]
                top, total, mixed = attend_head(h, q, kv, starts, biases, scores, weights, None)
                accs[group][core, :, cols] = mixed
                stats[group][core, :, h : h + 1] = top
                stats[group][core, :, HL + h : HL + h + 1] = total
            return carry

        lax.fori_loop(0, 2, one_tile, 0)


def chunk_devices_at(group, tile, late):
    plane = lax.axis_index("plane")
    me = plane * LANES + tile
    row, core = lax.div(tile, 2), lax.rem(tile, 2)
    if late == (group == 1):
        return [me - REACH, me + REACH, jnp.where(core == 0, me - REACH + 1, me + REACH - 1)]
    first = jnp.where(row == 0, (plane - 1) * LANES + 2, (plane + 1) * LANES)
    return [first, first + 1]


def finish_kernel(steps, mask, *refs):
    count = len(steps)
    q_refs, accs, stats = refs[:count], refs[count : 2 * count], refs[2 * count : 3 * count]
    kv_refs, o_refs = refs[3 * count : 3 * count + LANES], refs[3 * count + LANES : 4 * count + LANES]
    q_all, kv, scores, weights, sems = refs[4 * count + LANES :]
    rows = q_all.shape[1]
    per_dev = rows // BLK
    plane = lax.axis_index("plane")
    places = [part * LANES + lane_of(step) for part in (0, 2) for step in (2, 3)]
    pairs = [
        (ref, kv.at[pl.ds(pl.multiple_of(place * rows, BLK), rows)]) for ref, place in zip(kv_refs, places)
    ]
    pairs += [(ref, q_all.at[i]) for i, ref in enumerate(q_refs)]
    fetch(pairs, sems)
    for i, (step, acc, stat, o_ref) in enumerate(zip(steps, accs, stats, o_refs)):
        tile = lane_of(step)
        me = plane * LANES + tile
        devices = chunk_devices_at(step // 2, tile, True)
        starts = [pl.multiple_of((d - (plane - 1) * LANES) * rows, BLK) for d in devices]
        biases = biases_of(mask, me, devices, per_dev)
        for h in range(HL):
            cols = slice(h * HDIM, (h + 1) * HDIM)
            state = (stat[0, :, h : h + 1], stat[0, :, HL + h : HL + h + 1], acc[0, :, cols])
            _, total, mixed = attend_head(h, q_all[i, :, cols], kv, starts, biases, scores, weights, state)
            o_ref[:, cols] = (mixed / total).astype(jnp.bfloat16)


def attend_begin(mask, q, kv):
    rows = kv[1].shape[0]
    span = 7 * rows
    vmem = pl.BlockSpec(memory_space=pltpu.VMEM)
    return pl.pallas_call(
        begin_kernel,
        out_shape=[jax.ShapeDtypeStruct((2, rows, HC), jnp.float32)] * 2
        + [jax.ShapeDtypeStruct((2, rows, HDIM), jnp.float32)] * 2,
        in_specs=[pl.BlockSpec(memory_space=pltpu.SMEM)] + [pl.BlockSpec(memory_space=pl.ANY)] * (3 * LANES),
        out_specs=[vmem] * 4,
        scratch_shapes=[
            pltpu.VMEM((LANES, rows, HC), jnp.bfloat16),
            pltpu.VMEM((3 * LANES * rows, 2 * HC), jnp.bfloat16),
            pltpu.VMEM((HL, rows, span), jnp.float32),
            pltpu.VMEM((HL, rows, span), jnp.bfloat16),
            pltpu.SemaphoreType.DMA((3 * LANES,)),
        ],
        compiler_params=pltpu.CompilerParams(vmem_limit_bytes=56 * 1024 * 1024),
        cost_estimate=BRIEF,
    )(mask, *q, *kv)


def attend_finish(steps, mask, q, begun, kv):
    rows = begun[0].shape[1]
    span = 3 * rows
    vmem = pl.BlockSpec(memory_space=pltpu.VMEM)

    def of_tile(step, width):
        return pl.BlockSpec((1, rows, width), lambda i, step=step: (step % 2, 0, 0))

    return pl.pallas_call(
        lambda *refs: finish_kernel(steps, *refs),
        grid=(1,),
        out_shape=[jax.ShapeDtypeStruct((rows, HC), jnp.bfloat16)] * len(steps),
        in_specs=[pl.BlockSpec(memory_space=pltpu.SMEM)]
        + [pl.BlockSpec(memory_space=pl.ANY)] * len(steps)
        + [of_tile(step, HC) for step in steps]
        + [of_tile(step, HDIM) for step in steps]
        + [pl.BlockSpec(memory_space=pl.ANY)] * LANES,
        out_specs=[vmem] * len(steps),
        scratch_shapes=[
            pltpu.VMEM((len(steps), rows, HC), jnp.bfloat16),
            pltpu.VMEM((3 * LANES * rows, 2 * HC), jnp.bfloat16),
            pltpu.VMEM((HL, rows, span), jnp.float32),
            pltpu.VMEM((HL, rows, span), jnp.bfloat16),
            pltpu.SemaphoreType.DMA((LANES + len(steps),)),
        ],
        compiler_params=pltpu.CompilerParams(vmem_limit_bytes=56 * 1024 * 1024),
        cost_estimate=BRIEF,
    )(
        mask,
        *[q[step] for step in steps],
        *[begun[step // 2] for step in steps],
        *[begun[2 + step // 2] for step in steps],
        *kv,
    )


def project_kernel(order, groups, a_refs, w_refs, o_ref, by_lane, by_shard, sems):
    step = pl.program_id(0)
    depth = by_shard.shape[1]
    shard = depth // len(order)

    @pl.when(step == 0)
    def _():
        fetch([(a_refs[d], by_lane.at[lane_of(d)]) for d in range(LANES)], sems)
        parts = []
        for place in order:
            lane, at = place * shard // HC, place * shard % HC
            parts.append(by_lane[lane][:, at : at + shard])
        by_shard[...] = jnp.concatenate(parts, axis=1)

    mine, core = lax.axis_index("groups"), lax.axis_index("core")
    widths = [w.shape[1] for w in w_refs]
    steps = o_ref.shape[1] // (widths[0] + groups * widths[1])
    direct, strip, half = widths[0] * steps, widths[1] * steps, widths[1] * steps // 2
    for w_ref, place in zip(w_refs, (0, direct + mine * strip)):
        width = w_ref.shape[1]
        out = jnp.dot(by_shard[...], w_ref[...], preferred_element_type=jnp.float32)
        o_ref[:, pl.ds(pl.multiple_of(place + step * width, HDIM), width)] = out.astype(jnp.bfloat16)
    width = half // steps
    for dx in range(1, groups):
        both = jnp.concatenate([ref[...] for ref in w_refs[2 * dx : 2 * dx + 2]], axis=1)
        out = jnp.dot(by_shard[...], both, preferred_element_type=jnp.float32).astype(jnp.bfloat16)
        start = direct + lax.rem(mine + groups - dx, groups) * strip + step * width
        for i, which in enumerate((core, 1 - core)):
            at = pl.multiple_of(start + which * half, HDIM)
            o_ref[:, pl.ds(at, width)] = out[:, i * width : (i + 1) * width]


def project(attended, weights, order, groups):
    count, depth = attended[0].shape
    channels = weights[0].shape[0]
    steps = weights[-1].shape[1] // HDIM
    columns = weights[0].shape[1] + groups * weights[1].shape[1]
    return pl.pallas_call(
        lambda *refs: project_kernel(order, groups, refs[:LANES], refs[LANES:-4], *refs[-4:]),
        out_shape=jax.ShapeDtypeStruct((count, columns), jnp.bfloat16),
        grid=(steps,),
        in_specs=[pl.BlockSpec(memory_space=pltpu.HBM)] * LANES
        + [pl.BlockSpec((channels, w.shape[1] // steps), lambda n: (0, n)) for w in weights],
        out_specs=pl.BlockSpec((count, columns), lambda n: (0, 0)),
        scratch_shapes=[
            pltpu.VMEM((LANES, count, depth), jnp.bfloat16),
            pltpu.VMEM((count, channels), jnp.bfloat16),
            pltpu.SemaphoreType.DMA((LANES,)),
        ],
        compiler_params=pltpu.CompilerParams(vmem_limit_bytes=56 * 1024 * 1024),
    )(*attended, *weights)


def after(x, *others):
    return lax.optimization_barrier((x, *others))[0]


def on_device(queries, keys, values, frame_index, block_mask, out_weight):
    count = queries.shape[0]
    planes, groups = lax.axis_size("plane"), lax.axis_size("groups")
    seq = ("plane", "row", "core")

    def index(p, r, c):
        return (p * 2 + r) * 2 + c

    every = [(p, r, c) for p in range(planes) for r in range(2) for c in range(2)]

    def to_lane(x, dr, dc):
        return lax.ppermute(x, seq, [(index(p, r, c), index(p, r ^ dr, c ^ dc)) for p, r, c in every])

    def to_plane(x, dp):
        pairs = [(index(p, r, c), index(p + dp, r, c)) for p, r, c in every if 0 <= p + dp < planes]
        return lax.ppermute(x, seq, pairs)

    def swap(x):
        return to_lane(x[1], 0, 1)

    walk = [(p, 0) for p in range(planes)] + [(p, 1) for p in reversed(range(planes))]
    order = [index(p, r, c) for p, r in walk for c in range(2)]

    def gather(part):
        return lax.all_gather(part, seq, axis=0, tiled=True, axis_index_groups=[order])

    columns = out_weight.shape[1]
    strip = 2 * columns // 3 // (groups * 2 * HDIM) * 2 * HDIM
    direct = columns - groups * strip
    strip_at = direct + lax.axis_index("groups") * strip
    own_strip, direct_strip = [gather(x) for x in cut(out_weight, strip_at, strip, direct)]

    own, other, own_beside = pack(pack_kv_kernel, frame_index, (keys, values), 2 * HC)
    across = to_lane(other, 1, 0)
    early = [to_plane(own, dp) for dp in (1, -1)]
    beside = to_lane(own_beside, 0, 1)
    own_q, other_q, own_q_beside = pack(pack_q_kernel, frame_index, (after(queries, beside),), HC)
    across_q = to_lane(other_q, 1, 0)
    across_beside = swap(across)
    here = [own, beside, across, across_beside]
    q = [own_q, to_lane(own_q_beside, 0, 1), across_q, swap(across_q)]
    onward = after(across, *early)
    late = [to_plane(onward, dp) for dp in (1, -1)]

    own_strip = after(own_strip, *early, across_beside)
    half = strip // 2
    core_at = lax.axis_index("core") * half
    sent = lax.dynamic_slice_in_dim(own_strip, core_at, half, 1)
    halves = [
        lax.ppermute(sent, "groups", [(g, (g + dx) % groups) for g in range(groups)])
        for dx in range(1, groups)
    ]
    pieces = [piece for x in early for piece in (x, swap(x))]
    begun = attend_begin(after(block_mask, sent), q, here + pieces)
    late = [after(x, begun[0]) for x in late]
    late = [piece for x in late for piece in (x, swap(x))]
    mixed = attend_finish((2, 3), block_mask, q, begun, late)
    back = [to_lane(x, 1, d) for d, x in enumerate(mixed)]
    halves = [after(x, mixed[0]) for x in halves]
    rest = attend_finish((0, 1), after(block_mask, mixed[0], *halves), q, begun, late)
    mixed = [rest[0], to_lane(after(rest[1], back[0]), 0, 1)] + back
    weights = [direct_strip, own_strip]
    for x in halves:
        weights += [x, lax.ppermute(x, "core", [(0, 1), (1, 0)])]
    return project(mixed, weights, order, groups)


def solution(mesh):
    groups, seq = mesh.devices.shape
    split = Mesh(
        mesh.devices.reshape(groups, seq // LANES, LANES // 2, 2), ("groups", "plane", "row", "core")
    )
    along = ("plane", "row", "core")
    tokens = P(("groups",) + along, None)
    return jax.shard_map(
        on_device,
        mesh=split,
        in_specs=(tokens, tokens, tokens, P(("groups",) + along), P(), P(along, None)),
        out_specs=tokens,
        check_vma=False,
    )
```

```python
import math

import jax
import jax.numpy as jnp
from jax import lax
from jax.experimental import pallas as pl
from jax.experimental.pallas import tpu as pltpu
from jax.sharding import Mesh
from jax.sharding import PartitionSpec as P

HEADS = 12
HDIM = 128
TCH = 16
BLK = 128
LANES = 4
HL = HEADS // LANES
HC = HL * HDIM
REACH = 4
NEG = -1e30
BRIEF = pl.CostEstimate(flops=1024, bytes_accessed=1024, transcendentals=0)
TO_EXP2 = math.log2(math.e) / math.sqrt(HDIM)


def turn_tables(frames, same, other):
    lane = lax.broadcasted_iota(jnp.int32, (8, HDIM), 1)
    half = TCH // 2
    channel = lax.rem(lane, half).astype(jnp.float32)
    for block in range(same.shape[0]):
        angle = frames[block].astype(jnp.float32) * jnp.exp2(-channel)
        cosine, sine = jnp.cos(angle), jnp.sin(angle)
        same[block] = jnp.where(lane < TCH, cosine, 1.0)
        other[block] = jnp.where(lane < half, -sine, jnp.where(lane < TCH, sine, 0.0))


def cut(own, strip_at, strip, direct):
    def kernel(at, own_ref, strip_ref, direct_ref):
        strip_ref[...] = own_ref[:, pl.ds(pl.multiple_of(at[0], HDIM), strip)]
        direct_ref[...] = own_ref[:, :direct]

    rows = own.shape[0]
    vmem = pl.BlockSpec(memory_space=pltpu.VMEM)
    return pl.pallas_call(
        kernel,
        out_shape=[jax.ShapeDtypeStruct((rows, width), jnp.bfloat16) for width in (strip, direct)],
        in_specs=[pl.BlockSpec(memory_space=pltpu.SMEM), vmem],
        out_specs=[vmem] * 2,
    )(jnp.full((1,), strip_at, jnp.int32), own)


def lane_of(step):
    mine = lax.axis_index("row") * 2 + lax.axis_index("core")
    return lax.bitwise_xor(mine, step)


def turn_into(frames, x_ref, outs, same, other):
    turn_tables(frames, same, other)
    half = TCH // 2
    lane = lax.broadcasted_iota(jnp.int32, (BLK, HDIM), 1)
    for step in range(LANES):
        for head in range(HL):
            start = pl.multiple_of(lane_of(step) * HC + head * HDIM, HDIM)
            for block in range(x_ref.shape[0] // BLK):
                rows = slice(block * BLK, (block + 1) * BLK)
                x = x_ref[rows, pl.ds(start, HDIM)].astype(jnp.float32)
                partner = jnp.where(lane < half, pltpu.roll(x, HDIM - half, 1), pltpu.roll(x, half, 1))
                turned = x * same[block, :1] + partner * other[block, :1]
                cols = slice(head * HDIM, (head + 1) * HDIM)
                outs[step // 2][step % 2, rows, cols] = turned.astype(jnp.bfloat16)


def pack_kv_kernel(frames, k_ref, v_ref, *rest):
    outs, tables = rest[:3], rest[3:]
    turn_into(frames, k_ref, outs, *tables)
    for step in range(LANES):
        start = pl.multiple_of(lane_of(step) * HC, HDIM)
        outs[step // 2][step % 2, :, HC:] = v_ref[:, pl.ds(start, HC)]
    outs[2][...] = outs[0][1]


def pack_q_kernel(frames, q_ref, *rest):
    turn_into(frames, q_ref, rest[:3], *rest[3:])
    rest[2][...] = rest[0][1]


def pack(kernel, frames, arrays, width):
    count = arrays[0].shape[0]
    table = pltpu.VMEM((count // BLK, 8, HDIM), jnp.float32)
    return pl.pallas_call(
        kernel,
        out_shape=[jax.ShapeDtypeStruct((2, count, width), jnp.bfloat16)] * 2
        + [jax.ShapeDtypeStruct((count, width), jnp.bfloat16)],
        in_specs=[pl.BlockSpec(memory_space=pltpu.SMEM)]
        + [pl.BlockSpec(memory_space=pltpu.VMEM) for _ in arrays],
        out_specs=[pl.BlockSpec(memory_space=pltpu.VMEM)] * 3,
        scratch_shapes=[table, table],
        compiler_params=pltpu.CompilerParams(vmem_limit_bytes=56 * 1024 * 1024),
    )(frames, *arrays)


def biases_of(mask, me, devices, per_dev):
    nblk = mask.shape[0]
    biases = []
    for device in devices:
        for b in range(per_dev):
            key_block = device * per_dev + b
            inside = (key_block >= 0) & (key_block < nblk)
            column = jnp.clip(key_block, 0, nblk - 1)
            biases.append(
                [jnp.where(inside & (mask[me * per_dev + a, column] > 0), 0.0, NEG) for a in range(per_dev)]
            )
    return biases


def attend_head(h, q, kv, starts, biases, scores, weights, state):
    rows = q.shape[0]
    per_dev = rows // BLK
    kcols = slice(h * HDIM, (h + 1) * HDIM)
    vcols = slice(HC + h * HDIM, HC + (h + 1) * HDIM)
    peak = jnp.full((rows, BLK), NEG, jnp.float32)
    for i, start in enumerate(starts):
        keys = kv[pl.ds(start, rows), kcols]
        s = lax.dot_general(q, keys, (((1,), (1,)), ((), ())), preferred_element_type=jnp.float32)
        for b in range(per_dev):
            j = i * per_dev + b
            parts = [
                s[a * BLK : (a + 1) * BLK, b * BLK : (b + 1) * BLK] + biases[j][a] for a in range(per_dev)
            ]
            part = jnp.concatenate(parts, axis=0)
            peak = jnp.maximum(peak, part)
            scores[h, :, j * BLK : (j + 1) * BLK] = part
    top = jnp.max(peak, axis=1, keepdims=True)
    if state is not None:
        top = jnp.maximum(top, state[0])
    total = jnp.zeros((rows, BLK), jnp.float32)
    for j in range(len(starts) * per_dev):
        cols = slice(j * BLK, (j + 1) * BLK)
        e = jnp.exp2((scores[h, :, cols] - top) * TO_EXP2)
        total += e
        weights[h, :, cols] = e.astype(jnp.bfloat16)
    mixed = None
    for i, start in enumerate(starts):
        part = jnp.dot(
            weights[h, :, i * rows : (i + 1) * rows],
            kv[pl.ds(start, rows), vcols],
            preferred_element_type=jnp.float32,
        )
        mixed = part if mixed is None else mixed + part
    total = jnp.sum(total, axis=1, keepdims=True)
    if state is not None:
        shrink = jnp.exp2((state[0] - top) * TO_EXP2)
        total += state[1] * shrink
        mixed += state[2] * shrink
    return top, total, mixed


def fetch(pairs, sems):
    copies = []
    for i, (source, target) in enumerate(pairs):
        source = source.at[0] if len(source.shape) == 3 else source
        copies.append(pltpu.make_async_copy(source, target, sems.at[i]))
    for copy in copies:
        copy.start()
    for copy in copies:
        copy.wait()


def begin_kernel(mask, *refs):
    q_refs, kv_refs, rest = refs[:LANES], refs[LANES : 3 * LANES], refs[3 * LANES :]
    accs, stats, (q_all, kv, scores, weights, sems) = rest[:2], rest[2:4], rest[4:]
    rows = q_all.shape[1]
    per_dev = rows // BLK
    plane = lax.axis_index("plane")
    pairs = [(q_refs[step], q_all.at[step]) for step in range(LANES)]
    places = [LANES + lane_of(step) for step in range(LANES)]
    places += [part * LANES + lane_of(step) for part in (0, 2) for step in range(2)]
    for ref, place in zip(kv_refs, places):
        pairs.append((ref, kv.at[pl.ds(pl.multiple_of(place * rows, BLK), rows)]))
    fetch(pairs, sems)
    for group in range(2):

        def one_tile(core, carry):
            step = 2 * group + core
            tile = lane_of(step)
            me = plane * LANES + tile
            devices = [plane * LANES + lane for lane in range(LANES)]
            devices += chunk_devices_at(group, tile, False)
            starts = [pl.multiple_of((d - (plane - 1) * LANES) * rows, BLK) for d in devices]
            biases = biases_of(mask, me, devices, per_dev)
            for h in range(HL):
                cols = slice(h * HDIM, (h + 1) * HDIM)
                q = q_all[step, :, cols]
                top, total, mixed = attend_head(h, q, kv, starts, biases, scores, weights, None)
                accs[group][core, :, cols] = mixed
                stats[group][core, :, h : h + 1] = top
                stats[group][core, :, HL + h : HL + h + 1] = total
            return carry

        lax.fori_loop(0, 2, one_tile, 0)


def chunk_devices_at(group, tile, late):
    plane = lax.axis_index("plane")
    me = plane * LANES + tile
    row, core = lax.div(tile, 2), lax.rem(tile, 2)
    if late == (group == 1):
        return [me - REACH, me + REACH, jnp.where(core == 0, me - REACH + 1, me + REACH - 1)]
    first = jnp.where(row == 0, (plane - 1) * LANES + 2, (plane + 1) * LANES)
    return [first, first + 1]


def finish_kernel(steps, mask, *refs):
    count = len(steps)
    q_refs, accs, stats = refs[:count], refs[count : 2 * count], refs[2 * count : 3 * count]
    kv_refs, o_refs = refs[3 * count : 3 * count + LANES], refs[3 * count + LANES : 4 * count + LANES]
    q_all, kv, scores, weights, sems = refs[4 * count + LANES :]
    rows = q_all.shape[1]
    per_dev = rows // BLK
    plane = lax.axis_index("plane")
    places = [part * LANES + lane_of(step) for part in (0, 2) for step in (2, 3)]
    pairs = [
        (ref, kv.at[pl.ds(pl.multiple_of(place * rows, BLK), rows)]) for ref, place in zip(kv_refs, places)
    ]
    pairs += [(ref, q_all.at[i]) for i, ref in enumerate(q_refs)]
    fetch(pairs, sems)
    for i, (step, acc, stat, o_ref) in enumerate(zip(steps, accs, stats, o_refs)):
        tile = lane_of(step)
        me = plane * LANES + tile
        devices = chunk_devices_at(step // 2, tile, True)
        starts = [pl.multiple_of((d - (plane - 1) * LANES) * rows, BLK) for d in devices]
        biases = biases_of(mask, me, devices, per_dev)
        for h in range(HL):
            cols = slice(h * HDIM, (h + 1) * HDIM)
            state = (stat[0, :, h : h + 1], stat[0, :, HL + h : HL + h + 1], acc[0, :, cols])
            _, total, mixed = attend_head(h, q_all[i, :, cols], kv, starts, biases, scores, weights, state)
            o_ref[:, cols] = (mixed / total).astype(jnp.bfloat16)


def attend_begin(mask, q, kv):
    rows = kv[1].shape[0]
    span = 7 * rows
    vmem = pl.BlockSpec(memory_space=pltpu.VMEM)
    return pl.pallas_call(
        begin_kernel,
        out_shape=[jax.ShapeDtypeStruct((2, rows, HC), jnp.float32)] * 2
        + [jax.ShapeDtypeStruct((2, rows, HDIM), jnp.float32)] * 2,
        in_specs=[pl.BlockSpec(memory_space=pltpu.SMEM)] + [pl.BlockSpec(memory_space=pl.ANY)] * (3 * LANES),
        out_specs=[vmem] * 4,
        scratch_shapes=[
            pltpu.VMEM((LANES, rows, HC), jnp.bfloat16),
            pltpu.VMEM((3 * LANES * rows, 2 * HC), jnp.bfloat16),
            pltpu.VMEM((HL, rows, span), jnp.float32),
            pltpu.VMEM((HL, rows, span), jnp.bfloat16),
            pltpu.SemaphoreType.DMA((3 * LANES,)),
        ],
        compiler_params=pltpu.CompilerParams(vmem_limit_bytes=56 * 1024 * 1024),
        cost_estimate=BRIEF,
    )(mask, *q, *kv)


def attend_finish(steps, mask, q, begun, kv):
    rows = begun[0].shape[1]
    span = 3 * rows
    vmem = pl.BlockSpec(memory_space=pltpu.VMEM)

    def of_tile(step, width):
        return pl.BlockSpec((1, rows, width), lambda i, step=step: (step % 2, 0, 0))

    return pl.pallas_call(
        lambda *refs: finish_kernel(steps, *refs),
        grid=(1,),
        out_shape=[jax.ShapeDtypeStruct((rows, HC), jnp.bfloat16)] * len(steps),
        in_specs=[pl.BlockSpec(memory_space=pltpu.SMEM)]
        + [pl.BlockSpec(memory_space=pl.ANY)] * len(steps)
        + [of_tile(step, HC) for step in steps]
        + [of_tile(step, HDIM) for step in steps]
        + [pl.BlockSpec(memory_space=pl.ANY)] * LANES,
        out_specs=[vmem] * len(steps),
        scratch_shapes=[
            pltpu.VMEM((len(steps), rows, HC), jnp.bfloat16),
            pltpu.VMEM((3 * LANES * rows, 2 * HC), jnp.bfloat16),
            pltpu.VMEM((HL, rows, span), jnp.float32),
            pltpu.VMEM((HL, rows, span), jnp.bfloat16),
            pltpu.SemaphoreType.DMA((LANES + len(steps),)),
        ],
        compiler_params=pltpu.CompilerParams(vmem_limit_bytes=56 * 1024 * 1024),
        cost_estimate=BRIEF,
    )(
        mask,
        *[q[step] for step in steps],
        *[begun[step // 2] for step in steps],
        *[begun[2 + step // 2] for step in steps],
        *kv,
    )


def project_kernel(order, groups, a_refs, w_refs, o_ref, by_lane, by_shard, sems):
    step = pl.program_id(0)
    depth = by_shard.shape[1]
    shard = depth // len(order)

    @pl.when(step == 0)
    def _():
        fetch([(a_refs[d], by_lane.at[lane_of(d)]) for d in range(LANES)], sems)
        parts = []
        for place in order:
            lane, at = place * shard // HC, place * shard % HC
            parts.append(by_lane[lane][:, at : at + shard])
        by_shard[...] = jnp.concatenate(parts, axis=1)

    mine, core = lax.axis_index("groups"), lax.axis_index("core")
    widths = [w.shape[1] for w in w_refs]
    steps = o_ref.shape[1] // (widths[0] + groups * widths[1])
    direct, strip, half = widths[0] * steps, widths[1] * steps, widths[1] * steps // 2
    for w_ref, place in zip(w_refs, (0, direct + mine * strip)):
        width = w_ref.shape[1]
        out = jnp.dot(by_shard[...], w_ref[...], preferred_element_type=jnp.float32)
        o_ref[:, pl.ds(pl.multiple_of(place + step * width, HDIM), width)] = out.astype(jnp.bfloat16)
    width = half // steps
    for dx in range(1, groups):
        both = jnp.concatenate([ref[...] for ref in w_refs[2 * dx : 2 * dx + 2]], axis=1)
        out = jnp.dot(by_shard[...], both, preferred_element_type=jnp.float32).astype(jnp.bfloat16)
        start = direct + lax.rem(mine + groups - dx, groups) * strip + step * width
        for i, which in enumerate((core, 1 - core)):
            at = pl.multiple_of(start + which * half, HDIM)
            o_ref[:, pl.ds(at, width)] = out[:, i * width : (i + 1) * width]


def project(attended, weights, order, groups):
    count, depth = attended[0].shape
    channels = weights[0].shape[0]
    steps = weights[-1].shape[1] // (2 * HDIM)
    columns = weights[0].shape[1] + groups * weights[1].shape[1]
    return pl.pallas_call(
        lambda *refs: project_kernel(order, groups, refs[:LANES], refs[LANES:-4], *refs[-4:]),
        out_shape=jax.ShapeDtypeStruct((count, columns), jnp.bfloat16),
        grid=(steps,),
        in_specs=[pl.BlockSpec(memory_space=pltpu.HBM)] * LANES
        + [pl.BlockSpec((channels, w.shape[1] // steps), lambda n: (0, n)) for w in weights],
        out_specs=pl.BlockSpec((count, columns), lambda n: (0, 0)),
        scratch_shapes=[
            pltpu.VMEM((LANES, count, depth), jnp.bfloat16),
            pltpu.VMEM((count, channels), jnp.bfloat16),
            pltpu.SemaphoreType.DMA((LANES,)),
        ],
        compiler_params=pltpu.CompilerParams(vmem_limit_bytes=56 * 1024 * 1024),
    )(*attended, *weights)


def after(x, *others):
    return lax.optimization_barrier((x, *others))[0]


def on_device(queries, keys, values, frame_index, block_mask, out_weight):
    count = queries.shape[0]
    planes, groups = lax.axis_size("plane"), lax.axis_size("groups")
    seq = ("plane", "row", "core")

    def index(p, r, c):
        return (p * 2 + r) * 2 + c

    every = [(p, r, c) for p in range(planes) for r in range(2) for c in range(2)]

    def to_lane(x, dr, dc):
        return lax.ppermute(x, seq, [(index(p, r, c), index(p, r ^ dr, c ^ dc)) for p, r, c in every])

    def to_plane(x, dp):
        pairs = [(index(p, r, c), index(p + dp, r, c)) for p, r, c in every if 0 <= p + dp < planes]
        return lax.ppermute(x, seq, pairs)

    def swap(x):
        return to_lane(x[1], 0, 1)

    walk = [(p, 0) for p in range(planes)] + [(p, 1) for p in reversed(range(planes))]
    order = [index(p, r, c) for p, r in walk for c in range(2)]

    def gather(part):
        return lax.all_gather(part, seq, axis=0, tiled=True, axis_index_groups=[order])

    columns = out_weight.shape[1]
    strip = 2 * columns // 3 // (groups * 2 * HDIM) * 2 * HDIM
    direct = columns - groups * strip
    strip_at = direct + lax.axis_index("groups") * strip
    own_strip, direct_strip = [gather(x) for x in cut(out_weight, strip_at, strip, direct)]

    own, other, own_beside = pack(pack_kv_kernel, frame_index, (keys, values), 2 * HC)
    across = to_lane(other, 1, 0)
    early = [to_plane(own, dp) for dp in (1, -1)]
    beside = to_lane(own_beside, 0, 1)
    own_q, other_q, own_q_beside = pack(pack_q_kernel, frame_index, (after(queries, beside),), HC)
    across_q = to_lane(other_q, 1, 0)
    across_beside = swap(across)
    here = [own, beside, across, across_beside]
    q = [own_q, to_lane(own_q_beside, 0, 1), across_q, swap(across_q)]
    onward = after(across, *early)
    late = [to_plane(onward, dp) for dp in (1, -1)]

    own_strip = after(own_strip, *early, across_beside)
    half = strip // 2
    core_at = lax.axis_index("core") * half
    sent = lax.dynamic_slice_in_dim(own_strip, core_at, half, 1)
    halves = [
        lax.ppermute(sent, "groups", [(g, (g + dx) % groups) for g in range(groups)])
        for dx in range(1, groups)
    ]
    pieces = [piece for x in early for piece in (x, swap(x))]
    begun = attend_begin(after(block_mask, sent), q, here + pieces)
    late = [after(x, begun[0]) for x in late]
    late = [piece for x in late for piece in (x, swap(x))]
    mixed = attend_finish((2, 3), block_mask, q, begun, late)
    back = [to_lane(x, 1, d) for d, x in enumerate(mixed)]
    halves = [after(x, mixed[0]) for x in halves]
    rest = attend_finish((0, 1), after(block_mask, mixed[0], *halves), q, begun, late)
    mixed = [rest[0], to_lane(after(rest[1], back[0]), 0, 1)] + back
    weights = [direct_strip, own_strip]
    for x in halves:
        weights += [x, lax.ppermute(x, "core", [(0, 1), (1, 0)])]
    return project(mixed, weights, order, groups)


def solution(mesh):
    groups, seq = mesh.devices.shape
    split = Mesh(
        mesh.devices.reshape(groups, seq // LANES, LANES // 2, 2), ("groups", "plane", "row", "core")
    )
    along = ("plane", "row", "core")
    tokens = P(("groups",) + along, None)
    return jax.shard_map(
        on_device,
        mesh=split,
        in_specs=(tokens, tokens, tokens, P(("groups",) + along), P(), P(along, None)),
        out_specs=tokens,
        check_vma=False,
    )
```
